256 devices in a mesh: outer: 8 (over x_hi, y), inner: 32 (over x_lo, z, core).
Axes of the slice: x: 4 (x_hi: 2, x_lo: 2; x = x_hi * 2 + x_lo), y: 4, z: 8, core: 2. Of those that a mesh axis runs over, the one named last changes fastest.
Arguments:
- queries: bfloat16 [49152, 4096], P(('outer', 'inner'))
- keys: bfloat16 [49152, 1024], P(('outer', 'inner'))
- values: bfloat16 [49152, 1024], P(('outer', 'inner')), may hold values from -6 to 6
- stretch_of: int32 [8, 32, 2], replicated, may hold values from 0 to 511, as said below
Outputs:
- attended: bfloat16 [49152, 4096], P(('outer', 'inner'))
The draws below stay inside these ranges and needn't reach their ends.
Inputs may be any that keep to these rules, and one draw needn't show every extreme that they name: There is a permutation P of 0 to 7 with stretch_of[g, s] = (2 * 32 * P(g) + s, 2 * 32 * P(g) + 2 * 32 - 1 - s).
All inputs are finite; a program needn't handle non-finite values.
Results may differ from the reference program's by a relative error of at most 0.0095.
Values may be sent and summed in bfloat16 or wider, within the bound.
A program may use at most 64 MiB of HBM per device.

```python
import jax
import jax.numpy as jnp
from jax import lax

QUERY_HEADS = 32
KEY_VALUE_HEADS = 8
HEAD_SIZE = 128
TOKENS_PER_PART = 192
STRETCH = 96
GROUPS = 8
SHARDS = 32
SEQUENCE_TOKENS = 49152
N_OUTER = 8
N_INNER = 32


def base_keys(key):
    return jax.random.normal(key, (SEQUENCE_TOKENS, KEY_VALUE_HEADS * HEAD_SIZE), jnp.float32)


def draw_keys(key, part):
    shared_state = base_keys(key)
    return shared_state.astype(jnp.bfloat16)


def draw_queries(key, part):
    key = jax.random.fold_in(key, 12)
    fresh = jax.random.normal(key, (SEQUENCE_TOKENS, QUERY_HEADS * HEAD_SIZE), jnp.float32)
    return fresh.astype(jnp.bfloat16)


def draw_stretch_of(key, part):
    key = jax.random.fold_in(key, 13)
    ranks = jax.random.permutation(key, GROUPS).astype(jnp.int32)
    shard_ids = jnp.arange(SHARDS, dtype=jnp.int32)
    first = ranks[:, None] * (2 * SHARDS) + shard_ids[None, :]
    second = ranks[:, None] * (2 * SHARDS) + 2 * SHARDS - 1 - shard_ids[None, :]
    return jnp.stack((first, second), axis=-1).astype(jnp.int32)


def block_levels(key, shape, cuts, least, top_value):
    def one(position, blocks):
        draws = jax.random.uniform(jax.random.fold_in(jax.random.fold_in(key, 6), position), (blocks,), jnp.float32, least / len(cuts), top_value / len(cuts))
        return jnp.repeat(jnp.exp(draws), shape[position] // blocks).reshape((-1,) + (1,) * (len(shape) - position - 1))

    loudness = one(*cuts[0])
    for cut in cuts[1:]:
        loudness = loudness * one(*cut)
    return loudness


def gaussian(rng, dims, scale, limit, cuts=(), kind=jnp.bfloat16):
    gain = block_levels(rng, dims, cuts, -0.22, 0.18) if cuts else 1.0
    values = jax.random.normal(rng, dims, jnp.float32) * scale * gain
    return jnp.minimum(jnp.maximum(values, -limit), limit).astype(kind)


def setup_inputs(seed: int = 0) -> dict:
    key_of = jax.random.split(jax.random.key(seed), 5)
    return {
        "queries": draw_queries(jax.random.fold_in(key_of[4], 71), 0),
        "keys": draw_keys(jax.random.fold_in(key_of[4], 71), 0),
        "values": gaussian(key_of[2], (SEQUENCE_TOKENS, KEY_VALUE_HEADS * HEAD_SIZE), 1.0, 6.0, ((0, 256),)),
        "stretch_of": draw_stretch_of(jax.random.fold_in(key_of[4], 71), 0),
    }


def key_collections(source, query_groups, shard_pieces, width):
    source = source.reshape((query_groups, shard_pieces) + source.shape[1:])
    rolled = [jnp.roll(source, stride, axis=1) for stride in range(4)]
    rolled.append(jnp.roll(source, 1, axis=0))
    stacked = jnp.stack(rolled, axis=2)
    return stacked.reshape((query_groups * shard_pieces, 5 * TOKENS_PER_PART) + width)


def reference(queries, keys, values, stretch_of):
    query_groups = N_OUTER
    shard_pieces = N_INNER
    device_list = query_groups * shard_pieces
    queries_per_group = QUERY_HEADS // KEY_VALUE_HEADS
    score_scale = HEAD_SIZE ** -0.5
    offsets = jnp.arange(STRETCH, dtype=jnp.int32)
    token_pos = (stretch_of[:, :, :, None].astype(jnp.int32) * STRETCH + offsets).reshape(query_groups, shard_pieces, TOKENS_PER_PART)
    query_pos = token_pos.reshape(device_list, TOKENS_PER_PART)
    key_pos = key_collections(token_pos.reshape(device_list, TOKENS_PER_PART), query_groups, shard_pieces, ())
    key_matrix = key_collections(keys.reshape(device_list, TOKENS_PER_PART, KEY_VALUE_HEADS, HEAD_SIZE), query_groups, shard_pieces, (KEY_VALUE_HEADS, HEAD_SIZE))
    value_matrix = key_collections(values.reshape(device_list, TOKENS_PER_PART, KEY_VALUE_HEADS, HEAD_SIZE), query_groups, shard_pieces, (KEY_VALUE_HEADS, HEAD_SIZE))

    def attend(device_inputs):
        query_tile_block, key_block, value_block, rows_pos, cols_pos = device_inputs
        grouped_query = query_tile_block.reshape(TOKENS_PER_PART, KEY_VALUE_HEADS, queries_per_group, HEAD_SIZE).astype(jnp.float32)
        scores = jnp.einsum('tkgd,ukd->kgtu', grouped_query, key_block.astype(jnp.float32)) * score_scale
        visible = cols_pos[None, :] <= rows_pos[:, None]
        scores = jnp.where(visible, scores, -jnp.inf)
        row_max = jnp.max(scores, axis=-1, keepdims=True)
        weights = jnp.exp(scores - row_max)
        row_sum = jnp.sum(weights, axis=-1, keepdims=True)
        rounded = weights.astype(jnp.bfloat16).astype(jnp.float32)
        weighted = jnp.einsum('kgtu,ukd->kgtd', rounded, value_block.astype(jnp.float32)) / row_sum
        return weighted.transpose(2, 0, 1, 3).reshape(TOKENS_PER_PART, QUERY_HEADS * HEAD_SIZE).astype(jnp.bfloat16)

    result = lax.map(attend, (queries.reshape(device_list, TOKENS_PER_PART, QUERY_HEADS * HEAD_SIZE), key_matrix, value_matrix, query_pos, key_pos))
    return result.reshape(device_list * TOKENS_PER_PART, QUERY_HEADS * HEAD_SIZE)
```

```python
import jax
import jax.numpy as jnp
from jax import lax
from jax.experimental import pallas as pl
from jax.experimental.pallas import tpu as pltpu
from jax.sharding import PartitionSpec as P

MESH = pl.DeviceIdType.MESH
KVH = 8
REP = 4
D = 128
T = 96
SCALE = D ** (-0.5)
LEAD = 3
LEAD_EARLY = 5
INF = float("inf")

SLOTS = 12


def kernel(n_outer, n_inner, q_hbm, k_hbm, v_hbm, st_hbm, o_hbm, q_vm, kv, o_vm, st, diagonal,
           q_sem, own_sem, st_sem, o_sem, recv, send):
    g = lax.axis_index("outer")
    s = lax.axis_index("inner")
    g_next, g_prev = lax.rem(g + 1, n_outer), lax.rem(g + n_outer - 1, n_outer)

    def shard(distance):
        return lax.rem(s + distance + n_inner, n_inner)

    even = lax.rem(s, 2) == 0
    odd = lax.rem(s, 2) == 1

    def own_copies(h):
        columns = pl.ds(pl.multiple_of(h * D, D), D)
        return [
            pltpu.make_async_copy(
                ref.at[pl.ds(T * (1 - slot), T), columns], kv.at[h, i, slot], own_sem.at[h]
            )
            for i, ref in enumerate((k_hbm, v_hbm))
            for slot in range(2)
        ]

    @pl.loop(0, KVH)
    def _(h):
        for copy in own_copies(h):
            copy.start()

    st_copies = [
        pltpu.make_async_copy(st_hbm.at[group], st.at[i], st_sem.at[i])
        for i, group in enumerate((g, g_prev))
    ]
    for copy in st_copies:
        copy.start()
    q_copy = pltpu.make_async_copy(q_hbm, q_vm, q_sem)
    q_copy.start()

    @pl.when(s == 2)
    def _():
        kv[:, :, 7:9] = jnp.zeros((KVH, 2, 2, T, D), kv.dtype)

    @pl.when(s == 1)
    def _():
        kv[:, :, 7:8] = jnp.zeros((KVH, 2, 1, T, D), kv.dtype)

    half = n_inner // 2
    at_end = lax.rem(s, half) >= half - 2
    at_start = lax.rem(s, half) < 2
    flip = lax.rem(s + half, n_inner)
    ring_on = lax.rem(s + 2, half) + half * (s // half)
    ring_back = lax.rem(s + half - 2, half) + half * (s // half)
    last, lends = s >= n_inner - 2, at_end & (s < half)
    before_last = s == n_inner - 4

    def detours(h):
        return lax.rem(h, 3) == 1

    barrier = pltpu.get_barrier_semaphore()

    def greet(group, inner):
        pl.semaphore_signal(barrier, inc=1, device_id=(group, inner), device_id_type=MESH)

    greet(g_prev, s)
    greet(g, shard(-2))
    greet(g, shard(-1))

    @pl.when(even)
    def _():
        greet(g, shard(1))

    @pl.when(s < 2)
    def _():
        greet(g, ring_back)

    @pl.when(s == 0)
    def _():
        greet(g, shard(-4))

    @pl.when(lends)
    def _():
        greet(g, flip)

    more = last | lends | before_last

    @pl.when(even & jnp.logical_not(more))
    def _():
        pl.semaphore_wait(barrier, 3)

    @pl.when((even & more) | (odd & jnp.logical_not(more)))
    def _():
        pl.semaphore_wait(barrier, 4)

    @pl.when(odd & more)
    def _():
        pl.semaphore_wait(barrier, 5)

    def remote(h, src, dst, sem, target):
        return pltpu.make_async_remote_copy(
            src_ref=kv.at[h, :, src],
            dst_ref=kv.at[h, :, dst],
            send_sem=send.at[sem, h],
            recv_sem=recv.at[dst, h],
            device_id=target,
            device_id_type=MESH,
        )

    def to_next_group(h):
        return pltpu.make_async_remote_copy(
            src_ref=kv.at[h, :, pl.ds(0, 2)],
            dst_ref=kv.at[h, :, pl.ds(5, 2)],
            send_sem=send.at[0, h],
            recv_sem=recv.at[5, h],
            device_id=(g_next, s),
            device_id_type=MESH,
        )

    me = (g, s)
    two_on, one_on, one_back = (g, shard(2)), (g, shard(1)), (g, shard(-1))
    via, beside = (g, flip), (g, ring_on)
    starts = s < 2

    def first(h):
        detour = last & detours(h)
        straight = jnp.logical_not(detour)
        return [
            (straight, 1, 3, 1, two_on),
            (last & straight, 0, 8, 2, two_on),
            (detour, 1, 11, 1, via),
            (detour, 0, 10, 2, via),
            (even, 1, 2, 3, one_on),
            (s == n_inner - 3, 0, 7, 2, one_back),
        ]

    passed = [
        (None, 3, 4, 4, one_on),
        (s == 0, 8, 9, 5, one_on),
        (odd, 3, 2, 6, one_back),
        (s == 1, 8, 7, 7, one_back),
    ]
    passed_high = [
        (s == 0, 7, 9, 8, two_on),
        (before_last, 7, 9, 8, (g, shard(4))),
    ]
    between = [(None, 11, 3, 9, beside), (None, 10, 8, 10, beside)]

    def each(table, h, act):
        for condition, *entry in table:
            if condition is None:
                act(remote(h, *entry))
            else:
                @pl.when(condition)
                def _(entry=entry):
                    act(remote(h, *entry))

    def send_own(h):
        pltpu.make_async_copy(kv.at[h, :, pl.ds(0, 2)], kv.at[h, :, pl.ds(0, 2)], own_sem.at[h]).wait()
        each(first(h), h, lambda copy: copy.start())

    def send_on(h):
        to_next_group(h).start()

    for h in range(LEAD):
        send_own(h)
        send_on(h)

    early = lax.rem(s, half) >= half - 4

    @pl.when(early)
    def _():
        @pl.loop(LEAD, LEAD_EARLY)
        def _(h):
            send_own(h)

    def send_ahead(h):
        @pl.when(jnp.logical_not(early) & (h + LEAD < KVH))
        def _():
            send_own(h + LEAD)

        @pl.when(early & (h + LEAD_EARLY < KVH))
        def _():
            send_own(h + LEAD_EARLY)

        @pl.when(h + LEAD < KVH)
        def _():
            send_on(h + LEAD)

    def arrived(h, dst):
        remote(h, dst, dst, 0, me).wait_recv()

    def pass_on(h):
        arrived(h, 3)

        @pl.when(starts)
        def _():
            arrived(h, 8)

        each(passed, h, lambda copy: copy.start())

    def pass_high(h):
        arrived(h, 7)
        each(passed_high, h, lambda copy: copy.start())

    def relay(h):
        @pl.when(lends & detours(h))
        def _():
            arrived(h, 11)
            arrived(h, 10)
            each(between, h, lambda copy: copy.start())

    seam = at_end | starts
    for h in range(3):
        relay(h)
    pass_on(0)

    @pl.when(seam)
    def _():
        pass_on(1)

    @pl.when((s == 0) | before_last)
    def _():
        pass_high(0)

    @pl.when(before_last)
    def _():
        pass_high(1)

    for copy in st_copies:
        copy.wait()
    other = jnp.where(st[1, 0:1, 0:1] < st[0, 0:1, 0:1], INF, -INF).astype(jnp.float32)
    row = lax.broadcasted_iota(jnp.int32, (T, REP * T), 0)
    query = lax.rem(lax.broadcasted_iota(jnp.int32, (T, REP * T), 1), T)
    diagonal[...] = jnp.where(row <= query, INF, -INF).astype(jnp.float32)

    q_copy.wait()

    def columns(h, r):
        return pl.ds(pl.multiple_of(h * (REP * D) + r * D, D), D)

    def attend(h, wrapped):
        slots = 10 if wrapped else 7
        q = jnp.concatenate(
            [q_vm[row0:row0 + T, columns(h, r)] for row0 in (0, T) for r in range(REP)], axis=0
        )
        keys = kv[h, 0, 0:slots].reshape(slots * T, D)
        values = kv[h, 1, 0:slots].reshape(slots * T, D)
        results = []
        for c in range(2 * REP * T // 256):
            scores = lax.dot_general(
                keys, q[c * 256:(c + 1) * 256], (((1,), (1,)), ((), ())), preferred_element_type=jnp.float32
            )
            blocks, sums = [], []
            for b in range(2):
                block = 2 * c + b
                high = block >= 3
                lanes = slice((block % 3) * 128, (block % 3 + 1) * 128)
                parts = [scores[slot * T:(slot + 1) * T, b * 128:(b + 1) * 128] for slot in range(slots)]
                own = 0 if high else 1
                parts[own] = jnp.minimum(parts[own], diagonal[:, lanes])
                for slot in (5, 6):
                    parts[slot] = jnp.minimum(parts[slot], other)
                for j in range(1, 4):
                    if wrapped and high:
                        parts[6 + j] = jnp.minimum(parts[6 + j], jnp.where(s < j, INF, -INF))
                    if wrapped and not high:
                        parts[1 + j] = jnp.minimum(parts[1 + j], jnp.where(s >= j, INF, -INF))
                        parts[6 + j] = None
                if not high:
                    parts[0] = None
                top = None
                for part in parts:
                    if part is not None:
                        peak = jnp.max(part, axis=0, keepdims=True)
                        top = peak if top is None else jnp.maximum(top, peak)
                total, rounded = None, []
                for part in parts:
                    if part is None:
                        rounded.append(jnp.zeros((T, 128), jnp.bfloat16))
                    else:
                        weights = jnp.exp((part - top) * SCALE)
                        here = jnp.sum(weights, axis=0, keepdims=True)
                        total = here if total is None else total + here
                        rounded.append(weights.astype(jnp.bfloat16))
                blocks.append(jnp.concatenate(rounded, axis=0))
                sums.append(total)
            weighted = lax.dot_general(
                values, jnp.concatenate(blocks, axis=1), (((0,), (0,)), ((), ())), preferred_element_type=jnp.float32
            )
            results.append((weighted / jnp.concatenate(sums, axis=1)).T.astype(o_vm.dtype))
        result = jnp.concatenate(results, axis=0)
        for half_index in range(2):
            for r in range(REP):
                start = (half_index * REP + r) * T
                o_vm[half_index * T:(half_index + 1) * T, columns(h, r)] = result[start:start + T]

    def out_copy(h):
        columns = pl.ds(pl.multiple_of(h * (REP * D), REP * D), REP * D)
        return pltpu.make_async_copy(o_vm.at[:, columns], o_hbm.at[:, columns], o_sem.at[h])

    @pl.loop(0, KVH)
    def _(h):
        send_ahead(h)

        @pl.when(h + 3 < KVH)
        def _():
            relay(h + 3)

        @pl.when(seam & (h + 2 < KVH))
        def _():
            pass_on(h + 2)

        @pl.when(jnp.logical_not(seam) & (h + 1 < KVH))
        def _():
            pass_on(h + 1)

        @pl.when((s == 0) & (h + 1 < KVH))
        def _():
            pass_high(h + 1)

        @pl.when(before_last & (h + 2 < KVH))
        def _():
            pass_high(h + 2)

        arrived(h, 2)
        arrived(h, 4)

        @pl.when(s < 3)
        def _():
            arrived(h, 9)

        to_next_group(h).wait_recv()

        @pl.when(s >= 3)
        def _():
            attend(h, False)

        @pl.when(s < 3)
        def _():
            attend(h, True)

        out_copy(h).start()

    @pl.loop(0, KVH)
    def _(h):
        to_next_group(h).wait_send()
        each(first(h), h, lambda copy: copy.wait_send())
        each(passed, h, lambda copy: copy.wait_send())
        each(passed_high, h, lambda copy: copy.wait_send())

        @pl.when(lends & detours(h))
        def _():
            each(between, h, lambda copy: copy.wait_send())

        out_copy(h).wait()


def solution(mesh):
    n_outer, n_inner = mesh.shape["outer"], mesh.shape["inner"]

    def on_device(queries, keys, values, stretch_of):
        rows, width = queries.shape
        any_space = pl.BlockSpec(memory_space=pl.ANY)
        return pl.pallas_call(
            lambda *refs: kernel(n_outer, n_inner, *refs),
            out_shape=jax.ShapeDtypeStruct((rows, width), jnp.bfloat16),
            in_specs=[any_space] * 4,
            out_specs=any_space,
            scratch_shapes=[
                pltpu.VMEM((rows, width), jnp.bfloat16),
                pltpu.VMEM((KVH, 2, SLOTS, T, D), jnp.bfloat16),
                pltpu.VMEM((rows, width), jnp.bfloat16),
                pltpu.VMEM((2, 2, n_inner), jnp.int32),
                pltpu.VMEM((T, REP * T), jnp.float32),
                pltpu.SemaphoreType.DMA,
                pltpu.SemaphoreType.DMA((KVH,)),
                pltpu.SemaphoreType.DMA((2,)),
                pltpu.SemaphoreType.DMA((KVH,)),
                pltpu.SemaphoreType.DMA((SLOTS, KVH)),
                pltpu.SemaphoreType.DMA((11, KVH)),
            ],
            compiler_params=pltpu.CompilerParams(
                collective_id=0, has_side_effects=True, vmem_limit_bytes=48 * 1024 * 1024
            ),
            cost_estimate=pl.CostEstimate(flops=2 * 10**9, bytes_accessed=6 * 10**6, transcendentals=4 * 10**6),
        )(*(
            pltpu.with_memory_space_constraint(array, pltpu.HBM)
            for array in (queries, keys, values, stretch_of.transpose(0, 2, 1))
        ))

    rows = P(("outer", "inner"), None)
    return jax.shard_map(
        on_device, mesh=mesh, in_specs=(rows, rows, rows, P()), out_specs=rows, check_vma=False
    )
```

```python
import jax
import jax.numpy as jnp
from jax import lax
from jax.experimental import pallas as pl
from jax.experimental.pallas import tpu as pltpu
from jax.sharding import PartitionSpec as P

MESH = pl.DeviceIdType.MESH
KVH = 8
REP = 4
D = 128
T = 96
SCALE = D ** (-0.5)
LEAD = 3
LEAD_EARLY = 6
INF = float("inf")

SLOTS = 12


def kernel(n_outer, n_inner, q_hbm, k_hbm, v_hbm, st_hbm, o_hbm, q_vm, kv, o_vm, st, diagonal,
           q_sem, own_sem, st_sem, o_sem, recv, send):
    g = lax.axis_index("outer")
    s = lax.axis_index("inner")
    g_next, g_prev = lax.rem(g + 1, n_outer), lax.rem(g + n_outer - 1, n_outer)

    def shard(distance):
        return lax.rem(s + distance + n_inner, n_inner)

    even = lax.rem(s, 2) == 0
    odd = lax.rem(s, 2) == 1

    def own_copies(h):
        columns = pl.ds(pl.multiple_of(h * D, D), D)
        return [
            pltpu.make_async_copy(
                ref.at[pl.ds(T * (1 - slot), T), columns], kv.at[h, i, slot], own_sem.at[h]
            )
            for i, ref in enumerate((k_hbm, v_hbm))
            for slot in range(2)
        ]

    @pl.loop(0, KVH)
    def _(h):
        for copy in own_copies(h):
            copy.start()

    st_copies = [
        pltpu.make_async_copy(st_hbm.at[group], st.at[i], st_sem.at[i])
        for i, group in enumerate((g, g_prev))
    ]
    for copy in st_copies:
        copy.start()
    q_copy = pltpu.make_async_copy(q_hbm, q_vm, q_sem)
    q_copy.start()

    @pl.when(s == 2)
    def _():
        kv[:, :, 7:9] = jnp.zeros((KVH, 2, 2, T, D), kv.dtype)

    @pl.when(s == 1)
    def _():
        kv[:, :, 7:8] = jnp.zeros((KVH, 2, 1, T, D), kv.dtype)

    half = n_inner // 2
    at_end = lax.rem(s, half) >= half - 2
    at_start = lax.rem(s, half) < 2
    flip = lax.rem(s + half, n_inner)
    ring_on = lax.rem(s + 2, half) + half * (s // half)
    ring_back = lax.rem(s + half - 2, half) + half * (s // half)
    last, lends = s >= n_inner - 2, at_end & (s < half)
    before_last = s == n_inner - 4

    rows_y = n_outer // 2
    y_first, y_last = lax.rem(g, rows_y) == 0, lax.rem(g, rows_y) == rows_y - 1
    turns, turned = y_last & at_start, y_first & at_start
    far = lax.rem(g + rows_y, n_outer)
    turn = lax.rem(g_next + rows_y, n_outer)

    def detours(h):
        return jnp.where(y_first | y_last, lax.rem(h, 2) == 1, lax.rem(h, 3) == 1)

    barrier = pltpu.get_barrier_semaphore()

    def greet(group, inner):
        pl.semaphore_signal(barrier, inc=1, device_id=(group, inner), device_id_type=MESH)

    greet(g_prev, s)
    greet(g, shard(-2))
    greet(g, shard(-1))

    @pl.when(even)
    def _():
        greet(g, shard(1))

    @pl.when(s < 2)
    def _():
        greet(g, ring_back)

    @pl.when(s == 0)
    def _():
        greet(g, shard(-4))
        greet(g, ring_back + 1)

    @pl.when(lends)
    def _():
        greet(g, flip)

    @pl.when(turned)
    def _():
        greet(far, s)
        greet(lax.rem(g + n_outer + rows_y - 1, n_outer), s)

    count = 3 + lax.rem(s, 2)
    for extra in (last, lends, before_last, turns, turned, (s == half - 1)):
        count += extra.astype(jnp.int32)
    pl.semaphore_wait(barrier, count)

    def remote(h, src, dst, sem, target):
        return pltpu.make_async_remote_copy(
            src_ref=kv.at[h, :, src],
            dst_ref=kv.at[h, :, dst],
            send_sem=send.at[sem, h],
            recv_sem=recv.at[dst, h],
            device_id=target,
            device_id_type=MESH,
        )

    def pair(h, src, dst, sem, group):
        return pltpu.make_async_remote_copy(
            src_ref=kv.at[h, :, pl.ds(src, 2)],
            dst_ref=kv.at[h, :, pl.ds(dst, 2)],
            send_sem=send.at[sem, h],
            recv_sem=recv.at[dst, h],
            device_id=(group, s),
            device_id_type=MESH,
        )

    def to_next_group(h, act):
        turning = turns & (lax.rem(h, 2) == 1)

        @pl.when(turning)
        def _():
            act(pair(h, 0, 10, 0, turn))

        @pl.when(jnp.logical_not(turning))
        def _():
            act(pair(h, 0, 5, 0, g_next))

    def from_turn(h):
        return pair(h, 10, 5, 11, far)

    me = (g, s)
    two_on, one_on, one_back = (g, shard(2)), (g, shard(1)), (g, shard(-1))
    via, beside = (g, flip), (g, ring_on)

    def first(h):
        detour = last & detours(h)
        straight = jnp.logical_not(detour)
        return [
            (straight, 1, 3, 1, two_on),
            (even & last & straight, 0, 8, 2, two_on),
            (odd & last & straight, 0, 7, 2, one_on),
            (detour, 1, 11, 1, via),
            (detour, 0, 10, 2, via),
            (even, 1, 2, 3, one_on),
            (s == n_inner - 3, 0, 7, 2, one_back),
        ]

    passed = [
        (None, 3, 4, 4, one_on),
        (s == 0, 8, 9, 5, one_on),
        (odd, 3, 2, 6, one_back),
    ]
    passed_high = [
        (s == 0, 7, 8, 7, one_on),
        (s == 0, 7, 9, 8, two_on),
        (before_last, 7, 9, 8, (g, shard(4))),
    ]
    between = [
        (None, 11, 3, 9, beside),
        (even, 10, 8, 10, beside),
        (odd, 10, 7, 10, (g, ring_on - 1)),
    ]

    def each(table, h, act):
        for condition, *entry in table:
            if condition is None:
                act(remote(h, *entry))
            else:
                @pl.when(condition)
                def _(entry=entry):
                    act(remote(h, *entry))

    def send_own(h):
        pltpu.make_async_copy(kv.at[h, :, pl.ds(0, 2)], kv.at[h, :, pl.ds(0, 2)], own_sem.at[h]).wait()
        each(first(h), h, lambda copy: copy.start())

    def send_on(h):
        to_next_group(h, lambda copy: copy.start())

    for h in range(LEAD):
        send_own(h)
        send_on(h)

    early = lax.rem(s, half) >= half - 4

    @pl.when(early)
    def _():
        @pl.loop(LEAD, LEAD_EARLY)
        def _(h):
            send_own(h)

    lead = LEAD + turns.astype(jnp.int32)

    @pl.when(turns)
    def _():
        send_own(LEAD)
        send_on(LEAD)

    def send_ahead(h):
        @pl.when(jnp.logical_not(early) & (h + lead < KVH))
        def _():
            send_own(h + lead)

        @pl.when(early & (h + LEAD_EARLY < KVH))
        def _():
            send_own(h + LEAD_EARLY)

        @pl.when(h + lead < KVH)
        def _():
            send_on(h + lead)

    def arrived(h, dst):
        remote(h, dst, dst, 0, me).wait_recv()

    def pass_on(h):
        arrived(h, 3)

        @pl.when(s == 0)
        def _():
            arrived(h, 8)

        each(passed, h, lambda copy: copy.start())

    def pass_high(h):
        arrived(h, 7)
        each(passed_high, h, lambda copy: copy.start())

    def relay(h):
        @pl.when(lends & detours(h))
        def _():
            arrived(h, 11)
            arrived(h, 10)
            each(between, h, lambda copy: copy.start())

    def pass_turn(h):
        @pl.when(turned & (lax.rem(h, 2) == 1))
        def _():
            pair(h, 10, 10, 0, g).wait_recv()
            from_turn(h).start()

    seam = at_end | (s < 2)
    passes_high = (s == 0) | before_last
    for h in range(4):
        relay(h)
    pass_on(0)

    @pl.when(seam)
    def _():
        pass_on(1)
        pass_on(2)

    @pl.when(passes_high)
    def _():
        pass_high(0)
        pass_high(1)
        pass_high(2)

    pass_turn(1)

    for copy in st_copies:
        copy.wait()
    other = jnp.where(st[1, 0:1, 0:1] < st[0, 0:1, 0:1], INF, -INF).astype(jnp.float32)
    row = lax.broadcasted_iota(jnp.int32, (T, REP * T), 0)
    query = lax.rem(lax.broadcasted_iota(jnp.int32, (T, REP * T), 1), T)
    diagonal[...] = jnp.where(row <= query, INF, -INF).astype(jnp.float32)

    q_copy.wait()

    def columns(h, r):
        return pl.ds(pl.multiple_of(h * (REP * D) + r * D, D), D)

    def attend(h, wrapped):
        slots = 10 if wrapped else 7
        q = jnp.concatenate(
            [q_vm[row0:row0 + T, columns(h, r)] for row0 in (0, T) for r in range(REP)], axis=0
        )
        keys = kv[h, 0, 0:slots].reshape(slots * T, D)
        values = kv[h, 1, 0:slots].reshape(slots * T, D)
        results = []
        for c in range(2 * REP * T // 256):
            scores = lax.dot_general(
                keys, q[c * 256:(c + 1) * 256], (((1,), (1,)), ((), ())), preferred_element_type=jnp.float32
            )
            blocks, sums = [], []
            for b in range(2):
                block = 2 * c + b
                high = block >= 3
                lanes = slice((block % 3) * 128, (block % 3 + 1) * 128)
                parts = [scores[slot * T:(slot + 1) * T, b * 128:(b + 1) * 128] for slot in range(slots)]
                own = 0 if high else 1
                parts[own] = jnp.minimum(parts[own], diagonal[:, lanes])
                for slot in (5, 6):
                    parts[slot] = jnp.minimum(parts[slot], other)
                for j in range(1, 4):
                    if wrapped and high:
                        parts[6 + j] = jnp.minimum(parts[6 + j], jnp.where(s < j, INF, -INF))
                    if wrapped and not high:
                        parts[1 + j] = jnp.minimum(parts[1 + j], jnp.where(s >= j, INF, -INF))
                        parts[6 + j] = None
                if not high:
                    parts[0] = None
                top = None
                for part in parts:
                    if part is not None:
                        peak = jnp.max(part, axis=0, keepdims=True)
                        top = peak if top is None else jnp.maximum(top, peak)
                total, rounded = None, []
                for part in parts:
                    if part is None:
                        rounded.append(jnp.zeros((T, 128), jnp.bfloat16))
                    else:
                        weights = jnp.exp((part - top) * SCALE)
                        here = jnp.sum(weights, axis=0, keepdims=True)
                        total = here if total is None else total + here
                        rounded.append(weights.astype(jnp.bfloat16))
                blocks.append(jnp.concatenate(rounded, axis=0))
                sums.append(total)
            weighted = lax.dot_general(
                values, jnp.concatenate(blocks, axis=1), (((0,), (0,)), ((), ())), preferred_element_type=jnp.float32
            )
            results.append((weighted / jnp.concatenate(sums, axis=1)).T.astype(o_vm.dtype))
        result = jnp.concatenate(results, axis=0)
        for half_index in range(2):
            for r in range(REP):
                start = (half_index * REP + r) * T
                o_vm[half_index * T:(half_index + 1) * T, columns(h, r)] = result[start:start + T]

    def out_copy(h):
        columns = pl.ds(pl.multiple_of(h * (REP * D), REP * D), REP * D)
        return pltpu.make_async_copy(o_vm.at[:, columns], o_hbm.at[:, columns], o_sem.at[h])

    @pl.loop(0, KVH)
    def _(h):
        @pl.when(h + 4 < KVH)
        def _():
            relay(h + 4)

        @pl.when(seam & (h + 3 < KVH))
        def _():
            pass_on(h + 3)

        @pl.when(passes_high & (h + 3 < KVH))
        def _():
            pass_high(h + 3)

        send_ahead(h)

        @pl.when(h + 2 < KVH)
        def _():
            pass_turn(h + 2)

        @pl.when(jnp.logical_not(seam) & (h + 1 < KVH))
        def _():
            pass_on(h + 1)

        @pl.when(s == 1)
        def _():
            arrived(h, 8)

        arrived(h, 2)
        arrived(h, 4)

        @pl.when(s < 3)
        def _():
            arrived(h, 9)

        pair(h, 5, 5, 0, g).wait_recv()

        @pl.when(s >= 3)
        def _():
            attend(h, False)

        @pl.when(s < 3)
        def _():
            attend(h, True)

        out_copy(h).start()

    @pl.loop(0, KVH)
    def _(h):
        to_next_group(h, lambda copy: copy.wait_send())
        each(first(h), h, lambda copy: copy.wait_send())
        each(passed, h, lambda copy: copy.wait_send())
        each(passed_high, h, lambda copy: copy.wait_send())

        @pl.when(lends & detours(h))
        def _():
            each(between, h, lambda copy: copy.wait_send())

        @pl.when(turned & (lax.rem(h, 2) == 1))
        def _():
            from_turn(h).wait_send()

        out_copy(h).wait()


def solution(mesh):
    n_outer, n_inner = mesh.shape["outer"], mesh.shape["inner"]

    def on_device(queries, keys, values, stretch_of):
        rows, width = queries.shape
        any_space = pl.BlockSpec(memory_space=pl.ANY)
        return pl.pallas_call(
            lambda *refs: kernel(n_outer, n_inner, *refs),
            out_shape=jax.ShapeDtypeStruct((rows, width), jnp.bfloat16),
            in_specs=[any_space] * 4,
            out_specs=any_space,
            scratch_shapes=[
                pltpu.VMEM((rows, width), jnp.bfloat16),
                pltpu.VMEM((KVH, 2, SLOTS, T, D), jnp.bfloat16),
                pltpu.VMEM((rows, width), jnp.bfloat16),
                pltpu.VMEM((2, 2, n_inner), jnp.int32),
                pltpu.VMEM((T, REP * T), jnp.float32),
                pltpu.SemaphoreType.DMA,
                pltpu.SemaphoreType.DMA((KVH,)),
                pltpu.SemaphoreType.DMA((2,)),
                pltpu.SemaphoreType.DMA((KVH,)),
                pltpu.SemaphoreType.DMA((SLOTS, KVH)),
                pltpu.SemaphoreType.DMA((12, KVH)),
            ],
            compiler_params=pltpu.CompilerParams(
                collective_id=0, has_side_effects=True, vmem_limit_bytes=48 * 1024 * 1024
            ),
            cost_estimate=pl.CostEstimate(flops=2 * 10**9, bytes_accessed=6 * 10**6, transcendentals=4 * 10**6),
        )(*(
            pltpu.with_memory_space_constraint(array, pltpu.HBM)
            for array in (queries, keys, values, stretch_of.transpose(0, 2, 1))
        ))

    rows = P(("outer", "inner"), None)
    return jax.shard_map(
        on_device, mesh=mesh, in_specs=(rows, rows, rows, P()), out_specs=rows, check_vma=False
    )
```

```python
import jax
import jax.numpy as jnp
from jax import lax
from jax.experimental import pallas as pl
from jax.experimental.pallas import tpu as pltpu
from jax.sharding import PartitionSpec as P

MESH = pl.DeviceIdType.MESH
KVH = 8
REP = 4
D = 128
T = 96
SCALE = D ** (-0.5)
LEAD = 3
LEAD_EARLY = 6
INF = float("inf")

SLOTS = 12


def kernel(n_outer, n_inner, q_hbm, k_hbm, v_hbm, st_hbm, o_hbm, q_vm, kv, o_vm, st, diagonal,
           q_sem, own_sem, st_sem, o_sem, recv, send):
    g = lax.axis_index("outer")
    s = lax.axis_index("inner")
    g_next, g_prev = lax.rem(g + 1, n_outer), lax.rem(g + n_outer - 1, n_outer)

    def shard(distance):
        return lax.rem(s + distance + n_inner, n_inner)

    even = lax.rem(s, 2) == 0
    odd = lax.rem(s, 2) == 1

    def own_copies(h):
        columns = pl.ds(pl.multiple_of(h * D, D), D)
        return [
            pltpu.make_async_copy(
                ref.at[pl.ds(T * (1 - slot), T), columns], kv.at[h, i, slot], own_sem.at[h]
            )
            for i, ref in enumerate((k_hbm, v_hbm))
            for slot in range(2)
        ]

    @pl.loop(0, KVH)
    def _(h):
        for copy in own_copies(h):
            copy.start()

    st_copies = [
        pltpu.make_async_copy(st_hbm.at[group], st.at[i], st_sem.at[i])
        for i, group in enumerate((g, g_prev))
    ]
    for copy in st_copies:
        copy.start()
    q_copy = pltpu.make_async_copy(q_hbm, q_vm, q_sem)
    q_copy.start()

    @pl.when(s == 2)
    def _():
        kv[:, :, 7:9] = jnp.zeros((KVH, 2, 2, T, D), kv.dtype)

    @pl.when(s == 1)
    def _():
        kv[:, :, 7:8] = jnp.zeros((KVH, 2, 1, T, D), kv.dtype)

    half = n_inner // 2
    at_end = lax.rem(s, half) >= half - 2
    at_start = lax.rem(s, half) < 2
    flip = lax.rem(s + half, n_inner)
    ring_on = lax.rem(s + 2, half) + half * (s // half)
    ring_back = lax.rem(s + half - 2, half) + half * (s // half)
    last, lends = s >= n_inner - 2, at_end & (s < half)
    before_last = s == n_inner - 4

    rows_y = n_outer // 2
    y_first, y_last = lax.rem(g, rows_y) == 0, lax.rem(g, rows_y) == rows_y - 1
    turns, turned = y_last & at_start, y_first & at_start
    far = lax.rem(g + rows_y, n_outer)
    turn = lax.rem(g_next + rows_y, n_outer)

    def turns_for(h):
        return jnp.where(s < 2, lax.rem(h, 4) == 1, lax.rem(h, 2) == 1)

    def detours(h):
        return jnp.where(y_first | y_last, lax.rem(h, 2) == 1, lax.rem(h, 3) == 1)

    barrier = pltpu.get_barrier_semaphore()

    def greet(group, inner):
        pl.semaphore_signal(barrier, inc=1, device_id=(group, inner), device_id_type=MESH)

    greet(g_prev, s)
    greet(g, shard(-2))
    greet(g, shard(-1))

    @pl.when(even)
    def _():
        greet(g, shard(1))

    @pl.when(s < 2)
    def _():
        greet(g, ring_back)

    @pl.when(s == 0)
    def _():
        greet(g, shard(-4))
        greet(g, shard(2))

    @pl.when(lends)
    def _():
        greet(g, flip)

    @pl.when(turned)
    def _():
        greet(far, s)
        greet(lax.rem(g + n_outer + rows_y - 1, n_outer), s)

    count = 3 + lax.rem(s, 2)
    for extra in (last, lends, before_last, s == 2, turns, turned):
        count += extra.astype(jnp.int32)
    pl.semaphore_wait(barrier, count)

    def remote(h, src, dst, sem, target):
        return pltpu.make_async_remote_copy(
            src_ref=kv.at[h, :, src],
            dst_ref=kv.at[h, :, dst],
            send_sem=send.at[sem, h],
            recv_sem=recv.at[dst, h],
            device_id=target,
            device_id_type=MESH,
        )

    def pair(h, src, dst, sem, group):
        return pltpu.make_async_remote_copy(
            src_ref=kv.at[h, :, pl.ds(src, 2)],
            dst_ref=kv.at[h, :, pl.ds(dst, 2)],
            send_sem=send.at[sem, h],
            recv_sem=recv.at[dst, h],
            device_id=(group, s),
            device_id_type=MESH,
        )

    def to_next_group(h, act):
        turning = turns & turns_for(h)

        @pl.when(turning)
        def _():
            act(pair(h, 0, 10, 0, turn))

        @pl.when(jnp.logical_not(turning))
        def _():
            act(pair(h, 0, 5, 0, g_next))

    def from_turn(h):
        return pair(h, 10, 5, 11, far)

    me = (g, s)
    two_on, one_on, one_back = (g, shard(2)), (g, shard(1)), (g, shard(-1))
    via, beside = (g, flip), (g, ring_on)

    def first(h):
        detour = last & detours(h)
        straight = jnp.logical_not(detour)
        return [
            (straight, 1, 3, 1, two_on),
            (last & straight, 0, 8, 2, two_on),
            (detour, 1, 11, 1, via),
            (detour, 0, 10, 2, via),
            (even, 1, 2, 3, one_on),
            (s == n_inner - 3, 0, 7, 2, one_back),
        ]

    passed = [
        (None, 3, 4, 4, one_on),
        (s < 2, 8, 9, 5, one_on),
        (odd, 3, 2, 6, one_back),
    ]
    passed_high = [
        (s == 2, 9, 7, 8, (g, shard(-2))),
        (before_last, 7, 9, 8, (g, shard(4))),
    ]
    between = [(None, 11, 3, 9, beside), (None, 10, 8, 10, beside)]

    def each(table, h, act):
        for condition, *entry in table:
            if condition is None:
                act(remote(h, *entry))
            else:
                @pl.when(condition)
                def _(entry=entry):
                    act(remote(h, *entry))

    def send_own(h):
        pltpu.make_async_copy(kv.at[h, :, pl.ds(0, 2)], kv.at[h, :, pl.ds(0, 2)], own_sem.at[h]).wait()
        each(first(h), h, lambda copy: copy.start())

    def send_on(h):
        to_next_group(h, lambda copy: copy.start())

    for h in range(LEAD):
        send_own(h)
        send_on(h)

    early = lax.rem(s, half) >= half - 4

    @pl.when(early)
    def _():
        @pl.loop(LEAD, LEAD_EARLY)
        def _(h):
            send_own(h)

    lead = LEAD + turns.astype(jnp.int32)

    @pl.when(turns)
    def _():
        send_own(LEAD)
        send_on(LEAD)

    def send_ahead(h):
        @pl.when(jnp.logical_not(early) & (h + lead < KVH))
        def _():
            send_own(h + lead)

        @pl.when(early & (h + LEAD_EARLY < KVH))
        def _():
            send_own(h + LEAD_EARLY)

        @pl.when(h + lead < KVH)
        def _():
            send_on(h + lead)

    def arrived(h, dst):
        remote(h, dst, dst, 0, me).wait_recv()

    def pass_on(h):
        arrived(h, 3)

        @pl.when(s < 2)
        def _():
            arrived(h, 8)

        each(passed, h, lambda copy: copy.start())

    def pass_high(h):
        @pl.when(s == 2)
        def _():
            arrived(h, 9)

        @pl.when(before_last)
        def _():
            arrived(h, 7)

        each(passed_high, h, lambda copy: copy.start())

    def relay(h):
        @pl.when(lends & detours(h))
        def _():
            arrived(h, 11)
            arrived(h, 10)
            each(between, h, lambda copy: copy.start())

    def pass_turn(h):
        @pl.when(turned & turns_for(h))
        def _():
            pair(h, 10, 10, 0, g).wait_recv()
            from_turn(h).start()

    seam = at_end | (s < 2)
    passes_high = (s == 2) | before_last
    for h in range(4):
        relay(h)
    pass_on(0)

    @pl.when(seam)
    def _():
        pass_on(1)
        pass_on(2)

    @pl.when(passes_high)
    def _():
        pass_high(0)
        pass_high(1)

    @pl.when(before_last)
    def _():
        pass_high(2)

    pass_turn(1)

    for copy in st_copies:
        copy.wait()
    other = jnp.where(st[1, 0:1, 0:1] < st[0, 0:1, 0:1], INF, -INF).astype(jnp.float32)
    row = lax.broadcasted_iota(jnp.int32, (T, REP * T), 0)
    query = lax.rem(lax.broadcasted_iota(jnp.int32, (T, REP * T), 1), T)
    diagonal[...] = jnp.where(row <= query, INF, -INF).astype(jnp.float32)

    q_copy.wait()

    def columns(h, r):
        return pl.ds(pl.multiple_of(h * (REP * D) + r * D, D), D)

    def attend(h, wrapped):
        slots = 10 if wrapped else 7
        q = jnp.concatenate(
            [q_vm[row0:row0 + T, columns(h, r)] for row0 in (0, T) for r in range(REP)], axis=0
        )
        keys = kv[h, 0, 0:slots].reshape(slots * T, D)
        values = kv[h, 1, 0:slots].reshape(slots * T, D)
        results = []
        for c in range(2 * REP * T // 256):
            scores = lax.dot_general(
                keys, q[c * 256:(c + 1) * 256], (((1,), (1,)), ((), ())), preferred_element_type=jnp.float32
            )
            blocks, sums = [], []
            for b in range(2):
                block = 2 * c + b
                high = block >= 3
                lanes = slice((block % 3) * 128, (block % 3 + 1) * 128)
                parts = [scores[slot * T:(slot + 1) * T, b * 128:(b + 1) * 128] for slot in range(slots)]
                own = 0 if high else 1
                parts[own] = jnp.minimum(parts[own], diagonal[:, lanes])
                for slot in (5, 6):
                    parts[slot] = jnp.minimum(parts[slot], other)
                for j in range(1, 4):
                    if wrapped and high:
                        parts[6 + j] = jnp.minimum(parts[6 + j], jnp.where(s < j, INF, -INF))
                    if wrapped and not high:
                        parts[1 + j] = jnp.minimum(parts[1 + j], jnp.where(s >= j, INF, -INF))
                        parts[6 + j] = None
                if not high:
                    parts[0] = None
                top = None
                for part in parts:
                    if part is not None:
                        peak = jnp.max(part, axis=0, keepdims=True)
                        top = peak if top is None else jnp.maximum(top, peak)
                total, rounded = None, []
                for part in parts:
                    if part is None:
                        rounded.append(jnp.zeros((T, 128), jnp.bfloat16))
                    else:
                        weights = jnp.exp((part - top) * SCALE)
                        here = jnp.sum(weights, axis=0, keepdims=True)
                        total = here if total is None else total + here
                        rounded.append(weights.astype(jnp.bfloat16))
                blocks.append(jnp.concatenate(rounded, axis=0))
                sums.append(total)
            weighted = lax.dot_general(
                values, jnp.concatenate(blocks, axis=1), (((0,), (0,)), ((), ())), preferred_element_type=jnp.float32
            )
            results.append((weighted / jnp.concatenate(sums, axis=1)).T.astype(o_vm.dtype))
        result = jnp.concatenate(results, axis=0)
        for half_index in range(2):
            for r in range(REP):
                start = (half_index * REP + r) * T
                o_vm[half_index * T:(half_index + 1) * T, columns(h, r)] = result[start:start + T]

    def out_copy(h):
        columns = pl.ds(pl.multiple_of(h * (REP * D), REP * D), REP * D)
        return pltpu.make_async_copy(o_vm.at[:, columns], o_hbm.at[:, columns], o_sem.at[h])

    @pl.loop(0, KVH)
    def _(h):
        @pl.when(h + 4 < KVH)
        def _():
            relay(h + 4)

        @pl.when(seam & (h + 3 < KVH))
        def _():
            pass_on(h + 3)

        @pl.when(before_last & (h + 3 < KVH))
        def _():
            pass_high(h + 3)

        @pl.when((s == 2) & (h + 2 < KVH))
        def _():
            pass_high(h + 2)

        send_ahead(h)

        @pl.when(h + 2 < KVH)
        def _():
            pass_turn(h + 2)

        @pl.when(jnp.logical_not(seam) & (h + 1 < KVH))
        def _():
            pass_on(h + 1)

        arrived(h, 2)
        arrived(h, 4)

        @pl.when(s == 0)
        def _():
            arrived(h, 7)

        @pl.when(s < 2)
        def _():
            arrived(h, 9)

        pair(h, 5, 5, 0, g).wait_recv()

        @pl.when(s >= 3)
        def _():
            attend(h, False)

        @pl.when(s < 3)
        def _():
            attend(h, True)

        out_copy(h).start()

    @pl.loop(0, KVH)
    def _(h):
        to_next_group(h, lambda copy: copy.wait_send())
        each(first(h), h, lambda copy: copy.wait_send())
        each(passed, h, lambda copy: copy.wait_send())
        each(passed_high, h, lambda copy: copy.wait_send())

        @pl.when(lends & detours(h))
        def _():
            each(between, h, lambda copy: copy.wait_send())

        @pl.when(turned & turns_for(h))
        def _():
            from_turn(h).wait_send()

        out_copy(h).wait()


def solution(mesh):
    n_outer, n_inner = mesh.shape["outer"], mesh.shape["inner"]

    def on_device(queries, keys, values, stretch_of):
        rows, width = queries.shape
        any_space = pl.BlockSpec(memory_space=pl.ANY)
        return pl.pallas_call(
            lambda *refs: kernel(n_outer, n_inner, *refs),
            out_shape=jax.ShapeDtypeStruct((rows, width), jnp.bfloat16),
            in_specs=[any_space] * 4,
            out_specs=any_space,
            scratch_shapes=[
                pltpu.VMEM((rows, width), jnp.bfloat16),
                pltpu.VMEM((KVH, 2, SLOTS, T, D), jnp.bfloat16),
                pltpu.VMEM((rows, width), jnp.bfloat16),
                pltpu.VMEM((2, 2, n_inner), jnp.int32),
                pltpu.VMEM((T, REP * T), jnp.float32),
                pltpu.SemaphoreType.DMA,
                pltpu.SemaphoreType.DMA((KVH,)),
                pltpu.SemaphoreType.DMA((2,)),
                pltpu.SemaphoreType.DMA((KVH,)),
                pltpu.SemaphoreType.DMA((SLOTS, KVH)),
                pltpu.SemaphoreType.DMA((12, KVH)),
            ],
            compiler_params=pltpu.CompilerParams(
                collective_id=0, has_side_effects=True, vmem_limit_bytes=48 * 1024 * 1024
            ),
            cost_estimate=pl.CostEstimate(flops=2 * 10**9, bytes_accessed=6 * 10**6, transcendentals=4 * 10**6),
        )(*(
            pltpu.with_memory_space_constraint(array, pltpu.HBM)
            for array in (queries, keys, values, stretch_of.transpose(0, 2, 1))
        ))

    rows = P(("outer", "inner"), None)
    return jax.shard_map(
        on_device, mesh=mesh, in_specs=(rows, rows, rows, P()), out_specs=rows, check_vma=False
    )
```

```python
import jax
import jax.numpy as jnp
from jax import lax
from jax.experimental import pallas as pl
from jax.experimental.pallas import tpu as pltpu
from jax.sharding import PartitionSpec as P

MESH = pl.DeviceIdType.MESH
KVH = 8
REP = 4
D = 128
T = 96
SCALE = D ** (-0.5)
LEAD = 3
LEAD_EARLY = 6
LEAD_TURN = 6
LOG2_E = 1.4426950408889634
INF = float("inf")

SLOTS = 12


def kernel(n_outer, n_inner, q_hbm, k_hbm, v_hbm, st_hbm, o_hbm, q_vm, kv, o_vm, st, diagonal,
           q_sem, own_sem, st_sem, o_sem, recv, send):
    g = lax.axis_index("outer")
    s = lax.axis_index("inner")
    g_next, g_prev = lax.rem(g + 1, n_outer), lax.rem(g + n_outer - 1, n_outer)

    def shard(distance):
        return lax.rem(s + distance + n_inner, n_inner)

    even = lax.rem(s, 2) == 0
    odd = lax.rem(s, 2) == 1

    def own_copies(h):
        columns = pl.ds(pl.multiple_of(h * D, D), D)
        return [
            pltpu.make_async_copy(
                ref.at[pl.ds(T * (1 - slot), T), columns], kv.at[h, i, slot], own_sem.at[h]
            )
            for i, ref in enumerate((k_hbm, v_hbm))
            for slot in range(2)
        ]

    @pl.loop(0, KVH)
    def _(h):
        for copy in own_copies(h):
            copy.start()

    st_copies = [
        pltpu.make_async_copy(st_hbm.at[group], st.at[i], st_sem.at[i])
        for i, group in enumerate((g, g_prev))
    ]
    for copy in st_copies:
        copy.start()
    q_copy = pltpu.make_async_copy(q_hbm, q_vm, q_sem)
    q_copy.start()

    @pl.when(s == 2)
    def _():
        kv[:, :, 7:9] = jnp.zeros((KVH, 2, 2, T, D), kv.dtype)

    @pl.when(s == 1)
    def _():
        kv[:, :, 7:8] = jnp.zeros((KVH, 2, 1, T, D), kv.dtype)

    half = n_inner // 2
    at_end = lax.rem(s, half) >= half - 2
    at_start = lax.rem(s, half) < 2
    flip = lax.rem(s + half, n_inner)
    ring_on = lax.rem(s + 2, half) + half * (s // half)
    ring_back = lax.rem(s + half - 2, half) + half * (s // half)
    last, lends = s >= n_inner - 2, at_end & (s < half)
    before_last = s == n_inner - 4

    rows_y = n_outer // 2
    y_first, y_last = lax.rem(g, rows_y) == 0, lax.rem(g, rows_y) == rows_y - 1
    turns, turned = y_last & at_start, y_first & at_start
    far = lax.rem(g + rows_y, n_outer)
    turn = lax.rem(g_next + rows_y, n_outer)

    def turns_for(h):
        return jnp.where(s < 2, lax.rem(h, 4) == 1, lax.rem(h, 2) == 1)

    def detours(h):
        return jnp.where(y_first | y_last, lax.rem(h, 2) == 1, lax.rem(h, 3) == 1)

    barrier = pltpu.get_barrier_semaphore()

    def greet(group, inner):
        pl.semaphore_signal(barrier, inc=1, device_id=(group, inner), device_id_type=MESH)

    greet(g_prev, s)
    greet(g, shard(-2))
    greet(g, shard(-1))

    @pl.when(even)
    def _():
        greet(g, shard(1))

    @pl.when(s < 2)
    def _():
        greet(g, ring_back)

    @pl.when(s == 0)
    def _():
        greet(g, shard(-4))
        greet(g, shard(2))

    @pl.when(lends)
    def _():
        greet(g, flip)

    @pl.when(turned)
    def _():
        greet(far, s)
        greet(lax.rem(g + n_outer + rows_y - 1, n_outer), s)

    count = 3 + lax.rem(s, 2)
    for extra in (last, lends, before_last, s == 2, turns, turned):
        count += extra.astype(jnp.int32)
    pl.semaphore_wait(barrier, count)

    def remote(h, src, dst, sem, target):
        return pltpu.make_async_remote_copy(
            src_ref=kv.at[h, :, src],
            dst_ref=kv.at[h, :, dst],
            send_sem=send.at[sem, h],
            recv_sem=recv.at[dst, h],
            device_id=target,
            device_id_type=MESH,
        )

    def pair(h, src, dst, sem, group):
        return pltpu.make_async_remote_copy(
            src_ref=kv.at[h, :, pl.ds(src, 2)],
            dst_ref=kv.at[h, :, pl.ds(dst, 2)],
            send_sem=send.at[sem, h],
            recv_sem=recv.at[dst, h],
            device_id=(group, s),
            device_id_type=MESH,
        )

    def to_next_group(h, act):
        turning = turns & turns_for(h)

        @pl.when(turning)
        def _():
            act(pair(h, 0, 10, 0, turn))

        @pl.when(jnp.logical_not(turning))
        def _():
            act(pair(h, 0, 5, 0, g_next))

    def from_turn(h):
        return pair(h, 10, 5, 11, far)

    me = (g, s)
    two_on, one_on, one_back = (g, shard(2)), (g, shard(1)), (g, shard(-1))
    via, beside = (g, flip), (g, ring_on)

    def first(h):
        detour = last & detours(h)
        straight = jnp.logical_not(detour)
        return [
            (straight, 1, 3, 1, two_on),
            (last & straight, 0, 8, 2, two_on),
            (detour, 1, 11, 1, via),
            (detour, 0, 10, 2, via),
            (even, 1, 2, 3, one_on),
            (s == n_inner - 3, 0, 7, 2, one_back),
        ]

    passed = [
        (None, 3, 4, 4, one_on),
        (s < 2, 8, 9, 5, one_on),
        (odd, 3, 2, 6, one_back),
    ]
    passed_high = [
        (s == 2, 9, 7, 8, (g, shard(-2))),
        (before_last, 7, 9, 8, (g, shard(4))),
    ]
    between = [(None, 11, 3, 9, beside), (None, 10, 8, 10, beside)]

    def each(table, h, act):
        for condition, *entry in table:
            if condition is None:
                act(remote(h, *entry))
            else:
                @pl.when(condition)
                def _(entry=entry):
                    act(remote(h, *entry))

    def send_own(h):
        pltpu.make_async_copy(kv.at[h, :, pl.ds(0, 2)], kv.at[h, :, pl.ds(0, 2)], own_sem.at[h]).wait()
        each(first(h), h, lambda copy: copy.start())

    def send_on(h):
        to_next_group(h, lambda copy: copy.start())

    for h in range(LEAD):
        send_own(h)
        send_on(h)

    early = lax.rem(s, half) >= half - 4

    @pl.when(early)
    def _():
        @pl.loop(LEAD, LEAD_EARLY)
        def _(h):
            send_own(h)

    lead = jnp.where(turns, LEAD_TURN, LEAD)

    @pl.when(turns)
    def _():
        @pl.loop(LEAD, LEAD_TURN)
        def _(h):
            send_own(h)
            send_on(h)

    def send_ahead(h):
        @pl.when(jnp.logical_not(early) & (h + lead < KVH))
        def _():
            send_own(h + lead)

        @pl.when(early & (h + LEAD_EARLY < KVH))
        def _():
            send_own(h + LEAD_EARLY)

        @pl.when(h + lead < KVH)
        def _():
            send_on(h + lead)

    def arrived(h, dst):
        remote(h, dst, dst, 0, me).wait_recv()

    def pass_on(h):
        arrived(h, 3)

        @pl.when(s < 2)
        def _():
            arrived(h, 8)

        each(passed, h, lambda copy: copy.start())

    def pass_high(h):
        @pl.when(s == 2)
        def _():
            arrived(h, 9)

        @pl.when(before_last)
        def _():
            arrived(h, 7)

        each(passed_high, h, lambda copy: copy.start())

    def relay(h):
        @pl.when(lends & detours(h))
        def _():
            arrived(h, 11)
            arrived(h, 10)
            each(between, h, lambda copy: copy.start())

    def pass_turn(h):
        @pl.when(turned & turns_for(h))
        def _():
            pair(h, 10, 10, 0, g).wait_recv()
            from_turn(h).start()

    seam = at_end | (s < 2)
    passes_high = (s == 2) | before_last
    for h in range(4):
        relay(h)
    pass_on(0)

    @pl.when(seam)
    def _():
        pass_on(1)
        pass_on(2)

    @pl.when(passes_high)
    def _():
        pass_high(0)
        pass_high(1)

    @pl.when(before_last)
    def _():
        pass_high(2)

    pass_turn(1)
    pass_turn(3)

    for copy in st_copies:
        copy.wait()
    other = jnp.where(st[1, 0:1, 0:1] < st[0, 0:1, 0:1], INF, -INF).astype(jnp.float32)
    row = lax.broadcasted_iota(jnp.int32, (T, REP * T), 0)
    query = lax.rem(lax.broadcasted_iota(jnp.int32, (T, REP * T), 1), T)
    diagonal[...] = jnp.where(row <= query, INF, -INF).astype(jnp.float32)

    q_copy.wait()

    def columns(h, r):
        return pl.ds(pl.multiple_of(h * (REP * D) + r * D, D), D)

    def attend(h, wrapped):
        q = jnp.concatenate(
            [q_vm[row0:row0 + T, columns(h, r)] for row0 in (0, T) for r in range(REP)], axis=0
        )
        results = []
        for c in range(2 * REP * T // 256):
            slots = 10 if wrapped and c > 0 else 7
            keys = kv[h, 0, 0:slots].reshape(slots * T, D)
            values = kv[h, 1, 0:slots].reshape(slots * T, D)
            scores = lax.dot_general(
                keys, q[c * 256:(c + 1) * 256], (((1,), (1,)), ((), ())), preferred_element_type=jnp.float32
            )
            blocks, sums = [], []
            for b in range(2):
                block = 2 * c + b
                high = block >= 3
                lanes = slice((block % 3) * 128, (block % 3 + 1) * 128)
                parts = [scores[slot * T:(slot + 1) * T, b * 128:(b + 1) * 128] for slot in range(slots)]
                own = 0 if high else 1
                parts[own] = jnp.minimum(parts[own], diagonal[:, lanes])
                for slot in (5, 6):
                    parts[slot] = jnp.minimum(parts[slot], other)
                for j in range(1, 4):
                    if wrapped and high:
                        parts[6 + j] = jnp.minimum(parts[6 + j], jnp.where(s < j, INF, -INF))
                    if wrapped and not high:
                        parts[1 + j] = jnp.minimum(parts[1 + j], jnp.where(s >= j, INF, -INF))
                        if slots > 7:
                            parts[6 + j] = None
                if not high:
                    parts[0] = None
                top = None
                for part in parts:
                    if part is not None:
                        peak = jnp.max(part, axis=0, keepdims=True)
                        top = peak if top is None else jnp.maximum(top, peak)
                total, rounded = None, []
                for part in parts:
                    if part is None:
                        rounded.append(jnp.zeros((T, 128), jnp.bfloat16))
                    else:
                        weights = jnp.exp2((part - top) * (SCALE * LOG2_E))
                        here = jnp.sum(weights, axis=0, keepdims=True)
                        total = here if total is None else total + here
                        rounded.append(weights.astype(jnp.bfloat16))
                blocks.append(jnp.concatenate(rounded, axis=0))
                sums.append(total)
            weighted = lax.dot_general(
                values, jnp.concatenate(blocks, axis=1), (((0,), (0,)), ((), ())), preferred_element_type=jnp.float32
            )
            results.append((weighted / jnp.concatenate(sums, axis=1)).T.astype(o_vm.dtype))
        result = jnp.concatenate(results, axis=0)
        for half_index in range(2):
            for r in range(REP):
                start = (half_index * REP + r) * T
                o_vm[half_index * T:(half_index + 1) * T, columns(h, r)] = result[start:start + T]

    def out_copy(h):
        columns = pl.ds(pl.multiple_of(h * (REP * D), REP * D), REP * D)
        return pltpu.make_async_copy(o_vm.at[:, columns], o_hbm.at[:, columns], o_sem.at[h])

    @pl.loop(0, KVH)
    def _(h):
        @pl.when(h + 4 < KVH)
        def _():
            relay(h + 4)

        @pl.when(seam & (h + 3 < KVH))
        def _():
            pass_on(h + 3)

        @pl.when(before_last & (h + 3 < KVH))
        def _():
            pass_high(h + 3)

        @pl.when((s == 2) & (h + 2 < KVH))
        def _():
            pass_high(h + 2)

        send_ahead(h)

        @pl.when(h + 4 < KVH)
        def _():
            pass_turn(h + 4)

        @pl.when(jnp.logical_not(seam) & (h + 1 < KVH))
        def _():
            pass_on(h + 1)

        arrived(h, 2)
        arrived(h, 4)

        @pl.when(s == 0)
        def _():
            arrived(h, 7)

        @pl.when(s < 2)
        def _():
            arrived(h, 9)

        pair(h, 5, 5, 0, g).wait_recv()

        @pl.when(s >= 3)
        def _():
            attend(h, False)

        @pl.when(s < 3)
        def _():
            attend(h, True)

        out_copy(h).start()

    @pl.loop(0, KVH)
    def _(h):
        to_next_group(h, lambda copy: copy.wait_send())
        each(first(h), h, lambda copy: copy.wait_send())
        each(passed, h, lambda copy: copy.wait_send())
        each(passed_high, h, lambda copy: copy.wait_send())

        @pl.when(lends & detours(h))
        def _():
            each(between, h, lambda copy: copy.wait_send())

        @pl.when(turned & turns_for(h))
        def _():
            from_turn(h).wait_send()

        out_copy(h).wait()


def solution(mesh):
    n_outer, n_inner = mesh.shape["outer"], mesh.shape["inner"]

    def on_device(queries, keys, values, stretch_of):
        rows, width = queries.shape
        any_space = pl.BlockSpec(memory_space=pl.ANY)
        return pl.pallas_call(
            lambda *refs: kernel(n_outer, n_inner, *refs),
            out_shape=jax.ShapeDtypeStruct((rows, width), jnp.bfloat16),
            in_specs=[any_space] * 4,
            out_specs=any_space,
            scratch_shapes=[
                pltpu.VMEM((rows, width), jnp.bfloat16),
                pltpu.VMEM((KVH, 2, SLOTS, T, D), jnp.bfloat16),
                pltpu.VMEM((rows, width), jnp.bfloat16),
                pltpu.VMEM((2, 2, n_inner), jnp.int32),
                pltpu.VMEM((T, REP * T), jnp.float32),
                pltpu.SemaphoreType.DMA,
                pltpu.SemaphoreType.DMA((KVH,)),
                pltpu.SemaphoreType.DMA((2,)),
                pltpu.SemaphoreType.DMA((KVH,)),
                pltpu.SemaphoreType.DMA((SLOTS, KVH)),
                pltpu.SemaphoreType.DMA((12, KVH)),
            ],
            compiler_params=pltpu.CompilerParams(
                collective_id=0, has_side_effects=True, vmem_limit_bytes=48 * 1024 * 1024
            ),
            cost_estimate=pl.CostEstimate(flops=2 * 10**9, bytes_accessed=6 * 10**6, transcendentals=4 * 10**6),
        )(*(
            pltpu.with_memory_space_constraint(array, pltpu.HBM)
            for array in (queries, keys, values, stretch_of.transpose(0, 2, 1))
        ))

    rows = P(("outer", "inner"), None)
    return jax.shard_map(
        on_device, mesh=mesh, in_specs=(rows, rows, rows, P()), out_specs=rows, check_vma=False
    )
```

```python
import jax
import jax.numpy as jnp
from jax import lax
from jax.experimental import pallas as pl
from jax.experimental.pallas import tpu as pltpu
from jax.sharding import PartitionSpec as P

MESH = pl.DeviceIdType.MESH
KVH = 8
REP = 4
D = 128
T = 96
SCALE = D ** (-0.5)
LEAD = 3
LEAD_EARLY = 6
LEAD_TURN = 6
LOG2_E = 1.4426950408889634
INF = float("inf")

SLOTS = 12


def kernel(n_outer, n_inner, q_hbm, k_hbm, v_hbm, st_hbm, o_hbm, q_vm, kv, o_vm, st, diagonal,
           q_sem, own_sem, st_sem, o_sem, recv, send):
    g = lax.axis_index("outer")
    s = lax.axis_index("inner")
    g_next, g_prev = lax.rem(g + 1, n_outer), lax.rem(g + n_outer - 1, n_outer)

    def shard(distance):
        return lax.rem(s + distance + n_inner, n_inner)

    even = lax.rem(s, 2) == 0
    odd = lax.rem(s, 2) == 1

    def own_copies(h):
        columns = pl.ds(pl.multiple_of(h * D, D), D)
        return [
            pltpu.make_async_copy(
                ref.at[pl.ds(T * (1 - slot), T), columns], kv.at[h, i, slot], own_sem.at[h]
            )
            for i, ref in enumerate((k_hbm, v_hbm))
            for slot in range(2)
        ]

    @pl.loop(0, KVH)
    def _(h):
        for copy in own_copies(h):
            copy.start()

    st_copies = [
        pltpu.make_async_copy(st_hbm.at[group], st.at[i], st_sem.at[i])
        for i, group in enumerate((g, g_prev))
    ]
    for copy in st_copies:
        copy.start()
    q_copy = pltpu.make_async_copy(q_hbm, q_vm, q_sem)
    q_copy.start()

    @pl.when(s == 2)
    def _():
        kv[:, :, 7:9] = jnp.zeros((KVH, 2, 2, T, D), kv.dtype)

    @pl.when(s == 1)
    def _():
        kv[:, :, 7:8] = jnp.zeros((KVH, 2, 1, T, D), kv.dtype)

    half = n_inner // 2
    at_end = lax.rem(s, half) >= half - 2
    at_start = lax.rem(s, half) < 2
    flip = lax.rem(s + half, n_inner)
    ring_on = lax.rem(s + 2, half) + half * (s // half)
    ring_back = lax.rem(s + half - 2, half) + half * (s // half)
    last, lends = s >= n_inner - 2, at_end & (s < half)
    before_last = s == n_inner - 4

    rows_y = n_outer // 2
    y_first, y_last = lax.rem(g, rows_y) == 0, lax.rem(g, rows_y) == rows_y - 1
    turns = y_last & at_start
    turned = y_first & (lax.rem(s, half) >= 2) & (lax.rem(s, half) < 4)

    def turns_for(h):
        return jnp.where(s < 4, lax.rem(h, 4) == 1, lax.rem(h, 2) == 1)

    def detours(h):
        return jnp.where(y_last, lax.rem(h, 2) == 1, lax.rem(h, 3) == 1)

    barrier = pltpu.get_barrier_semaphore()

    def greet(group, inner):
        pl.semaphore_signal(barrier, inc=1, device_id=(group, inner), device_id_type=MESH)

    greet(g_prev, s)
    greet(g, shard(-2))
    greet(g, shard(-1))

    @pl.when(even)
    def _():
        greet(g, shard(1))

    @pl.when(s < 2)
    def _():
        greet(g, ring_back)

    @pl.when(s == 0)
    def _():
        greet(g, shard(-4))
        greet(g, shard(2))

    @pl.when(lends)
    def _():
        greet(g, flip)

    @pl.when(turned)
    def _():
        greet(g_prev, shard(-2))

    @pl.when(y_first & at_start)
    def _():
        greet(g, shard(2))

    count = 3 + lax.rem(s, 2)
    for extra in (last, lends, before_last, s == 2, turns, turned):
        count += extra.astype(jnp.int32)
    pl.semaphore_wait(barrier, count)

    def remote(h, src, dst, sem, target):
        return pltpu.make_async_remote_copy(
            src_ref=kv.at[h, :, src],
            dst_ref=kv.at[h, :, dst],
            send_sem=send.at[sem, h],
            recv_sem=recv.at[dst, h],
            device_id=target,
            device_id_type=MESH,
        )

    def pair(h, src, dst, sem, target):
        return pltpu.make_async_remote_copy(
            src_ref=kv.at[h, :, pl.ds(src, 2)],
            dst_ref=kv.at[h, :, pl.ds(dst, 2)],
            send_sem=send.at[sem, h],
            recv_sem=recv.at[dst, h],
            device_id=target,
            device_id_type=MESH,
        )

    def to_next_group(h, act):
        turning = turns & turns_for(h)

        @pl.when(turning)
        def _():
            act(pair(h, 0, 10, 0, (g_next, shard(2))))

        @pl.when(jnp.logical_not(turning))
        def _():
            act(pair(h, 0, 5, 0, (g_next, s)))

    def from_turn(h):
        return pair(h, 10, 5, 11, (g, shard(-2)))

    me = (g, s)
    two_on, one_on, one_back = (g, shard(2)), (g, shard(1)), (g, shard(-1))
    via, beside = (g, flip), (g, ring_on)

    def first(h):
        detour = last & detours(h)
        straight = jnp.logical_not(detour)
        return [
            (straight, 1, 3, 1, two_on),
            (last & straight, 0, 8, 2, two_on),
            (detour, 1, 11, 1, via),
            (detour, 0, 10, 2, via),
            (even, 1, 2, 3, one_on),
            (s == n_inner - 3, 0, 7, 2, one_back),
        ]

    passed = [
        (None, 3, 4, 4, one_on),
        (s < 2, 8, 9, 5, one_on),
        (odd, 3, 2, 6, one_back),
    ]
    passed_high = [
        (s == 2, 9, 7, 8, (g, shard(-2))),
        (before_last, 7, 9, 8, (g, shard(4))),
    ]
    between = [(None, 11, 3, 9, beside), (None, 10, 8, 10, beside)]

    def each(table, h, act):
        for condition, *entry in table:
            if condition is None:
                act(remote(h, *entry))
            else:
                @pl.when(condition)
                def _(entry=entry):
                    act(remote(h, *entry))

    def send_own(h):
        pltpu.make_async_copy(kv.at[h, :, pl.ds(0, 2)], kv.at[h, :, pl.ds(0, 2)], own_sem.at[h]).wait()
        each(first(h), h, lambda copy: copy.start())

    def send_on(h):
        to_next_group(h, lambda copy: copy.start())

    for h in range(LEAD):
        send_own(h)
        send_on(h)

    early = lax.rem(s, half) >= half - 4

    @pl.when(early)
    def _():
        @pl.loop(LEAD, LEAD_EARLY)
        def _(h):
            send_own(h)

    lead = jnp.where(turns, LEAD_TURN, LEAD)

    @pl.when(turns)
    def _():
        @pl.loop(LEAD, LEAD_TURN)
        def _(h):
            send_own(h)
            send_on(h)

    def send_ahead(h):
        @pl.when(jnp.logical_not(early) & (h + lead < KVH))
        def _():
            send_own(h + lead)

        @pl.when(early & (h + LEAD_EARLY < KVH))
        def _():
            send_own(h + LEAD_EARLY)

        @pl.when(h + lead < KVH)
        def _():
            send_on(h + lead)

    def arrived(h, dst):
        remote(h, dst, dst, 0, me).wait_recv()

    def pass_on(h):
        arrived(h, 3)

        @pl.when(s < 2)
        def _():
            arrived(h, 8)

        each(passed, h, lambda copy: copy.start())

    def pass_high(h):
        @pl.when(s == 2)
        def _():
            arrived(h, 9)

        @pl.when(before_last)
        def _():
            arrived(h, 7)

        each(passed_high, h, lambda copy: copy.start())

    def relay(h):
        @pl.when(lends & detours(h))
        def _():
            arrived(h, 11)
            arrived(h, 10)
            each(between, h, lambda copy: copy.start())

    def pass_turn(h):
        @pl.when(turned & turns_for(h))
        def _():
            pair(h, 10, 10, 0, me).wait_recv()
            from_turn(h).start()

    seam = at_end | (s < 2)
    passes_high = (s == 2) | before_last
    for h in range(4):
        relay(h)
    pass_on(0)

    @pl.when(seam)
    def _():
        pass_on(1)
        pass_on(2)

    @pl.when(passes_high)
    def _():
        pass_high(0)
        pass_high(1)

    @pl.when(before_last)
    def _():
        pass_high(2)

    pass_turn(1)
    pass_turn(3)

    for copy in st_copies:
        copy.wait()
    other = jnp.where(st[1, 0:1, 0:1] < st[0, 0:1, 0:1], INF, -INF).astype(jnp.float32)
    row = lax.broadcasted_iota(jnp.int32, (T, REP * T), 0)
    query = lax.rem(lax.broadcasted_iota(jnp.int32, (T, REP * T), 1), T)
    diagonal[...] = jnp.where(row <= query, INF, -INF).astype(jnp.float32)

    q_copy.wait()

    def columns(h, r):
        return pl.ds(pl.multiple_of(h * (REP * D) + r * D, D), D)

    def attend(h, wrapped):
        q = jnp.concatenate(
            [q_vm[row0:row0 + T, columns(h, r)] for row0 in (0, T) for r in range(REP)], axis=0
        )
        results = []
        for c in range(2 * REP * T // 256):
            slots = 10 if wrapped and c > 0 else 7
            keys = kv[h, 0, 0:slots].reshape(slots * T, D)
            values = kv[h, 1, 0:slots].reshape(slots * T, D)
            scores = lax.dot_general(
                keys, q[c * 256:(c + 1) * 256], (((1,), (1,)), ((), ())), preferred_element_type=jnp.float32
            )
            blocks, sums = [], []
            for b in range(2):
                block = 2 * c + b
                high = block >= 3
                lanes = slice((block % 3) * 128, (block % 3 + 1) * 128)
                parts = [scores[slot * T:(slot + 1) * T, b * 128:(b + 1) * 128] for slot in range(slots)]
                own = 0 if high else 1
                parts[own] = jnp.minimum(parts[own], diagonal[:, lanes])
                for slot in (5, 6):
                    parts[slot] = jnp.minimum(parts[slot], other)
                for j in range(1, 4):
                    if wrapped and high:
                        parts[6 + j] = jnp.minimum(parts[6 + j], jnp.where(s < j, INF, -INF))
                    if wrapped and not high:
                        parts[1 + j] = jnp.minimum(parts[1 + j], jnp.where(s >= j, INF, -INF))
                        if slots > 7:
                            parts[6 + j] = None
                if not high:
                    parts[0] = None
                top = None
                for part in parts:
                    if part is not None:
                        peak = jnp.max(part, axis=0, keepdims=True)
                        top = peak if top is None else jnp.maximum(top, peak)
                total, rounded = None, []
                for part in parts:
                    if part is None:
                        rounded.append(jnp.zeros((T, 128), jnp.bfloat16))
                    else:
                        weights = jnp.exp2((part - top) * (SCALE * LOG2_E))
                        here = jnp.sum(weights, axis=0, keepdims=True)
                        total = here if total is None else total + here
                        rounded.append(weights.astype(jnp.bfloat16))
                blocks.append(jnp.concatenate(rounded, axis=0))
                sums.append(total)
            weighted = lax.dot_general(
                values, jnp.concatenate(blocks, axis=1), (((0,), (0,)), ((), ())), preferred_element_type=jnp.float32
            )
            results.append((weighted / jnp.concatenate(sums, axis=1)).T.astype(o_vm.dtype))
        result = jnp.concatenate(results, axis=0)
        for half_index in range(2):
            for r in range(REP):
                start = (half_index * REP + r) * T
                o_vm[half_index * T:(half_index + 1) * T, columns(h, r)] = result[start:start + T]

    def out_copy(h):
        columns = pl.ds(pl.multiple_of(h * (REP * D), REP * D), REP * D)
        return pltpu.make_async_copy(o_vm.at[:, columns], o_hbm.at[:, columns], o_sem.at[h])

    @pl.loop(0, KVH)
    def _(h):
        @pl.when(h + 4 < KVH)
        def _():
            relay(h + 4)

        @pl.when(seam & (h + 3 < KVH))
        def _():
            pass_on(h + 3)

        @pl.when(before_last & (h + 3 < KVH))
        def _():
            pass_high(h + 3)

        @pl.when((s == 2) & (h + 2 < KVH))
        def _():
            pass_high(h + 2)

        send_ahead(h)

        @pl.when(h + 4 < KVH)
        def _():
            pass_turn(h + 4)

        @pl.when(jnp.logical_not(seam) & (h + 1 < KVH))
        def _():
            pass_on(h + 1)

        arrived(h, 2)
        arrived(h, 4)

        @pl.when(s == 0)
        def _():
            arrived(h, 7)

        @pl.when(s < 2)
        def _():
            arrived(h, 9)

        pair(h, 5, 5, 0, me).wait_recv()

        @pl.when(s >= 3)
        def _():
            attend(h, False)

        @pl.when(s < 3)
        def _():
            attend(h, True)

        out_copy(h).start()

    @pl.loop(0, KVH)
    def _(h):
        to_next_group(h, lambda copy: copy.wait_send())
        each(first(h), h, lambda copy: copy.wait_send())
        each(passed, h, lambda copy: copy.wait_send())
        each(passed_high, h, lambda copy: copy.wait_send())

        @pl.when(lends & detours(h))
        def _():
            each(between, h, lambda copy: copy.wait_send())

        @pl.when(turned & turns_for(h))
        def _():
            from_turn(h).wait_send()

        out_copy(h).wait()


def solution(mesh):
    n_outer, n_inner = mesh.shape["outer"], mesh.shape["inner"]

    def on_device(queries, keys, values, stretch_of):
        rows, width = queries.shape
        any_space = pl.BlockSpec(memory_space=pl.ANY)
        return pl.pallas_call(
            lambda *refs: kernel(n_outer, n_inner, *refs),
            out_shape=jax.ShapeDtypeStruct((rows, width), jnp.bfloat16),
            in_specs=[any_space] * 4,
            out_specs=any_space,
            scratch_shapes=[
                pltpu.VMEM((rows, width), jnp.bfloat16),
                pltpu.VMEM((KVH, 2, SLOTS, T, D), jnp.bfloat16),
                pltpu.VMEM((rows, width), jnp.bfloat16),
                pltpu.VMEM((2, 2, n_inner), jnp.int32),
                pltpu.VMEM((T, REP * T), jnp.float32),
                pltpu.SemaphoreType.DMA,
                pltpu.SemaphoreType.DMA((KVH,)),
                pltpu.SemaphoreType.DMA((2,)),
                pltpu.SemaphoreType.DMA((KVH,)),
                pltpu.SemaphoreType.DMA((SLOTS, KVH)),
                pltpu.SemaphoreType.DMA((12, KVH)),
            ],
            compiler_params=pltpu.CompilerParams(
                collective_id=0, has_side_effects=True, vmem_limit_bytes=48 * 1024 * 1024
            ),
            cost_estimate=pl.CostEstimate(flops=2 * 10**9, bytes_accessed=6 * 10**6, transcendentals=4 * 10**6),
        )(*(
            pltpu.with_memory_space_constraint(array, pltpu.HBM)
            for array in (queries, keys, values, stretch_of.transpose(0, 2, 1))
        ))

    rows = P(("outer", "inner"), None)
    return jax.shard_map(
        on_device, mesh=mesh, in_specs=(rows, rows, rows, P()), out_specs=rows, check_vma=False
    )
```

```python
import jax
import jax.numpy as jnp
from jax import lax
from jax.experimental import pallas as pl
from jax.experimental.pallas import tpu as pltpu
from jax.sharding import PartitionSpec as P

MESH = pl.DeviceIdType.MESH
KVH = 8
REP = 4
D = 128
T = 96
SCALE = D ** (-0.5)
LEAD = 3
LEAD_EARLY = 6
LEAD_TURN = 6
LOG2_E = 1.4426950408889634
INF = float("inf")

SLOTS = 12


def kernel(n_outer, n_inner, q_hbm, k_hbm, v_hbm, st_hbm, o_hbm, q_vm, kv, o_vm, st, diagonal,
           q_sem, own_sem, st_sem, o_sem, recv, send):
    g = lax.axis_index("outer")
    s = lax.axis_index("inner")
    g_next, g_prev = lax.rem(g + 1, n_outer), lax.rem(g + n_outer - 1, n_outer)

    def shard(distance):
        return lax.rem(s + distance + n_inner, n_inner)

    even = lax.rem(s, 2) == 0
    odd = lax.rem(s, 2) == 1

    def own_copies(h):
        columns = pl.ds(pl.multiple_of(h * D, D), D)
        return [
            pltpu.make_async_copy(
                ref.at[pl.ds(T * (1 - slot), T), columns], kv.at[h, i, slot], own_sem.at[h]
            )
            for i, ref in enumerate((k_hbm, v_hbm))
            for slot in range(2)
        ]

    @pl.loop(0, KVH)
    def _(h):
        for copy in own_copies(h):
            copy.start()

    st_copies = [
        pltpu.make_async_copy(st_hbm.at[group], st.at[i], st_sem.at[i])
        for i, group in enumerate((g, g_prev))
    ]
    for copy in st_copies:
        copy.start()
    q_copy = pltpu.make_async_copy(q_hbm, q_vm, q_sem)
    q_copy.start()

    @pl.when(s == 2)
    def _():
        kv[:, :, 7:9] = jnp.zeros((KVH, 2, 2, T, D), kv.dtype)

    @pl.when(s == 1)
    def _():
        kv[:, :, 7:8] = jnp.zeros((KVH, 2, 1, T, D), kv.dtype)

    half = n_inner // 2
    at_end = lax.rem(s, half) >= half - 2
    at_start = lax.rem(s, half) < 2
    flip = lax.rem(s + half, n_inner)
    ring_on = lax.rem(s + 2, half) + half * (s // half)
    ring_back = lax.rem(s + half - 2, half) + half * (s // half)
    last, lends = s >= n_inner - 2, at_end & (s < half)
    before_last = s == n_inner - 4

    rows_y = n_outer // 2
    turns = (lax.rem(g, rows_y) == rows_y - 1) & at_start

    def detours(h):
        return lax.rem(h, 3) == 1

    barrier = pltpu.get_barrier_semaphore()

    def greet(group, inner):
        pl.semaphore_signal(barrier, inc=1, device_id=(group, inner), device_id_type=MESH)

    greet(g_prev, s)
    greet(g, shard(-2))
    greet(g, shard(-1))

    @pl.when(even)
    def _():
        greet(g, shard(1))

    @pl.when(s < 2)
    def _():
        greet(g, ring_back)

    @pl.when(s == 0)
    def _():
        greet(g, shard(-4))
        greet(g, shard(2))

    @pl.when(lends)
    def _():
        greet(g, flip)

    count = 3 + lax.rem(s, 2)
    for extra in (last, lends, before_last, s == 2):
        count += extra.astype(jnp.int32)
    pl.semaphore_wait(barrier, count)

    def remote(h, src, dst, sem, target):
        return pltpu.make_async_remote_copy(
            src_ref=kv.at[h, :, src],
            dst_ref=kv.at[h, :, dst],
            send_sem=send.at[sem, h],
            recv_sem=recv.at[dst, h],
            device_id=target,
            device_id_type=MESH,
        )

    def pair(h, src, dst, sem, target):
        return pltpu.make_async_remote_copy(
            src_ref=kv.at[h, :, pl.ds(src, 2)],
            dst_ref=kv.at[h, :, pl.ds(dst, 2)],
            send_sem=send.at[sem, h],
            recv_sem=recv.at[dst, h],
            device_id=target,
            device_id_type=MESH,
        )

    def to_next_group(h):
        return pair(h, 0, 5, 0, (g_next, s))

    me = (g, s)
    two_on, one_on, one_back = (g, shard(2)), (g, shard(1)), (g, shard(-1))
    via, beside = (g, flip), (g, ring_on)

    def first(h):
        detour = last & detours(h)
        straight = jnp.logical_not(detour)
        return [
            (straight, 1, 3, 1, two_on),
            (last & straight, 0, 8, 2, two_on),
            (detour, 1, 11, 1, via),
            (detour, 0, 10, 2, via),
            (even, 1, 2, 3, one_on),
            (s == n_inner - 3, 0, 7, 2, one_back),
        ]

    passed = [
        (None, 3, 4, 4, one_on),
        (s < 2, 8, 9, 5, one_on),
        (odd, 3, 2, 6, one_back),
    ]
    passed_high = [
        (s == 2, 9, 7, 8, (g, shard(-2))),
        (before_last, 7, 9, 8, (g, shard(4))),
    ]
    between = [(None, 11, 3, 9, beside), (None, 10, 8, 10, beside)]

    def each(table, h, act):
        for condition, *entry in table:
            if condition is None:
                act(remote(h, *entry))
            else:
                @pl.when(condition)
                def _(entry=entry):
                    act(remote(h, *entry))

    def send_own(h):
        pltpu.make_async_copy(kv.at[h, :, pl.ds(0, 2)], kv.at[h, :, pl.ds(0, 2)], own_sem.at[h]).wait()
        each(first(h), h, lambda copy: copy.start())

    def send_on(h):
        to_next_group(h).start()

    for h in range(LEAD):
        send_own(h)
        send_on(h)

    early = ((lax.rem(s, half) >= half - 4) | (lax.rem(s, half) < 4)) & jnp.logical_not(turns)

    @pl.when(early)
    def _():
        @pl.loop(LEAD, LEAD_EARLY)
        def _(h):
            send_own(h)

    lead = jnp.where(turns, LEAD_TURN, LEAD)

    @pl.when(turns)
    def _():
        @pl.loop(LEAD, LEAD_TURN)
        def _(h):
            send_own(h)
            send_on(h)

    def send_ahead(h):
        @pl.when(jnp.logical_not(early) & (h + lead < KVH))
        def _():
            send_own(h + lead)

        @pl.when(early & (h + LEAD_EARLY < KVH))
        def _():
            send_own(h + LEAD_EARLY)

        @pl.when(h + lead < KVH)
        def _():
            send_on(h + lead)

    def arrived(h, dst):
        remote(h, dst, dst, 0, me).wait_recv()

    def pass_on(h):
        arrived(h, 3)

        @pl.when(s < 2)
        def _():
            arrived(h, 8)

        each(passed, h, lambda copy: copy.start())

    def pass_high(h):
        @pl.when(s == 2)
        def _():
            arrived(h, 9)

        @pl.when(before_last)
        def _():
            arrived(h, 7)

        each(passed_high, h, lambda copy: copy.start())

    def relay(h):
        @pl.when(lends & detours(h))
        def _():
            arrived(h, 11)
            arrived(h, 10)
            each(between, h, lambda copy: copy.start())

    seam = at_end | (s < 2)
    passes_high = (s == 2) | before_last
    for h in range(4):
        relay(h)
    pass_on(0)

    @pl.when(seam)
    def _():
        pass_on(1)
        pass_on(2)

    @pl.when(passes_high)
    def _():
        pass_high(0)
        pass_high(1)

    @pl.when(before_last)
    def _():
        pass_high(2)


    for copy in st_copies:
        copy.wait()
    other = jnp.where(st[1, 0:1, 0:1] < st[0, 0:1, 0:1], INF, -INF).astype(jnp.float32)
    row = lax.broadcasted_iota(jnp.int32, (T, REP * T), 0)
    query = lax.rem(lax.broadcasted_iota(jnp.int32, (T, REP * T), 1), T)
    diagonal[...] = jnp.where(row <= query, INF, -INF).astype(jnp.float32)

    q_copy.wait()

    def columns(h, r):
        return pl.ds(pl.multiple_of(h * (REP * D) + r * D, D), D)

    def attend(h, wrapped):
        q = jnp.concatenate(
            [q_vm[row0:row0 + T, columns(h, r)] for row0 in (0, T) for r in range(REP)], axis=0
        )
        results = []
        for c in range(2 * REP * T // 256):
            slots = 10 if wrapped and c > 0 else 7
            keys = kv[h, 0, 0:slots].reshape(slots * T, D)
            values = kv[h, 1, 0:slots].reshape(slots * T, D)
            scores = lax.dot_general(
                keys, q[c * 256:(c + 1) * 256], (((1,), (1,)), ((), ())), preferred_element_type=jnp.float32
            )
            blocks, sums = [], []
            for b in range(2):
                block = 2 * c + b
                high = block >= 3
                lanes = slice((block % 3) * 128, (block % 3 + 1) * 128)
                parts = [scores[slot * T:(slot + 1) * T, b * 128:(b + 1) * 128] for slot in range(slots)]
                own = 0 if high else 1
                parts[own] = jnp.minimum(parts[own], diagonal[:, lanes])
                for slot in (5, 6):
                    parts[slot] = jnp.minimum(parts[slot], other)
                for j in range(1, 4):
                    if wrapped and high:
                        parts[6 + j] = jnp.minimum(parts[6 + j], jnp.where(s < j, INF, -INF))
                    if wrapped and not high:
                        parts[1 + j] = jnp.minimum(parts[1 + j], jnp.where(s >= j, INF, -INF))
                        if slots > 7:
                            parts[6 + j] = None
                if not high:
                    parts[0] = None
                top = None
                for part in parts:
                    if part is not None:
                        peak = jnp.max(part, axis=0, keepdims=True)
                        top = peak if top is None else jnp.maximum(top, peak)
                total, rounded = None, []
                for part in parts:
                    if part is None:
                        rounded.append(jnp.zeros((T, 128), jnp.bfloat16))
                    else:
                        weights = jnp.exp2((part - top) * (SCALE * LOG2_E))
                        here = jnp.sum(weights, axis=0, keepdims=True)
                        total = here if total is None else total + here
                        rounded.append(weights.astype(jnp.bfloat16))
                blocks.append(jnp.concatenate(rounded, axis=0))
                sums.append(total)
            weighted = lax.dot_general(
                values, jnp.concatenate(blocks, axis=1), (((0,), (0,)), ((), ())), preferred_element_type=jnp.float32
            )
            results.append((weighted / jnp.concatenate(sums, axis=1)).T.astype(o_vm.dtype))
        result = jnp.concatenate(results, axis=0)
        for half_index in range(2):
            for r in range(REP):
                start = (half_index * REP + r) * T
                o_vm[half_index * T:(half_index + 1) * T, columns(h, r)] = result[start:start + T]

    def out_copy(h):
        columns = pl.ds(pl.multiple_of(h * (REP * D), REP * D), REP * D)
        return pltpu.make_async_copy(o_vm.at[:, columns], o_hbm.at[:, columns], o_sem.at[h])

    @pl.loop(0, KVH)
    def _(h):
        @pl.when(h + 4 < KVH)
        def _():
            relay(h + 4)

        @pl.when(seam & (h + 3 < KVH))
        def _():
            pass_on(h + 3)

        @pl.when(before_last & (h + 3 < KVH))
        def _():
            pass_high(h + 3)

        @pl.when((s == 2) & (h + 2 < KVH))
        def _():
            pass_high(h + 2)

        send_ahead(h)

        @pl.when(jnp.logical_not(seam) & (h + 1 < KVH))
        def _():
            pass_on(h + 1)

        arrived(h, 2)
        arrived(h, 4)

        @pl.when(s == 0)
        def _():
            arrived(h, 7)

        @pl.when(s < 2)
        def _():
            arrived(h, 9)

        pair(h, 5, 5, 0, me).wait_recv()

        @pl.when(s >= 3)
        def _():
            attend(h, False)

        @pl.when(s < 3)
        def _():
            attend(h, True)

        out_copy(h).start()

    @pl.loop(0, KVH)
    def _(h):
        to_next_group(h).wait_send()
        each(first(h), h, lambda copy: copy.wait_send())
        each(passed, h, lambda copy: copy.wait_send())
        each(passed_high, h, lambda copy: copy.wait_send())

        @pl.when(lends & detours(h))
        def _():
            each(between, h, lambda copy: copy.wait_send())

        out_copy(h).wait()


def solution(mesh):
    n_outer, n_inner = mesh.shape["outer"], mesh.shape["inner"]

    def on_device(queries, keys, values, stretch_of):
        rows, width = queries.shape
        any_space = pl.BlockSpec(memory_space=pl.ANY)
        return pl.pallas_call(
            lambda *refs: kernel(n_outer, n_inner, *refs),
            out_shape=jax.ShapeDtypeStruct((rows, width), jnp.bfloat16),
            in_specs=[any_space] * 4,
            out_specs=any_space,
            scratch_shapes=[
                pltpu.VMEM((rows, width), jnp.bfloat16),
                pltpu.VMEM((KVH, 2, SLOTS, T, D), jnp.bfloat16),
                pltpu.VMEM((rows, width), jnp.bfloat16),
                pltpu.VMEM((2, 2, n_inner), jnp.int32),
                pltpu.VMEM((T, REP * T), jnp.float32),
                pltpu.SemaphoreType.DMA,
                pltpu.SemaphoreType.DMA((KVH,)),
                pltpu.SemaphoreType.DMA((2,)),
                pltpu.SemaphoreType.DMA((KVH,)),
                pltpu.SemaphoreType.DMA((SLOTS, KVH)),
                pltpu.SemaphoreType.DMA((12, KVH)),
            ],
            compiler_params=pltpu.CompilerParams(
                collective_id=0, has_side_effects=True, vmem_limit_bytes=48 * 1024 * 1024
            ),
            cost_estimate=pl.CostEstimate(flops=2 * 10**9, bytes_accessed=6 * 10**6, transcendentals=4 * 10**6),
        )(*(
            pltpu.with_memory_space_constraint(array, pltpu.HBM)
            for array in (queries, keys, values, stretch_of.transpose(0, 2, 1))
        ))

    rows = P(("outer", "inner"), None)
    return jax.shard_map(
        on_device, mesh=mesh, in_specs=(rows, rows, rows, P()), out_specs=rows, check_vma=False
    )
```

```python
import jax
import jax.numpy as jnp
from jax import lax
from jax.experimental import pallas as pl
from jax.experimental.pallas import tpu as pltpu
from jax.sharding import PartitionSpec as P

MESH = pl.DeviceIdType.MESH
KVH = 8
REP = 4
D = 128
T = 96
SCALE = D ** (-0.5)
LEAD = 3
LEAD_EARLY = 6
LEAD_TURN = 6
LOG2_E = 1.4426950408889634
INF = float("inf")

SLOTS = 12


def kernel(n_outer, n_inner, q_hbm, k_hbm, v_hbm, st_hbm, o_hbm, q_vm, kv, o_vm, st, diagonal,
           q_sem, own_sem, st_sem, o_sem, recv, send):
    g = lax.axis_index("outer")
    s = lax.axis_index("inner")
    g_next, g_prev = lax.rem(g + 1, n_outer), lax.rem(g + n_outer - 1, n_outer)

    def shard(distance):
        return lax.rem(s + distance + n_inner, n_inner)

    even = lax.rem(s, 2) == 0
    odd = lax.rem(s, 2) == 1

    def own_copies(h):
        columns = pl.ds(pl.multiple_of(h * D, D), D)
        return [
            pltpu.make_async_copy(
                ref.at[pl.ds(T * (1 - slot), T), columns], kv.at[h, i, slot], own_sem.at[h]
            )
            for i, ref in enumerate((k_hbm, v_hbm))
            for slot in range(2)
        ]

    @pl.loop(0, KVH)
    def _(h):
        for copy in own_copies(h):
            copy.start()

    st_copies = [
        pltpu.make_async_copy(st_hbm.at[group], st.at[i], st_sem.at[i])
        for i, group in enumerate((g, g_prev))
    ]
    for copy in st_copies:
        copy.start()
    q_copy = pltpu.make_async_copy(q_hbm, q_vm, q_sem)
    q_copy.start()

    @pl.when(s == 2)
    def _():
        kv[:, :, 7:9] = jnp.zeros((KVH, 2, 2, T, D), kv.dtype)

    @pl.when(s == 1)
    def _():
        kv[:, :, 7:8] = jnp.zeros((KVH, 2, 1, T, D), kv.dtype)

    half = n_inner // 2
    at_end = lax.rem(s, half) >= half - 2
    at_start = lax.rem(s, half) < 2
    flip = lax.rem(s + half, n_inner)
    ring_on = lax.rem(s + 2, half) + half * (s // half)
    ring_back = lax.rem(s + half - 2, half) + half * (s // half)
    last, lends = s >= n_inner - 2, at_end & (s < half)
    before_last = s == n_inner - 4

    rows_y = n_outer // 2
    y_first = lax.rem(g, rows_y) == 0
    turns = (lax.rem(g, rows_y) == rows_y - 1) & at_start
    far, far_next = lax.rem(g + rows_y, n_outer), lax.rem(g_next + rows_y, n_outer)

    turned = (lax.rem(g, rows_y) == rows_y - 1) & (lax.rem(s, half) // 2 == 1)

    def turns_for(h):
        return lax.rem(h, 2) == 1

    def detours(h):
        return lax.rem(h, 3) == 1

    barrier = pltpu.get_barrier_semaphore()

    def greet(group, inner):
        pl.semaphore_signal(barrier, inc=1, device_id=(group, inner), device_id_type=MESH)

    greet(g_prev, s)
    greet(g, shard(-2))
    greet(g, shard(-1))

    @pl.when(even)
    def _():
        greet(g, shard(1))

    @pl.when(s < 2)
    def _():
        greet(g, ring_back)

    @pl.when(s == 0)
    def _():
        greet(g, shard(-4))
        greet(g, shard(2))

    @pl.when(lends)
    def _():
        greet(g, flip)

    @pl.when(turned)
    def _():
        greet(far, shard(-2))

    @pl.when(y_first & at_start)
    def _():
        greet(lax.rem(g_prev + rows_y, n_outer), shard(2))

    count = 3 + lax.rem(s, 2)
    for extra in (last, lends, before_last, s == 2, turns, turned):
        count += extra.astype(jnp.int32)
    pl.semaphore_wait(barrier, count)

    def remote(h, src, dst, sem, target):
        return pltpu.make_async_remote_copy(
            src_ref=kv.at[h, :, src],
            dst_ref=kv.at[h, :, dst],
            send_sem=send.at[sem, h],
            recv_sem=recv.at[dst, h],
            device_id=target,
            device_id_type=MESH,
        )

    def pair(h, src, dst, sem, target):
        return pltpu.make_async_remote_copy(
            src_ref=kv.at[h, :, pl.ds(src, 2)],
            dst_ref=kv.at[h, :, pl.ds(dst, 2)],
            send_sem=send.at[sem, h],
            recv_sem=recv.at[dst, h],
            device_id=target,
            device_id_type=MESH,
        )

    def to_next_group(h, act):
        @pl.when(turns & turns_for(h))
        def _():
            act(pair(h, 0, 10, 0, (far, shard(2))))

        @pl.when(jnp.logical_not(turns & turns_for(h)))
        def _():
            act(pair(h, 0, 5, 0, (g_next, s)))

    def from_turn(h, act):
        @pl.when(turned & turns_for(h))
        def _():
            act(pair(h, 10, 5, 11, (far_next, shard(-2))))

    me = (g, s)
    two_on, one_on, one_back = (g, shard(2)), (g, shard(1)), (g, shard(-1))
    via, beside = (g, flip), (g, ring_on)

    def first(h):
        detour = last & detours(h)
        straight = jnp.logical_not(detour)
        return [
            (straight, 1, 3, 1, two_on),
            (last & straight, 0, 8, 2, two_on),
            (detour, 1, 11, 1, via),
            (detour, 0, 10, 2, via),
            (even, 1, 2, 3, one_on),
            (s == n_inner - 3, 0, 7, 2, one_back),
        ]

    passed = [
        (None, 3, 4, 4, one_on),
        (s < 2, 8, 9, 5, one_on),
        (odd, 3, 2, 6, one_back),
    ]
    passed_high = [
        (s == 2, 9, 7, 8, (g, shard(-2))),
        (before_last, 7, 9, 8, (g, shard(4))),
    ]
    between = [(None, 11, 3, 9, beside), (None, 10, 8, 10, beside)]

    def each(table, h, act):
        for condition, *entry in table:
            if condition is None:
                act(remote(h, *entry))
            else:
                @pl.when(condition)
                def _(entry=entry):
                    act(remote(h, *entry))

    def send_own(h):
        pltpu.make_async_copy(kv.at[h, :, pl.ds(0, 2)], kv.at[h, :, pl.ds(0, 2)], own_sem.at[h]).wait()
        each(first(h), h, lambda copy: copy.start())

    def send_on(h):
        to_next_group(h, lambda copy: copy.start())

    for h in range(LEAD):
        send_own(h)
        send_on(h)

    early = ((lax.rem(s, half) >= half - 4) | (lax.rem(s, half) < 4)) & jnp.logical_not(turns)

    @pl.when(early)
    def _():
        @pl.loop(LEAD, LEAD_EARLY)
        def _(h):
            send_own(h)

    lead = jnp.where(turns, LEAD_TURN, LEAD)

    @pl.when(turns)
    def _():
        @pl.loop(LEAD, LEAD_TURN)
        def _(h):
            send_own(h)
            send_on(h)

    def send_ahead(h):
        @pl.when(jnp.logical_not(early) & (h + lead < KVH))
        def _():
            send_own(h + lead)

        @pl.when(early & (h + LEAD_EARLY < KVH))
        def _():
            send_own(h + LEAD_EARLY)

        @pl.when(h + lead < KVH)
        def _():
            send_on(h + lead)

    def arrived(h, dst):
        remote(h, dst, dst, 0, me).wait_recv()

    def pass_on(h):
        arrived(h, 3)

        @pl.when(s < 2)
        def _():
            arrived(h, 8)

        each(passed, h, lambda copy: copy.start())

    def pass_high(h):
        @pl.when(s == 2)
        def _():
            arrived(h, 9)

        @pl.when(before_last)
        def _():
            arrived(h, 7)

        each(passed_high, h, lambda copy: copy.start())

    def relay(h):
        @pl.when(lends & detours(h))
        def _():
            arrived(h, 11)
            arrived(h, 10)
            each(between, h, lambda copy: copy.start())

    def pass_turn(h):
        @pl.when(turned & turns_for(h))
        def _():
            pair(h, 10, 10, 0, me).wait_recv()

        from_turn(h, lambda copy: copy.start())

    seam = at_end | (s < 2)
    passes_high = (s == 2) | before_last
    for h in range(4):
        relay(h)
    pass_on(0)

    @pl.when(seam)
    def _():
        pass_on(1)
        pass_on(2)

    @pl.when(passes_high)
    def _():
        pass_high(0)
        pass_high(1)

    @pl.when(before_last)
    def _():
        pass_high(2)


    pass_turn(1)

    for copy in st_copies:
        copy.wait()
    other = jnp.where(st[1, 0:1, 0:1] < st[0, 0:1, 0:1], INF, -INF).astype(jnp.float32)
    row = lax.broadcasted_iota(jnp.int32, (T, REP * T), 0)
    query = lax.rem(lax.broadcasted_iota(jnp.int32, (T, REP * T), 1), T)
    diagonal[...] = jnp.where(row <= query, INF, -INF).astype(jnp.float32)

    q_copy.wait()

    def columns(h, r):
        return pl.ds(pl.multiple_of(h * (REP * D) + r * D, D), D)

    def attend(h, wrapped):
        q = jnp.concatenate(
            [q_vm[row0:row0 + T, columns(h, r)] for row0 in (0, T) for r in range(REP)], axis=0
        )
        results = []
        for c in range(2 * REP * T // 256):
            slots = 10 if wrapped and c > 0 else 7
            keys = kv[h, 0, 0:slots].reshape(slots * T, D)
            values = kv[h, 1, 0:slots].reshape(slots * T, D)
            scores = lax.dot_general(
                keys, q[c * 256:(c + 1) * 256], (((1,), (1,)), ((), ())), preferred_element_type=jnp.float32
            )
            blocks, sums = [], []
            for b in range(2):
                block = 2 * c + b
                high = block >= 3
                lanes = slice((block % 3) * 128, (block % 3 + 1) * 128)
                parts = [scores[slot * T:(slot + 1) * T, b * 128:(b + 1) * 128] for slot in range(slots)]
                own = 0 if high else 1
                parts[own] = jnp.minimum(parts[own], diagonal[:, lanes])
                for slot in (5, 6):
                    parts[slot] = jnp.minimum(parts[slot], other)
                for j in range(1, 4):
                    if wrapped and high:
                        parts[6 + j] = jnp.minimum(parts[6 + j], jnp.where(s < j, INF, -INF))
                    if wrapped and not high:
                        parts[1 + j] = jnp.minimum(parts[1 + j], jnp.where(s >= j, INF, -INF))
                        if slots > 7:
                            parts[6 + j] = None
                if not high:
                    parts[0] = None
                top = None
                for part in parts:
                    if part is not None:
                        peak = jnp.max(part, axis=0, keepdims=True)
                        top = peak if top is None else jnp.maximum(top, peak)
                total, rounded = None, []
                for part in parts:
                    if part is None:
                        rounded.append(jnp.zeros((T, 128), jnp.bfloat16))
                    else:
                        weights = jnp.exp2((part - top) * (SCALE * LOG2_E))
                        here = jnp.sum(weights, axis=0, keepdims=True)
                        total = here if total is None else total + here
                        rounded.append(weights.astype(jnp.bfloat16))
                blocks.append(jnp.concatenate(rounded, axis=0))
                sums.append(total)
            weighted = lax.dot_general(
                values, jnp.concatenate(blocks, axis=1), (((0,), (0,)), ((), ())), preferred_element_type=jnp.float32
            )
            results.append((weighted / jnp.concatenate(sums, axis=1)).T.astype(o_vm.dtype))
        result = jnp.concatenate(results, axis=0)
        for half_index in range(2):
            for r in range(REP):
                start = (half_index * REP + r) * T
                o_vm[half_index * T:(half_index + 1) * T, columns(h, r)] = result[start:start + T]

    def out_copy(h):
        columns = pl.ds(pl.multiple_of(h * (REP * D), REP * D), REP * D)
        return pltpu.make_async_copy(o_vm.at[:, columns], o_hbm.at[:, columns], o_sem.at[h])

    @pl.loop(0, KVH)
    def _(h):
        @pl.when(h + 4 < KVH)
        def _():
            relay(h + 4)

        @pl.when(seam & (h + 3 < KVH))
        def _():
            pass_on(h + 3)

        @pl.when(before_last & (h + 3 < KVH))
        def _():
            pass_high(h + 3)

        @pl.when((s == 2) & (h + 2 < KVH))
        def _():
            pass_high(h + 2)

        send_ahead(h)

        @pl.when(jnp.logical_not(seam) & (h + 1 < KVH))
        def _():
            pass_on(h + 1)

        @pl.when(h + 3 < KVH)
        def _():
            pass_turn(h + 3)

        arrived(h, 2)
        arrived(h, 4)

        @pl.when(s == 0)
        def _():
            arrived(h, 7)

        @pl.when(s < 2)
        def _():
            arrived(h, 9)

        pair(h, 5, 5, 0, me).wait_recv()

        @pl.when(s >= 3)
        def _():
            attend(h, False)

        @pl.when(s < 3)
        def _():
            attend(h, True)

        out_copy(h).start()

    @pl.loop(0, KVH)
    def _(h):
        to_next_group(h, lambda copy: copy.wait_send())
        from_turn(h, lambda copy: copy.wait_send())
        each(first(h), h, lambda copy: copy.wait_send())
        each(passed, h, lambda copy: copy.wait_send())
        each(passed_high, h, lambda copy: copy.wait_send())

        @pl.when(lends & detours(h))
        def _():
            each(between, h, lambda copy: copy.wait_send())

        out_copy(h).wait()


def solution(mesh):
    n_outer, n_inner = mesh.shape["outer"], mesh.shape["inner"]

    def on_device(queries, keys, values, stretch_of):
        rows, width = queries.shape
        any_space = pl.BlockSpec(memory_space=pl.ANY)
        return pl.pallas_call(
            lambda *refs: kernel(n_outer, n_inner, *refs),
            out_shape=jax.ShapeDtypeStruct((rows, width), jnp.bfloat16),
            in_specs=[any_space] * 4,
            out_specs=any_space,
            scratch_shapes=[
                pltpu.VMEM((rows, width), jnp.bfloat16),
                pltpu.VMEM((KVH, 2, SLOTS, T, D), jnp.bfloat16),
                pltpu.VMEM((rows, width), jnp.bfloat16),
                pltpu.VMEM((2, 2, n_inner), jnp.int32),
                pltpu.VMEM((T, REP * T), jnp.float32),
                pltpu.SemaphoreType.DMA,
                pltpu.SemaphoreType.DMA((KVH,)),
                pltpu.SemaphoreType.DMA((2,)),
                pltpu.SemaphoreType.DMA((KVH,)),
                pltpu.SemaphoreType.DMA((SLOTS, KVH)),
                pltpu.SemaphoreType.DMA((12, KVH)),
            ],
            compiler_params=pltpu.CompilerParams(
                collective_id=0, has_side_effects=True, vmem_limit_bytes=48 * 1024 * 1024
            ),
            cost_estimate=pl.CostEstimate(flops=2 * 10**9, bytes_accessed=6 * 10**6, transcendentals=4 * 10**6),
        )(*(
            pltpu.with_memory_space_constraint(array, pltpu.HBM)
            for array in (queries, keys, values, stretch_of.transpose(0, 2, 1))
        ))

    rows = P(("outer", "inner"), None)
    return jax.shard_map(
        on_device, mesh=mesh, in_specs=(rows, rows, rows, P()), out_specs=rows, check_vma=False
    )
```

```python
import jax
import jax.numpy as jnp
from jax import lax
from jax.experimental import pallas as pl
from jax.experimental.pallas import tpu as pltpu
from jax.sharding import PartitionSpec as P

MESH = pl.DeviceIdType.MESH
KVH = 8
REP = 4
D = 128
T = 96
SCALE = D ** (-0.5)
LEAD = 3
LEAD_EARLY = 6
LEAD_TURN = 6
LOG2_E = 1.4426950408889634
INF = float("inf")

SLOTS = 12


def kernel(n_outer, n_inner, q_hbm, k_hbm, v_hbm, st_hbm, o_hbm, q_vm, kv, o_vm, st, diagonal,
           q_sem, own_sem, st_sem, o_sem, recv, send):
    g = lax.axis_index("outer")
    s = lax.axis_index("inner")
    g_next, g_prev = lax.rem(g + 1, n_outer), lax.rem(g + n_outer - 1, n_outer)

    def shard(distance):
        return lax.rem(s + distance + n_inner, n_inner)

    even = lax.rem(s, 2) == 0
    odd = lax.rem(s, 2) == 1

    def own_copies(h):
        columns = pl.ds(pl.multiple_of(h * D, D), D)
        return [
            pltpu.make_async_copy(
                ref.at[pl.ds(T * (1 - slot), T), columns], kv.at[h, i, slot], own_sem.at[h]
            )
            for i, ref in enumerate((k_hbm, v_hbm))
            for slot in range(2)
        ]

    @pl.loop(0, KVH)
    def _(h):
        for copy in own_copies(h):
            copy.start()

    st_copies = [
        pltpu.make_async_copy(st_hbm.at[group], st.at[i], st_sem.at[i])
        for i, group in enumerate((g, g_prev))
    ]
    for copy in st_copies:
        copy.start()
    q_copy = pltpu.make_async_copy(q_hbm, q_vm, q_sem)
    q_copy.start()

    @pl.when(s == 2)
    def _():
        kv[:, :, 7:9] = jnp.zeros((KVH, 2, 2, T, D), kv.dtype)

    @pl.when(s == 1)
    def _():
        kv[:, :, 7:8] = jnp.zeros((KVH, 2, 1, T, D), kv.dtype)

    half = n_inner // 2
    at_end = lax.rem(s, half) >= half - 2
    at_start = lax.rem(s, half) < 2
    flip = lax.rem(s + half, n_inner)
    ring_on = lax.rem(s + 2, half) + half * (s // half)
    ring_back = lax.rem(s + half - 2, half) + half * (s // half)
    last, lends = s >= n_inner - 2, at_end & (s < half)
    before_last = s == n_inner - 4

    rows_y = n_outer // 2
    y_first = lax.rem(g, rows_y) == 0
    turns = (lax.rem(g, rows_y) == rows_y - 1) & at_start
    far, far_next = lax.rem(g + rows_y, n_outer), lax.rem(g_next + rows_y, n_outer)

    turned = (lax.rem(g, rows_y) == rows_y - 1) & (lax.rem(s, half) // 2 == 1)

    def turns_for(h):
        return (lax.rem(h, 2) == 1) | (s >= half)

    def detours(h):
        return lax.rem(h, 3) == 1

    barrier = pltpu.get_barrier_semaphore()

    def greet(group, inner):
        pl.semaphore_signal(barrier, inc=1, device_id=(group, inner), device_id_type=MESH)

    greet(g_prev, s)
    greet(g, shard(-2))
    greet(g, shard(-1))

    @pl.when(even)
    def _():
        greet(g, shard(1))

    @pl.when(s < 2)
    def _():
        greet(g, ring_back)

    @pl.when(s == 0)
    def _():
        greet(g, shard(-4))
        greet(g, shard(2))

    @pl.when(lends)
    def _():
        greet(g, flip)

    @pl.when(turned)
    def _():
        greet(far, shard(-2))

    @pl.when(y_first & at_start)
    def _():
        greet(lax.rem(g_prev + rows_y, n_outer), shard(2))

    count = 3 + lax.rem(s, 2)
    for extra in (last, lends, before_last, s == 2, turns, turned):
        count += extra.astype(jnp.int32)
    pl.semaphore_wait(barrier, count)

    def remote(h, src, dst, sem, target):
        return pltpu.make_async_remote_copy(
            src_ref=kv.at[h, :, src],
            dst_ref=kv.at[h, :, dst],
            send_sem=send.at[sem, h],
            recv_sem=recv.at[dst, h],
            device_id=target,
            device_id_type=MESH,
        )

    def pair(h, src, dst, sem, target):
        return pltpu.make_async_remote_copy(
            src_ref=kv.at[h, :, pl.ds(src, 2)],
            dst_ref=kv.at[h, :, pl.ds(dst, 2)],
            send_sem=send.at[sem, h],
            recv_sem=recv.at[dst, h],
            device_id=target,
            device_id_type=MESH,
        )

    def to_next_group(h, act):
        @pl.when(turns & turns_for(h))
        def _():
            act(pair(h, 0, 10, 0, (far, shard(2))))

        @pl.when(jnp.logical_not(turns & turns_for(h)))
        def _():
            act(pair(h, 0, 5, 0, (g_next, s)))

    def from_turn(h, act):
        @pl.when(turned & turns_for(h))
        def _():
            act(pair(h, 10, 5, 11, (far_next, shard(-2))))

    me = (g, s)
    two_on, one_on, one_back = (g, shard(2)), (g, shard(1)), (g, shard(-1))
    via, beside = (g, flip), (g, ring_on)

    def first(h):
        detour = last & detours(h)
        straight = jnp.logical_not(detour)
        return [
            (straight, 1, 3, 1, two_on),
            (last & straight, 0, 8, 2, two_on),
            (detour, 1, 11, 1, via),
            (detour, 0, 10, 2, via),
            (even, 1, 2, 3, one_on),
            (s == n_inner - 3, 0, 7, 2, one_back),
        ]

    passed = [
        (None, 3, 4, 4, one_on),
        (s < 2, 8, 9, 5, one_on),
        (odd, 3, 2, 6, one_back),
    ]
    passed_high = [
        (s == 2, 9, 7, 8, (g, shard(-2))),
        (before_last, 7, 9, 8, (g, shard(4))),
    ]
    between = [(None, 11, 3, 9, beside), (None, 10, 8, 10, beside)]

    def each(table, h, act):
        for condition, *entry in table:
            if condition is None:
                act(remote(h, *entry))
            else:
                @pl.when(condition)
                def _(entry=entry):
                    act(remote(h, *entry))

    def send_own(h):
        pltpu.make_async_copy(kv.at[h, :, pl.ds(0, 2)], kv.at[h, :, pl.ds(0, 2)], own_sem.at[h]).wait()
        each(first(h), h, lambda copy: copy.start())

    def send_on(h):
        to_next_group(h, lambda copy: copy.start())

    for h in range(LEAD):
        send_own(h)
        send_on(h)

    early = ((lax.rem(s, half) >= half - 4) | (lax.rem(s, half) < 4)) & jnp.logical_not(turns)

    @pl.when(early)
    def _():
        @pl.loop(LEAD, LEAD_EARLY)
        def _(h):
            send_own(h)

    lead = jnp.where(turns, LEAD_TURN, LEAD)

    @pl.when(turns)
    def _():
        @pl.loop(LEAD, LEAD_TURN)
        def _(h):
            send_own(h)
            send_on(h)

    def send_ahead(h):
        @pl.when(jnp.logical_not(early) & (h + lead < KVH))
        def _():
            send_own(h + lead)

        @pl.when(early & (h + LEAD_EARLY < KVH))
        def _():
            send_own(h + LEAD_EARLY)

        @pl.when(h + lead < KVH)
        def _():
            send_on(h + lead)

    def arrived(h, dst):
        remote(h, dst, dst, 0, me).wait_recv()

    def pass_on(h):
        arrived(h, 3)

        @pl.when(s < 2)
        def _():
            arrived(h, 8)

        each(passed, h, lambda copy: copy.start())

    def pass_high(h):
        @pl.when(s == 2)
        def _():
            arrived(h, 9)

        @pl.when(before_last)
        def _():
            arrived(h, 7)

        each(passed_high, h, lambda copy: copy.start())

    def relay(h):
        @pl.when(lends & detours(h))
        def _():
            arrived(h, 11)
            arrived(h, 10)
            each(between, h, lambda copy: copy.start())

    def pass_turn(h):
        @pl.when(turned & turns_for(h))
        def _():
            pair(h, 10, 10, 0, me).wait_recv()

        from_turn(h, lambda copy: copy.start())

    seam = at_end | (s < 2)
    passes_high = (s == 2) | before_last
    for h in range(4):
        relay(h)
    pass_on(0)

    @pl.when(seam)
    def _():
        pass_on(1)
        pass_on(2)

    @pl.when(passes_high)
    def _():
        pass_high(0)
        pass_high(1)

    @pl.when(before_last)
    def _():
        pass_high(2)


    for h in range(3):
        pass_turn(h)

    for copy in st_copies:
        copy.wait()
    other = jnp.where(st[1, 0:1, 0:1] < st[0, 0:1, 0:1], INF, -INF).astype(jnp.float32)
    row = lax.broadcasted_iota(jnp.int32, (T, REP * T), 0)
    query = lax.rem(lax.broadcasted_iota(jnp.int32, (T, REP * T), 1), T)
    diagonal[...] = jnp.where(row <= query, INF, -INF).astype(jnp.float32)

    q_copy.wait()

    def columns(h, r):
        return pl.ds(pl.multiple_of(h * (REP * D) + r * D, D), D)

    def attend(h, wrapped):
        q = jnp.concatenate(
            [q_vm[row0:row0 + T, columns(h, r)] for row0 in (0, T) for r in range(REP)], axis=0
        )
        results = []
        for c in range(2 * REP * T // 256):
            slots = 10 if wrapped and c > 0 else 7
            keys = kv[h, 0, 0:slots].reshape(slots * T, D)
            values = kv[h, 1, 0:slots].reshape(slots * T, D)
            scores = lax.dot_general(
                keys, q[c * 256:(c + 1) * 256], (((1,), (1,)), ((), ())), preferred_element_type=jnp.float32
            )
            blocks, sums = [], []
            for b in range(2):
                block = 2 * c + b
                high = block >= 3
                lanes = slice((block % 3) * 128, (block % 3 + 1) * 128)
                parts = [scores[slot * T:(slot + 1) * T, b * 128:(b + 1) * 128] for slot in range(slots)]
                own = 0 if high else 1
                parts[own] = jnp.minimum(parts[own], diagonal[:, lanes])
                for slot in (5, 6):
                    parts[slot] = jnp.minimum(parts[slot], other)
                for j in range(1, 4):
                    if wrapped and high:
                        parts[6 + j] = jnp.minimum(parts[6 + j], jnp.where(s < j, INF, -INF))
                    if wrapped and not high:
                        parts[1 + j] = jnp.minimum(parts[1 + j], jnp.where(s >= j, INF, -INF))
                        if slots > 7:
                            parts[6 + j] = None
                if not high:
                    parts[0] = None
                top = None
                for part in parts:
                    if part is not None:
                        peak = jnp.max(part, axis=0, keepdims=True)
                        top = peak if top is None else jnp.maximum(top, peak)
                total, rounded = None, []
                for part in parts:
                    if part is None:
                        rounded.append(jnp.zeros((T, 128), jnp.bfloat16))
                    else:
                        weights = jnp.exp2((part - top) * (SCALE * LOG2_E))
                        here = jnp.sum(weights, axis=0, keepdims=True)
                        total = here if total is None else total + here
                        rounded.append(weights.astype(jnp.bfloat16))
                blocks.append(jnp.concatenate(rounded, axis=0))
                sums.append(total)
            weighted = lax.dot_general(
                values, jnp.concatenate(blocks, axis=1), (((0,), (0,)), ((), ())), preferred_element_type=jnp.float32
            )
            results.append((weighted / jnp.concatenate(sums, axis=1)).T.astype(o_vm.dtype))
        result = jnp.concatenate(results, axis=0)
        for half_index in range(2):
            for r in range(REP):
                start = (half_index * REP + r) * T
                o_vm[half_index * T:(half_index + 1) * T, columns(h, r)] = result[start:start + T]

    def out_copy(h):
        columns = pl.ds(pl.multiple_of(h * (REP * D), REP * D), REP * D)
        return pltpu.make_async_copy(o_vm.at[:, columns], o_hbm.at[:, columns], o_sem.at[h])

    @pl.loop(0, KVH)
    def _(h):
        @pl.when(h + 4 < KVH)
        def _():
            relay(h + 4)

        @pl.when(seam & (h + 3 < KVH))
        def _():
            pass_on(h + 3)

        @pl.when(before_last & (h + 3 < KVH))
        def _():
            pass_high(h + 3)

        @pl.when((s == 2) & (h + 2 < KVH))
        def _():
            pass_high(h + 2)

        send_ahead(h)

        @pl.when(jnp.logical_not(seam) & (h + 1 < KVH))
        def _():
            pass_on(h + 1)

        @pl.when(h + 3 < KVH)
        def _():
            pass_turn(h + 3)

        arrived(h, 2)
        arrived(h, 4)

        @pl.when(s == 0)
        def _():
            arrived(h, 7)

        @pl.when(s < 2)
        def _():
            arrived(h, 9)

        pair(h, 5, 5, 0, me).wait_recv()

        @pl.when(s >= 3)
        def _():
            attend(h, False)

        @pl.when(s < 3)
        def _():
            attend(h, True)

        out_copy(h).start()

    @pl.loop(0, KVH)
    def _(h):
        to_next_group(h, lambda copy: copy.wait_send())
        from_turn(h, lambda copy: copy.wait_send())
        each(first(h), h, lambda copy: copy.wait_send())
        each(passed, h, lambda copy: copy.wait_send())
        each(passed_high, h, lambda copy: copy.wait_send())

        @pl.when(lends & detours(h))
        def _():
            each(between, h, lambda copy: copy.wait_send())

        out_copy(h).wait()


def solution(mesh):
    n_outer, n_inner = mesh.shape["outer"], mesh.shape["inner"]

    def on_device(queries, keys, values, stretch_of):
        rows, width = queries.shape
        any_space = pl.BlockSpec(memory_space=pl.ANY)
        return pl.pallas_call(
            lambda *refs: kernel(n_outer, n_inner, *refs),
            out_shape=jax.ShapeDtypeStruct((rows, width), jnp.bfloat16),
            in_specs=[any_space] * 4,
            out_specs=any_space,
            scratch_shapes=[
                pltpu.VMEM((rows, width), jnp.bfloat16),
                pltpu.VMEM((KVH, 2, SLOTS, T, D), jnp.bfloat16),
                pltpu.VMEM((rows, width), jnp.bfloat16),
                pltpu.VMEM((2, 2, n_inner), jnp.int32),
                pltpu.VMEM((T, REP * T), jnp.float32),
                pltpu.SemaphoreType.DMA,
                pltpu.SemaphoreType.DMA((KVH,)),
                pltpu.SemaphoreType.DMA((2,)),
                pltpu.SemaphoreType.DMA((KVH,)),
                pltpu.SemaphoreType.DMA((SLOTS, KVH)),
                pltpu.SemaphoreType.DMA((12, KVH)),
            ],
            compiler_params=pltpu.CompilerParams(
                collective_id=0, has_side_effects=True, vmem_limit_bytes=48 * 1024 * 1024
            ),
            cost_estimate=pl.CostEstimate(flops=2 * 10**9, bytes_accessed=6 * 10**6, transcendentals=4 * 10**6),
        )(*(
            pltpu.with_memory_space_constraint(array, pltpu.HBM)
            for array in (queries, keys, values, stretch_of.transpose(0, 2, 1))
        ))

    rows = P(("outer", "inner"), None)
    return jax.shard_map(
        on_device, mesh=mesh, in_specs=(rows, rows, rows, P()), out_specs=rows, check_vma=False
    )
```

```python
import jax
import jax.numpy as jnp
from jax import lax
from jax.experimental import pallas as pl
from jax.experimental.pallas import tpu as pltpu
from jax.sharding import PartitionSpec as P

MESH = pl.DeviceIdType.MESH
KVH = 8
REP = 4
D = 128
T = 96
SCALE = D ** (-0.5)
LEAD = 3
LEAD_EARLY = 6
LEAD_TURN = 6
LOG2_E = 1.4426950408889634
INF = float("inf")

SLOTS = 12


def kernel(n_outer, n_inner, q_hbm, k_hbm, v_hbm, st_hbm, o_hbm, q_vm, kv, o_vm, st, diagonal,
           q_sem, own_sem, st_sem, o_sem, recv, send):
    g = lax.axis_index("outer")
    s = lax.axis_index("inner")
    g_next, g_prev = lax.rem(g + 1, n_outer), lax.rem(g + n_outer - 1, n_outer)

    def shard(distance):
        return lax.rem(s + distance + n_inner, n_inner)

    even = lax.rem(s, 2) == 0
    odd = lax.rem(s, 2) == 1

    def own_copies(h):
        columns = pl.ds(pl.multiple_of(h * D, D), D)
        return [
            pltpu.make_async_copy(
                ref.at[pl.ds(T * (1 - slot), T), columns], kv.at[h, i, slot], own_sem.at[h]
            )
            for i, ref in enumerate((k_hbm, v_hbm))
            for slot in range(2)
        ]

    @pl.loop(0, KVH)
    def _(h):
        for copy in own_copies(h):
            copy.start()

    st_copies = [
        pltpu.make_async_copy(st_hbm.at[group], st.at[i], st_sem.at[i])
        for i, group in enumerate((g, g_prev))
    ]
    for copy in st_copies:
        copy.start()
    q_copy = pltpu.make_async_copy(q_hbm, q_vm, q_sem)
    q_copy.start()

    @pl.when(s == 2)
    def _():
        kv[:, :, 7:9] = jnp.zeros((KVH, 2, 2, T, D), kv.dtype)

    @pl.when(s == 1)
    def _():
        kv[:, :, 7:8] = jnp.zeros((KVH, 2, 1, T, D), kv.dtype)

    half = n_inner // 2
    at_end = lax.rem(s, half) >= half - 2
    at_start = lax.rem(s, half) < 2
    flip = lax.rem(s + half, n_inner)
    ring_on = lax.rem(s + 2, half) + half * (s // half)
    ring_back = lax.rem(s + half - 2, half) + half * (s // half)
    last, lends = s >= n_inner - 2, at_end & (s < half)
    before_last = s == n_inner - 4

    rows_y = n_outer // 2
    y_first = lax.rem(g, rows_y) == 0
    turns = (lax.rem(g, rows_y) == rows_y - 1) & at_start
    far, far_next = lax.rem(g + rows_y, n_outer), lax.rem(g_next + rows_y, n_outer)

    turned = (lax.rem(g, rows_y) == rows_y - 1) & (lax.rem(s, half) // 2 == 1)

    def turns_for(h):
        return (lax.rem(h, 2) == 1) | ((s >= half) & (lax.rem(h, 4) != 0))

    def detours(h):
        return lax.rem(h, 3) == 1

    barrier = pltpu.get_barrier_semaphore()

    def greet(group, inner):
        pl.semaphore_signal(barrier, inc=1, device_id=(group, inner), device_id_type=MESH)

    greet(g_prev, s)
    greet(g, shard(-2))
    greet(g, shard(-1))

    @pl.when(even)
    def _():
        greet(g, shard(1))

    @pl.when(s < 2)
    def _():
        greet(g, ring_back)

    @pl.when(s == 0)
    def _():
        greet(g, shard(-4))
        greet(g, shard(2))

    @pl.when(lends)
    def _():
        greet(g, flip)

    @pl.when(turned)
    def _():
        greet(far, shard(-2))

    @pl.when(y_first & at_start)
    def _():
        greet(lax.rem(g_prev + rows_y, n_outer), shard(2))

    count = 3 + lax.rem(s, 2)
    for extra in (last, lends, before_last, s == 2, turns, turned):
        count += extra.astype(jnp.int32)
    pl.semaphore_wait(barrier, count)

    def remote(h, src, dst, sem, target):
        return pltpu.make_async_remote_copy(
            src_ref=kv.at[h, :, src],
            dst_ref=kv.at[h, :, dst],
            send_sem=send.at[sem, h],
            recv_sem=recv.at[dst, h],
            device_id=target,
            device_id_type=MESH,
        )

    def pair(h, src, dst, sem, target):
        return pltpu.make_async_remote_copy(
            src_ref=kv.at[h, :, pl.ds(src, 2)],
            dst_ref=kv.at[h, :, pl.ds(dst, 2)],
            send_sem=send.at[sem, h],
            recv_sem=recv.at[dst, h],
            device_id=target,
            device_id_type=MESH,
        )

    def to_next_group(h, act):
        @pl.when(turns & turns_for(h))
        def _():
            act(pair(h, 0, 10, 0, (far, shard(2))))

        @pl.when(jnp.logical_not(turns & turns_for(h)))
        def _():
            act(pair(h, 0, 5, 0, (g_next, s)))

    def from_turn(h, act):
        @pl.when(turned & turns_for(h))
        def _():
            act(pair(h, 10, 5, 11, (far_next, shard(-2))))

    me = (g, s)
    two_on, one_on, one_back = (g, shard(2)), (g, shard(1)), (g, shard(-1))
    via, beside = (g, flip), (g, ring_on)

    def first(h):
        detour = last & detours(h)
        straight = jnp.logical_not(detour)
        return [
            (straight, 1, 3, 1, two_on),
            (last & straight, 0, 8, 2, two_on),
            (detour, 1, 11, 1, via),
            (detour, 0, 10, 2, via),
            (even, 1, 2, 3, one_on),
            (s == n_inner - 3, 0, 7, 2, one_back),
        ]

    passed = [
        (None, 3, 4, 4, one_on),
        (s < 2, 8, 9, 5, one_on),
        (odd, 3, 2, 6, one_back),
    ]
    passed_high = [
        (s == 2, 9, 7, 8, (g, shard(-2))),
        (before_last, 7, 9, 8, (g, shard(4))),
    ]
    between = [(None, 11, 3, 9, beside), (None, 10, 8, 10, beside)]

    def each(table, h, act):
        for condition, *entry in table:
            if condition is None:
                act(remote(h, *entry))
            else:
                @pl.when(condition)
                def _(entry=entry):
                    act(remote(h, *entry))

    def send_own(h):
        pltpu.make_async_copy(kv.at[h, :, pl.ds(0, 2)], kv.at[h, :, pl.ds(0, 2)], own_sem.at[h]).wait()
        each(first(h), h, lambda copy: copy.start())

    def send_on(h):
        to_next_group(h, lambda copy: copy.start())

    for h in range(LEAD):
        send_own(h)
        send_on(h)

    early = ((lax.rem(s, half) >= half - 4) | (lax.rem(s, half) < 4)) & jnp.logical_not(turns)

    @pl.when(early)
    def _():
        @pl.loop(LEAD, LEAD_EARLY)
        def _(h):
            send_own(h)

    lead = jnp.where(turns, LEAD_TURN, LEAD)

    @pl.when(turns)
    def _():
        @pl.loop(LEAD, LEAD_TURN)
        def _(h):
            send_own(h)
            send_on(h)

    def send_ahead(h):
        @pl.when(jnp.logical_not(early) & (h + lead < KVH))
        def _():
            send_own(h + lead)

        @pl.when(early & (h + LEAD_EARLY < KVH))
        def _():
            send_own(h + LEAD_EARLY)

        @pl.when(h + lead < KVH)
        def _():
            send_on(h + lead)

    def arrived(h, dst):
        remote(h, dst, dst, 0, me).wait_recv()

    def pass_on(h):
        arrived(h, 3)

        @pl.when(s < 2)
        def _():
            arrived(h, 8)

        each(passed, h, lambda copy: copy.start())

    def pass_high(h):
        @pl.when(s == 2)
        def _():
            arrived(h, 9)

        @pl.when(before_last)
        def _():
            arrived(h, 7)

        each(passed_high, h, lambda copy: copy.start())

    def relay(h):
        @pl.when(lends & detours(h))
        def _():
            arrived(h, 11)
            arrived(h, 10)
            each(between, h, lambda copy: copy.start())

    def pass_turn(h):
        @pl.when(turned & turns_for(h))
        def _():
            pair(h, 10, 10, 0, me).wait_recv()

        from_turn(h, lambda copy: copy.start())

    seam = at_end | (s < 2)
    passes_high = (s == 2) | before_last
    for h in range(4):
        relay(h)
    pass_on(0)

    @pl.when(seam)
    def _():
        pass_on(1)
        pass_on(2)

    @pl.when(passes_high)
    def _():
        pass_high(0)
        pass_high(1)

    @pl.when(before_last)
    def _():
        pass_high(2)


    for h in range(3):
        pass_turn(h)

    for copy in st_copies:
        copy.wait()
    other = jnp.where(st[1, 0:1, 0:1] < st[0, 0:1, 0:1], INF, -INF).astype(jnp.float32)
    row = lax.broadcasted_iota(jnp.int32, (T, REP * T), 0)
    query = lax.rem(lax.broadcasted_iota(jnp.int32, (T, REP * T), 1), T)
    diagonal[...] = jnp.where(row <= query, INF, -INF).astype(jnp.float32)

    q_copy.wait()

    def columns(h, r):
        return pl.ds(pl.multiple_of(h * (REP * D) + r * D, D), D)

    def attend(h, wrapped):
        q = jnp.concatenate(
            [q_vm[row0:row0 + T, columns(h, r)] for row0 in (0, T) for r in range(REP)], axis=0
        )
        results = []
        for c in range(2 * REP * T // 256):
            slots = 10 if wrapped and c > 0 else 7
            keys = kv[h, 0, 0:slots].reshape(slots * T, D)
            values = kv[h, 1, 0:slots].reshape(slots * T, D)
            scores = lax.dot_general(
                keys, q[c * 256:(c + 1) * 256], (((1,), (1,)), ((), ())), preferred_element_type=jnp.float32
            )
            blocks, sums = [], []
            for b in range(2):
                block = 2 * c + b
                high = block >= 3
                lanes = slice((block % 3) * 128, (block % 3 + 1) * 128)
                parts = [scores[slot * T:(slot + 1) * T, b * 128:(b + 1) * 128] for slot in range(slots)]
                own = 0 if high else 1
                parts[own] = jnp.minimum(parts[own], diagonal[:, lanes])
                for slot in (5, 6):
                    parts[slot] = jnp.minimum(parts[slot], other)
                for j in range(1, 4):
                    if wrapped and high:
                        parts[6 + j] = jnp.minimum(parts[6 + j], jnp.where(s < j, INF, -INF))
                    if wrapped and not high:
                        parts[1 + j] = jnp.minimum(parts[1 + j], jnp.where(s >= j, INF, -INF))
                        if slots > 7:
                            parts[6 + j] = None
                if not high:
                    parts[0] = None
                top = None
                for part in parts:
                    if part is not None:
                        peak = jnp.max(part, axis=0, keepdims=True)
                        top = peak if top is None else jnp.maximum(top, peak)
                total, rounded = None, []
                for part in parts:
                    if part is None:
                        rounded.append(jnp.zeros((T, 128), jnp.bfloat16))
                    else:
                        weights = jnp.exp2((part - top) * (SCALE * LOG2_E))
                        here = jnp.sum(weights, axis=0, keepdims=True)
                        total = here if total is None else total + here
                        rounded.append(weights.astype(jnp.bfloat16))
                blocks.append(jnp.concatenate(rounded, axis=0))
                sums.append(total)
            weighted = lax.dot_general(
                values, jnp.concatenate(blocks, axis=1), (((0,), (0,)), ((), ())), preferred_element_type=jnp.float32
            )
            results.append((weighted / jnp.concatenate(sums, axis=1)).T.astype(o_vm.dtype))
        result = jnp.concatenate(results, axis=0)
        for half_index in range(2):
            for r in range(REP):
                start = (half_index * REP + r) * T
                o_vm[half_index * T:(half_index + 1) * T, columns(h, r)] = result[start:start + T]

    def out_copy(h):
        columns = pl.ds(pl.multiple_of(h * (REP * D), REP * D), REP * D)
        return pltpu.make_async_copy(o_vm.at[:, columns], o_hbm.at[:, columns], o_sem.at[h])

    @pl.loop(0, KVH)
    def _(h):
        @pl.when(h + 4 < KVH)
        def _():
            relay(h + 4)

        @pl.when(seam & (h + 3 < KVH))
        def _():
            pass_on(h + 3)

        @pl.when(before_last & (h + 3 < KVH))
        def _():
            pass_high(h + 3)

        @pl.when((s == 2) & (h + 2 < KVH))
        def _():
            pass_high(h + 2)

        send_ahead(h)

        @pl.when(jnp.logical_not(seam) & (h + 1 < KVH))
        def _():
            pass_on(h + 1)

        @pl.when(h + 3 < KVH)
        def _():
            pass_turn(h + 3)

        arrived(h, 2)
        arrived(h, 4)

        @pl.when(s == 0)
        def _():
            arrived(h, 7)

        @pl.when(s < 2)
        def _():
            arrived(h, 9)

        pair(h, 5, 5, 0, me).wait_recv()

        @pl.when(s >= 3)
        def _():
            attend(h, False)

        @pl.when(s < 3)
        def _():
            attend(h, True)

        out_copy(h).start()

    @pl.loop(0, KVH)
    def _(h):
        to_next_group(h, lambda copy: copy.wait_send())
        from_turn(h, lambda copy: copy.wait_send())
        each(first(h), h, lambda copy: copy.wait_send())
        each(passed, h, lambda copy: copy.wait_send())
        each(passed_high, h, lambda copy: copy.wait_send())

        @pl.when(lends & detours(h))
        def _():
            each(between, h, lambda copy: copy.wait_send())

        out_copy(h).wait()


def solution(mesh):
    n_outer, n_inner = mesh.shape["outer"], mesh.shape["inner"]

    def on_device(queries, keys, values, stretch_of):
        rows, width = queries.shape
        any_space = pl.BlockSpec(memory_space=pl.ANY)
        return pl.pallas_call(
            lambda *refs: kernel(n_outer, n_inner, *refs),
            out_shape=jax.ShapeDtypeStruct((rows, width), jnp.bfloat16),
            in_specs=[any_space] * 4,
            out_specs=any_space,
            scratch_shapes=[
                pltpu.VMEM((rows, width), jnp.bfloat16),
                pltpu.VMEM((KVH, 2, SLOTS, T, D), jnp.bfloat16),
                pltpu.VMEM((rows, width), jnp.bfloat16),
                pltpu.VMEM((2, 2, n_inner), jnp.int32),
                pltpu.VMEM((T, REP * T), jnp.float32),
                pltpu.SemaphoreType.DMA,
                pltpu.SemaphoreType.DMA((KVH,)),
                pltpu.SemaphoreType.DMA((2,)),
                pltpu.SemaphoreType.DMA((KVH,)),
                pltpu.SemaphoreType.DMA((SLOTS, KVH)),
                pltpu.SemaphoreType.DMA((12, KVH)),
            ],
            compiler_params=pltpu.CompilerParams(
                collective_id=0, has_side_effects=True, vmem_limit_bytes=48 * 1024 * 1024
            ),
            cost_estimate=pl.CostEstimate(flops=2 * 10**9, bytes_accessed=6 * 10**6, transcendentals=4 * 10**6),
        )(*(
            pltpu.with_memory_space_constraint(array, pltpu.HBM)
            for array in (queries, keys, values, stretch_of.transpose(0, 2, 1))
        ))

    rows = P(("outer", "inner"), None)
    return jax.shard_map(
        on_device, mesh=mesh, in_specs=(rows, rows, rows, P()), out_specs=rows, check_vma=False
    )
```

```python
import jax
import jax.numpy as jnp
from jax import lax
from jax.experimental import pallas as pl
from jax.experimental.pallas import tpu as pltpu
from jax.sharding import PartitionSpec as P

MESH = pl.DeviceIdType.MESH
KVH = 8
REP = 4
D = 128
T = 96
SCALE = D ** (-0.5)
LEAD = 3
LEAD_EARLY = 6
LEAD_TURN = 6
LOG2_E = 1.4426950408889634
INF = float("inf")

SLOTS = 12


def kernel(n_outer, n_inner, q_hbm, k_hbm, v_hbm, st_hbm, o_hbm, q_vm, kv, o_vm, st, diagonal,
           q_sem, own_sem, st_sem, o_sem, recv, send):
    g = lax.axis_index("outer")
    s = lax.axis_index("inner")
    g_next, g_prev = lax.rem(g + 1, n_outer), lax.rem(g + n_outer - 1, n_outer)

    def shard(distance):
        return lax.rem(s + distance + n_inner, n_inner)

    even = lax.rem(s, 2) == 0
    odd = lax.rem(s, 2) == 1

    def own_copies(h):
        columns = pl.ds(pl.multiple_of(h * D, D), D)
        return [
            pltpu.make_async_copy(
                ref.at[pl.ds(T * (1 - slot), T), columns], kv.at[h, i, slot], own_sem.at[h]
            )
            for i, ref in enumerate((k_hbm, v_hbm))
            for slot in range(2)
        ]

    @pl.loop(0, KVH)
    def _(h):
        for copy in own_copies(h):
            copy.start()

    st_copies = [
        pltpu.make_async_copy(st_hbm.at[group], st.at[i], st_sem.at[i])
        for i, group in enumerate((g, g_prev))
    ]
    for copy in st_copies:
        copy.start()
    q_copy = pltpu.make_async_copy(q_hbm, q_vm, q_sem)
    q_copy.start()

    @pl.when(s == 2)
    def _():
        kv[:, :, 7:9] = jnp.zeros((KVH, 2, 2, T, D), kv.dtype)

    @pl.when(s == 1)
    def _():
        kv[:, :, 7:8] = jnp.zeros((KVH, 2, 1, T, D), kv.dtype)

    half = n_inner // 2
    at_end = lax.rem(s, half) >= half - 2
    at_start = lax.rem(s, half) < 2
    flip = lax.rem(s + half, n_inner)
    ring_on = lax.rem(s + 2, half) + half * (s // half)
    ring_back = lax.rem(s + half - 2, half) + half * (s // half)
    last, lends = s >= n_inner - 2, at_end & (s < half)
    before_last = s == n_inner - 4

    rows_y = n_outer // 2
    y_first = lax.rem(g, rows_y) == 0
    turns = (lax.rem(g, rows_y) == rows_y - 1) & at_start
    far, far_next = lax.rem(g + rows_y, n_outer), lax.rem(g_next + rows_y, n_outer)

    turned = (lax.rem(g, rows_y) == rows_y - 1) & (lax.rem(s, half) // 2 == 1)

    def turns_for(h):
        return (lax.rem(h, 4) == 1) | ((s >= half) & (lax.rem(h, 4) != 0))

    def detours(h):
        return lax.rem(h, 3) == 1

    barrier = pltpu.get_barrier_semaphore()

    def greet(group, inner):
        pl.semaphore_signal(barrier, inc=1, device_id=(group, inner), device_id_type=MESH)

    greet(g_prev, s)
    greet(g, shard(-2))
    greet(g, shard(-1))

    @pl.when(even)
    def _():
        greet(g, shard(1))

    @pl.when(s < 2)
    def _():
        greet(g, ring_back)

    @pl.when(s == 0)
    def _():
        greet(g, shard(-4))
        greet(g, shard(2))

    @pl.when(lends)
    def _():
        greet(g, flip)

    @pl.when(turned)
    def _():
        greet(far, shard(-2))

    @pl.when(y_first & at_start)
    def _():
        greet(lax.rem(g_prev + rows_y, n_outer), shard(2))

    count = 3 + lax.rem(s, 2)
    for extra in (last, lends, before_last, s == 2, turns, turned):
        count += extra.astype(jnp.int32)
    pl.semaphore_wait(barrier, count)

    def remote(h, src, dst, sem, target):
        return pltpu.make_async_remote_copy(
            src_ref=kv.at[h, :, src],
            dst_ref=kv.at[h, :, dst],
            send_sem=send.at[sem, h],
            recv_sem=recv.at[dst, h],
            device_id=target,
            device_id_type=MESH,
        )

    def pair(h, src, dst, sem, target):
        return pltpu.make_async_remote_copy(
            src_ref=kv.at[h, :, pl.ds(src, 2)],
            dst_ref=kv.at[h, :, pl.ds(dst, 2)],
            send_sem=send.at[sem, h],
            recv_sem=recv.at[dst, h],
            device_id=target,
            device_id_type=MESH,
        )

    def to_next_group(h, act):
        @pl.when(turns & turns_for(h))
        def _():
            act(pair(h, 0, 10, 0, (far, shard(2))))

        @pl.when(jnp.logical_not(turns & turns_for(h)))
        def _():
            act(pair(h, 0, 5, 0, (g_next, s)))

    def from_turn(h, act):
        @pl.when(turned & turns_for(h))
        def _():
            act(pair(h, 10, 5, 11, (far_next, shard(-2))))

    me = (g, s)
    two_on, one_on, one_back = (g, shard(2)), (g, shard(1)), (g, shard(-1))
    via, beside = (g, flip), (g, ring_on)

    def first(h):
        detour = last & detours(h)
        straight = jnp.logical_not(detour)
        return [
            (straight, 1, 3, 1, two_on),
            (last & straight, 0, 8, 2, two_on),
            (detour, 1, 11, 1, via),
            (detour, 0, 10, 2, via),
            (even, 1, 2, 3, one_on),
            (s == n_inner - 3, 0, 7, 2, one_back),
        ]

    passed = [
        (None, 3, 4, 4, one_on),
        (s < 2, 8, 9, 5, one_on),
        (odd, 3, 2, 6, one_back),
    ]
    passed_high = [
        (s == 2, 9, 7, 8, (g, shard(-2))),
        (before_last, 7, 9, 8, (g, shard(4))),
    ]
    between = [(None, 11, 3, 9, beside), (None, 10, 8, 10, beside)]

    def each(table, h, act):
        for condition, *entry in table:
            if condition is None:
                act(remote(h, *entry))
            else:
                @pl.when(condition)
                def _(entry=entry):
                    act(remote(h, *entry))

    def send_own(h):
        pltpu.make_async_copy(kv.at[h, :, pl.ds(0, 2)], kv.at[h, :, pl.ds(0, 2)], own_sem.at[h]).wait()
        each(first(h), h, lambda copy: copy.start())

    def send_on(h):
        to_next_group(h, lambda copy: copy.start())

    for h in range(LEAD):
        send_own(h)
        send_on(h)

    early = ((lax.rem(s, half) >= half - 4) | (lax.rem(s, half) < 4)) & jnp.logical_not(turns)

    @pl.when(early)
    def _():
        @pl.loop(LEAD, LEAD_EARLY)
        def _(h):
            send_own(h)

    lead = jnp.where(turns, jnp.where(s < 2, LEAD + 1, LEAD_TURN), LEAD)

    @pl.when(turns)
    def _():
        @pl.loop(LEAD, lead)
        def _(h):
            send_own(h)
            send_on(h)

    def send_ahead(h):
        @pl.when(jnp.logical_not(early) & (h + lead < KVH))
        def _():
            send_own(h + lead)

        @pl.when(early & (h + LEAD_EARLY < KVH))
        def _():
            send_own(h + LEAD_EARLY)

        @pl.when(h + lead < KVH)
        def _():
            send_on(h + lead)

    def arrived(h, dst):
        remote(h, dst, dst, 0, me).wait_recv()

    def pass_on(h):
        arrived(h, 3)

        @pl.when(s < 2)
        def _():
            arrived(h, 8)

        each(passed, h, lambda copy: copy.start())

    def pass_high(h):
        @pl.when(s == 2)
        def _():
            arrived(h, 9)

        @pl.when(before_last)
        def _():
            arrived(h, 7)

        each(passed_high, h, lambda copy: copy.start())

    def relay(h):
        @pl.when(lends & detours(h))
        def _():
            arrived(h, 11)
            arrived(h, 10)
            each(between, h, lambda copy: copy.start())

    def pass_turn(h):
        @pl.when(turned & turns_for(h))
        def _():
            pair(h, 10, 10, 0, me).wait_recv()

        from_turn(h, lambda copy: copy.start())

    seam = at_end | (s < 2)
    passes_high = (s == 2) | before_last
    for h in range(4):
        relay(h)
    pass_on(0)

    @pl.when(seam)
    def _():
        pass_on(1)
        pass_on(2)

    @pl.when(passes_high)
    def _():
        pass_high(0)
        pass_high(1)

    @pl.when(before_last)
    def _():
        pass_high(2)


    for h in range(3):
        pass_turn(h)

    for copy in st_copies:
        copy.wait()
    other = jnp.where(st[1, 0:1, 0:1] < st[0, 0:1, 0:1], INF, -INF).astype(jnp.float32)
    row = lax.broadcasted_iota(jnp.int32, (T, REP * T), 0)
    query = lax.rem(lax.broadcasted_iota(jnp.int32, (T, REP * T), 1), T)
    diagonal[...] = jnp.where(row <= query, INF, -INF).astype(jnp.float32)

    q_copy.wait()

    def columns(h, r):
        return pl.ds(pl.multiple_of(h * (REP * D) + r * D, D), D)

    def attend(h, wrapped):
        q = jnp.concatenate(
            [q_vm[row0:row0 + T, columns(h, r)] for row0 in (0, T) for r in range(REP)], axis=0
        )
        results = []
        for c in range(2 * REP * T // 256):
            slots = 10 if wrapped and c > 0 else 7
            keys = kv[h, 0, 0:slots].reshape(slots * T, D)
            values = kv[h, 1, 0:slots].reshape(slots * T, D)
            scores = lax.dot_general(
                keys, q[c * 256:(c + 1) * 256], (((1,), (1,)), ((), ())), preferred_element_type=jnp.float32
            )
            blocks, sums = [], []
            for b in range(2):
                block = 2 * c + b
                high = block >= 3
                lanes = slice((block % 3) * 128, (block % 3 + 1) * 128)
                parts = [scores[slot * T:(slot + 1) * T, b * 128:(b + 1) * 128] for slot in range(slots)]
                own = 0 if high else 1
                parts[own] = jnp.minimum(parts[own], diagonal[:, lanes])
                for slot in (5, 6):
                    parts[slot] = jnp.minimum(parts[slot], other)
                for j in range(1, 4):
                    if wrapped and high:
                        parts[6 + j] = jnp.minimum(parts[6 + j], jnp.where(s < j, INF, -INF))
                    if wrapped and not high:
                        parts[1 + j] = jnp.minimum(parts[1 + j], jnp.where(s >= j, INF, -INF))
                        if slots > 7:
                            parts[6 + j] = None
                if not high:
                    parts[0] = None
                top = None
                for part in parts:
                    if part is not None:
                        peak = jnp.max(part, axis=0, keepdims=True)
                        top = peak if top is None else jnp.maximum(top, peak)
                total, rounded = None, []
                for part in parts:
                    if part is None:
                        rounded.append(jnp.zeros((T, 128), jnp.bfloat16))
                    else:
                        weights = jnp.exp2((part - top) * (SCALE * LOG2_E))
                        here = jnp.sum(weights, axis=0, keepdims=True)
                        total = here if total is None else total + here
                        rounded.append(weights.astype(jnp.bfloat16))
                blocks.append(jnp.concatenate(rounded, axis=0))
                sums.append(total)
            weighted = lax.dot_general(
                values, jnp.concatenate(blocks, axis=1), (((0,), (0,)), ((), ())), preferred_element_type=jnp.float32
            )
            results.append((weighted / jnp.concatenate(sums, axis=1)).T.astype(o_vm.dtype))
        result = jnp.concatenate(results, axis=0)
        for half_index in range(2):
            for r in range(REP):
                start = (half_index * REP + r) * T
                o_vm[half_index * T:(half_index + 1) * T, columns(h, r)] = result[start:start + T]

    def out_copy(h):
        columns = pl.ds(pl.multiple_of(h * (REP * D), REP * D), REP * D)
        return pltpu.make_async_copy(o_vm.at[:, columns], o_hbm.at[:, columns], o_sem.at[h])

    @pl.loop(0, KVH)
    def _(h):
        @pl.when(h + 4 < KVH)
        def _():
            relay(h + 4)

        @pl.when(seam & (h + 3 < KVH))
        def _():
            pass_on(h + 3)

        @pl.when(before_last & (h + 3 < KVH))
        def _():
            pass_high(h + 3)

        @pl.when((s == 2) & (h + 2 < KVH))
        def _():
            pass_high(h + 2)

        send_ahead(h)

        @pl.when(jnp.logical_not(seam) & (h + 1 < KVH))
        def _():
            pass_on(h + 1)

        @pl.when(h + 3 < KVH)
        def _():
            pass_turn(h + 3)

        arrived(h, 2)
        arrived(h, 4)

        @pl.when(s == 0)
        def _():
            arrived(h, 7)

        @pl.when(s < 2)
        def _():
            arrived(h, 9)

        pair(h, 5, 5, 0, me).wait_recv()

        @pl.when(s >= 3)
        def _():
            attend(h, False)

        @pl.when(s < 3)
        def _():
            attend(h, True)

        out_copy(h).start()

    @pl.loop(0, KVH)
    def _(h):
        to_next_group(h, lambda copy: copy.wait_send())
        from_turn(h, lambda copy: copy.wait_send())
        each(first(h), h, lambda copy: copy.wait_send())
        each(passed, h, lambda copy: copy.wait_send())
        each(passed_high, h, lambda copy: copy.wait_send())

        @pl.when(lends & detours(h))
        def _():
            each(between, h, lambda copy: copy.wait_send())

        out_copy(h).wait()


def solution(mesh):
    n_outer, n_inner = mesh.shape["outer"], mesh.shape["inner"]

    def on_device(queries, keys, values, stretch_of):
        rows, width = queries.shape
        any_space = pl.BlockSpec(memory_space=pl.ANY)
        return pl.pallas_call(
            lambda *refs: kernel(n_outer, n_inner, *refs),
            out_shape=jax.ShapeDtypeStruct((rows, width), jnp.bfloat16),
            in_specs=[any_space] * 4,
            out_specs=any_space,
            scratch_shapes=[
                pltpu.VMEM((rows, width), jnp.bfloat16),
                pltpu.VMEM((KVH, 2, SLOTS, T, D), jnp.bfloat16),
                pltpu.VMEM((rows, width), jnp.bfloat16),
                pltpu.VMEM((2, 2, n_inner), jnp.int32),
                pltpu.VMEM((T, REP * T), jnp.float32),
                pltpu.SemaphoreType.DMA,
                pltpu.SemaphoreType.DMA((KVH,)),
                pltpu.SemaphoreType.DMA((2,)),
                pltpu.SemaphoreType.DMA((KVH,)),
                pltpu.SemaphoreType.DMA((SLOTS, KVH)),
                pltpu.SemaphoreType.DMA((12, KVH)),
            ],
            compiler_params=pltpu.CompilerParams(
                collective_id=0, has_side_effects=True, vmem_limit_bytes=48 * 1024 * 1024
            ),
            cost_estimate=pl.CostEstimate(flops=2 * 10**9, bytes_accessed=6 * 10**6, transcendentals=4 * 10**6),
        )(*(
            pltpu.with_memory_space_constraint(array, pltpu.HBM)
            for array in (queries, keys, values, stretch_of.transpose(0, 2, 1))
        ))

    rows = P(("outer", "inner"), None)
    return jax.shard_map(
        on_device, mesh=mesh, in_specs=(rows, rows, rows, P()), out_specs=rows, check_vma=False
    )
```

```python
import jax
import jax.numpy as jnp
from jax import lax
from jax.experimental import pallas as pl
from jax.experimental.pallas import tpu as pltpu
from jax.sharding import PartitionSpec as P

MESH = pl.DeviceIdType.MESH
KVH = 8
REP = 4
D = 128
T = 96
SCALE = D ** (-0.5)
LEAD = 3
LEAD_EARLY = 6
LEAD_TURN = 6
LOG2_E = 1.4426950408889634
INF = float("inf")

SLOTS = 12


def kernel(n_outer, n_inner, q_hbm, k_hbm, v_hbm, st_hbm, o_hbm, q_vm, kv, o_vm, st, diagonal,
           q_sem, own_sem, st_sem, o_sem, recv, send):
    g = lax.axis_index("outer")
    s = lax.axis_index("inner")
    g_next, g_prev = lax.rem(g + 1, n_outer), lax.rem(g + n_outer - 1, n_outer)

    def shard(distance):
        return lax.rem(s + distance + n_inner, n_inner)

    even = lax.rem(s, 2) == 0
    odd = lax.rem(s, 2) == 1

    def own_copies(h):
        columns = pl.ds(pl.multiple_of(h * D, D), D)
        return [
            pltpu.make_async_copy(
                ref.at[pl.ds(T * (1 - slot), T), columns], kv.at[h, i, slot], own_sem.at[h]
            )
            for i, ref in enumerate((k_hbm, v_hbm))
            for slot in range(2)
        ]

    @pl.loop(0, KVH)
    def _(h):
        for copy in own_copies(h):
            copy.start()

    st_copies = [
        pltpu.make_async_copy(st_hbm.at[group], st.at[i], st_sem.at[i])
        for i, group in enumerate((g, g_prev))
    ]
    for copy in st_copies:
        copy.start()
    q_copy = pltpu.make_async_copy(q_hbm, q_vm, q_sem)
    q_copy.start()

    @pl.when(s == 2)
    def _():
        kv[:, :, 7:9] = jnp.zeros((KVH, 2, 2, T, D), kv.dtype)

    @pl.when(s == 1)
    def _():
        kv[:, :, 7:8] = jnp.zeros((KVH, 2, 1, T, D), kv.dtype)

    half = n_inner // 2
    at_end = lax.rem(s, half) >= half - 2
    at_start = lax.rem(s, half) < 2
    flip = lax.rem(s + half, n_inner)
    ring_on = lax.rem(s + 2, half) + half * (s // half)
    ring_back = lax.rem(s + half - 2, half) + half * (s // half)
    last, lends = s >= n_inner - 2, at_end & (s < half)
    before_last = s == n_inner - 4

    rows_y = n_outer // 2
    y_first = lax.rem(g, rows_y) == 0
    turns = (lax.rem(g, rows_y) == rows_y - 1) & at_start
    far, far_next = lax.rem(g + rows_y, n_outer), lax.rem(g_next + rows_y, n_outer)

    turned = (lax.rem(g, rows_y) == rows_y - 1) & (lax.rem(s, half) // 2 == 1)

    def turns_for(h):
        return (lax.rem(h, 2) == 1) | ((s >= half) & (lax.rem(h, 4) != 0))

    def detours(h):
        return lax.rem(h, 3) == 1

    barrier = pltpu.get_barrier_semaphore()

    def greet(group, inner):
        pl.semaphore_signal(barrier, inc=1, device_id=(group, inner), device_id_type=MESH)

    greet(g_prev, s)
    greet(g, shard(-2))
    greet(g, shard(-1))

    @pl.when(even)
    def _():
        greet(g, shard(1))

    @pl.when(s < 2)
    def _():
        greet(g, ring_back)

    @pl.when(s == 0)
    def _():
        greet(g, shard(-4))
        greet(g, shard(2))

    @pl.when(lends)
    def _():
        greet(g, flip)

    @pl.when(turned)
    def _():
        greet(far, shard(-2))

    @pl.when(y_first & at_start)
    def _():
        greet(lax.rem(g_prev + rows_y, n_outer), shard(2))

    count = 3 + lax.rem(s, 2)
    for extra in (last, lends, before_last, s == 2, turns, turned):
        count += extra.astype(jnp.int32)
    pl.semaphore_wait(barrier, count)

    def remote(h, src, dst, sem, target):
        return pltpu.make_async_remote_copy(
            src_ref=kv.at[h, :, src],
            dst_ref=kv.at[h, :, dst],
            send_sem=send.at[sem, h],
            recv_sem=recv.at[dst, h],
            device_id=target,
            device_id_type=MESH,
        )

    def pair(h, src, dst, sem, target):
        return pltpu.make_async_remote_copy(
            src_ref=kv.at[h, :, pl.ds(src, 2)],
            dst_ref=kv.at[h, :, pl.ds(dst, 2)],
            send_sem=send.at[sem, h],
            recv_sem=recv.at[dst, h],
            device_id=target,
            device_id_type=MESH,
        )

    def to_next_group(h, act):
        @pl.when(turns & turns_for(h))
        def _():
            act(pair(h, 0, 10, 0, (far, shard(2))))

        @pl.when(jnp.logical_not(turns & turns_for(h)))
        def _():
            act(pair(h, 0, 5, 0, (g_next, s)))

    def from_turn(h, act):
        @pl.when(turned & turns_for(h))
        def _():
            act(pair(h, 10, 5, 11, (far_next, shard(-2))))

    me = (g, s)
    two_on, one_on, one_back = (g, shard(2)), (g, shard(1)), (g, shard(-1))
    via, beside = (g, flip), (g, ring_on)

    def first(h):
        detour = last & detours(h)
        straight = jnp.logical_not(detour)
        return [
            (straight, 1, 3, 1, two_on),
            (last & straight, 0, 8, 2, two_on),
            (detour, 1, 11, 1, via),
            (detour, 0, 10, 2, via),
            (even, 1, 2, 3, one_on),
            (s == n_inner - 3, 0, 7, 2, one_back),
        ]

    passed = [
        (None, 3, 4, 4, one_on),
        (s < 2, 8, 9, 5, one_on),
        (odd, 3, 2, 6, one_back),
    ]
    passed_high = [
        (s == 2, 9, 7, 8, (g, shard(-2))),
        (before_last, 7, 9, 8, (g, shard(4))),
    ]
    between = [(None, 11, 3, 9, beside), (None, 10, 8, 10, beside)]

    def each(table, h, act):
        for condition, *entry in table:
            if condition is None:
                act(remote(h, *entry))
            else:
                @pl.when(condition)
                def _(entry=entry):
                    act(remote(h, *entry))

    def send_own(h):
        pltpu.make_async_copy(kv.at[h, :, pl.ds(0, 2)], kv.at[h, :, pl.ds(0, 2)], own_sem.at[h]).wait()
        each(first(h), h, lambda copy: copy.start())

    def send_on(h):
        to_next_group(h, lambda copy: copy.start())

    for h in range(LEAD):
        send_own(h)
        send_on(h)

    early = ((lax.rem(s, half) >= half - 4) | (lax.rem(s, half) < 4)) & jnp.logical_not(turns)

    @pl.when(early)
    def _():
        @pl.loop(LEAD, LEAD_EARLY)
        def _(h):
            send_own(h)

    lead = jnp.where(turns, LEAD_TURN, LEAD)

    @pl.when(turns)
    def _():
        @pl.loop(LEAD, LEAD_TURN)
        def _(h):
            send_own(h)
            send_on(h)

    def send_ahead(h):
        @pl.when(jnp.logical_not(early) & (h + lead < KVH))
        def _():
            send_own(h + lead)

        @pl.when(early & (h + LEAD_EARLY < KVH))
        def _():
            send_own(h + LEAD_EARLY)

        @pl.when(h + lead < KVH)
        def _():
            send_on(h + lead)

    def arrived(h, dst):
        remote(h, dst, dst, 0, me).wait_recv()

    def pass_on(h):
        arrived(h, 3)

        @pl.when(s < 2)
        def _():
            arrived(h, 8)

        each(passed, h, lambda copy: copy.start())

    def pass_high(h):
        @pl.when(s == 2)
        def _():
            arrived(h, 9)

        @pl.when(before_last)
        def _():
            arrived(h, 7)

        each(passed_high, h, lambda copy: copy.start())

    def relay(h):
        @pl.when(lends & detours(h))
        def _():
            arrived(h, 11)
            arrived(h, 10)
            each(between, h, lambda copy: copy.start())

    def pass_turn(h):
        @pl.when(turned & turns_for(h))
        def _():
            pair(h, 10, 10, 0, me).wait_recv()

        from_turn(h, lambda copy: copy.start())

    seam = at_end | (s < 2)
    passes_high = (s == 2) | before_last
    for h in range(4):
        relay(h)
    pass_on(0)

    @pl.when(seam)
    def _():
        pass_on(1)
        pass_on(2)

    @pl.when(passes_high)
    def _():
        pass_high(0)
        pass_high(1)

    @pl.when(before_last)
    def _():
        pass_high(2)


    for h in range(4):
        pass_turn(h)

    for copy in st_copies:
        copy.wait()
    other = jnp.where(st[1, 0:1, 0:1] < st[0, 0:1, 0:1], INF, -INF).astype(jnp.float32)
    row = lax.broadcasted_iota(jnp.int32, (T, REP * T), 0)
    query = lax.rem(lax.broadcasted_iota(jnp.int32, (T, REP * T), 1), T)
    diagonal[...] = jnp.where(row <= query, INF, -INF).astype(jnp.float32)

    q_copy.wait()

    def columns(h, r):
        return pl.ds(pl.multiple_of(h * (REP * D) + r * D, D), D)

    def attend(h, wrapped):
        q = jnp.concatenate(
            [q_vm[row0:row0 + T, columns(h, r)] for row0 in (0, T) for r in range(REP)], axis=0
        )
        results = []
        for c in range(2 * REP * T // 256):
            slots = 10 if wrapped and c > 0 else 7
            keys = kv[h, 0, 0:slots].reshape(slots * T, D)
            values = kv[h, 1, 0:slots].reshape(slots * T, D)
            scores = lax.dot_general(
                keys, q[c * 256:(c + 1) * 256], (((1,), (1,)), ((), ())), preferred_element_type=jnp.float32
            )
            blocks, sums = [], []
            for b in range(2):
                block = 2 * c + b
                high = block >= 3
                lanes = slice((block % 3) * 128, (block % 3 + 1) * 128)
                parts = [scores[slot * T:(slot + 1) * T, b * 128:(b + 1) * 128] for slot in range(slots)]
                own = 0 if high else 1
                parts[own] = jnp.minimum(parts[own], diagonal[:, lanes])
                for slot in (5, 6):
                    parts[slot] = jnp.minimum(parts[slot], other)
                for j in range(1, 4):
                    if wrapped and high:
                        parts[6 + j] = jnp.minimum(parts[6 + j], jnp.where(s < j, INF, -INF))
                    if wrapped and not high:
                        parts[1 + j] = jnp.minimum(parts[1 + j], jnp.where(s >= j, INF, -INF))
                        if slots > 7:
                            parts[6 + j] = None
                if not high:
                    parts[0] = None
                top = None
                for part in parts:
                    if part is not None:
                        peak = jnp.max(part, axis=0, keepdims=True)
                        top = peak if top is None else jnp.maximum(top, peak)
                total, rounded = None, []
                for part in parts:
                    if part is None:
                        rounded.append(jnp.zeros((T, 128), jnp.bfloat16))
                    else:
                        weights = jnp.exp2((part - top) * (SCALE * LOG2_E))
                        here = jnp.sum(weights, axis=0, keepdims=True)
                        total = here if total is None else total + here
                        rounded.append(weights.astype(jnp.bfloat16))
                blocks.append(jnp.concatenate(rounded, axis=0))
                sums.append(total)
            weighted = lax.dot_general(
                values, jnp.concatenate(blocks, axis=1), (((0,), (0,)), ((), ())), preferred_element_type=jnp.float32
            )
            results.append((weighted / jnp.concatenate(sums, axis=1)).T.astype(o_vm.dtype))
        result = jnp.concatenate(results, axis=0)
        for half_index in range(2):
            for r in range(REP):
                start = (half_index * REP + r) * T
                o_vm[half_index * T:(half_index + 1) * T, columns(h, r)] = result[start:start + T]

    def out_copy(h):
        columns = pl.ds(pl.multiple_of(h * (REP * D), REP * D), REP * D)
        return pltpu.make_async_copy(o_vm.at[:, columns], o_hbm.at[:, columns], o_sem.at[h])

    @pl.loop(0, KVH)
    def _(h):
        @pl.when(h + 4 < KVH)
        def _():
            relay(h + 4)

        @pl.when(seam & (h + 3 < KVH))
        def _():
            pass_on(h + 3)

        @pl.when(before_last & (h + 3 < KVH))
        def _():
            pass_high(h + 3)

        @pl.when((s == 2) & (h + 2 < KVH))
        def _():
            pass_high(h + 2)

        send_ahead(h)

        @pl.when(jnp.logical_not(seam) & (h + 1 < KVH))
        def _():
            pass_on(h + 1)

        @pl.when(h + 4 < KVH)
        def _():
            pass_turn(h + 4)

        arrived(h, 2)
        arrived(h, 4)

        @pl.when(s == 0)
        def _():
            arrived(h, 7)

        @pl.when(s < 2)
        def _():
            arrived(h, 9)

        pair(h, 5, 5, 0, me).wait_recv()

        @pl.when(s >= 3)
        def _():
            attend(h, False)

        @pl.when(s < 3)
        def _():
            attend(h, True)

        out_copy(h).start()

    @pl.loop(0, KVH)
    def _(h):
        to_next_group(h, lambda copy: copy.wait_send())
        from_turn(h, lambda copy: copy.wait_send())
        each(first(h), h, lambda copy: copy.wait_send())
        each(passed, h, lambda copy: copy.wait_send())
        each(passed_high, h, lambda copy: copy.wait_send())

        @pl.when(lends & detours(h))
        def _():
            each(between, h, lambda copy: copy.wait_send())

        out_copy(h).wait()


def solution(mesh):
    n_outer, n_inner = mesh.shape["outer"], mesh.shape["inner"]

    def on_device(queries, keys, values, stretch_of):
        rows, width = queries.shape
        any_space = pl.BlockSpec(memory_space=pl.ANY)
        return pl.pallas_call(
            lambda *refs: kernel(n_outer, n_inner, *refs),
            out_shape=jax.ShapeDtypeStruct((rows, width), jnp.bfloat16),
            in_specs=[any_space] * 4,
            out_specs=any_space,
            scratch_shapes=[
                pltpu.VMEM((rows, width), jnp.bfloat16),
                pltpu.VMEM((KVH, 2, SLOTS, T, D), jnp.bfloat16),
                pltpu.VMEM((rows, width), jnp.bfloat16),
                pltpu.VMEM((2, 2, n_inner), jnp.int32),
                pltpu.VMEM((T, REP * T), jnp.float32),
                pltpu.SemaphoreType.DMA,
                pltpu.SemaphoreType.DMA((KVH,)),
                pltpu.SemaphoreType.DMA((2,)),
                pltpu.SemaphoreType.DMA((KVH,)),
                pltpu.SemaphoreType.DMA((SLOTS, KVH)),
                pltpu.SemaphoreType.DMA((12, KVH)),
            ],
            compiler_params=pltpu.CompilerParams(
                collective_id=0, has_side_effects=True, vmem_limit_bytes=48 * 1024 * 1024
            ),
            cost_estimate=pl.CostEstimate(flops=2 * 10**9, bytes_accessed=6 * 10**6, transcendentals=4 * 10**6),
        )(*(
            pltpu.with_memory_space_constraint(array, pltpu.HBM)
            for array in (queries, keys, values, stretch_of.transpose(0, 2, 1))
        ))

    rows = P(("outer", "inner"), None)
    return jax.shard_map(
        on_device, mesh=mesh, in_specs=(rows, rows, rows, P()), out_specs=rows, check_vma=False
    )
```

```python
import jax
import jax.numpy as jnp
from jax import lax
from jax.experimental import pallas as pl
from jax.experimental.pallas import tpu as pltpu
from jax.sharding import PartitionSpec as P

MESH = pl.DeviceIdType.MESH
KVH = 8
REP = 4
D = 128
T = 96
SCALE = D ** (-0.5)
LEAD = 3
LEAD_EARLY = 6
LEAD_TURN = 6
LOG2_E = 1.4426950408889634
INF = float("inf")

SLOTS = 12


def kernel(n_outer, n_inner, q_hbm, k_hbm, v_hbm, st_hbm, o_hbm, q_vm, kv, o_vm, st, diagonal,
           q_sem, own_sem, st_sem, o_sem, recv, send):
    g = lax.axis_index("outer")
    s = lax.axis_index("inner")
    g_next, g_prev = lax.rem(g + 1, n_outer), lax.rem(g + n_outer - 1, n_outer)

    def shard(distance):
        return lax.rem(s + distance + n_inner, n_inner)

    even = lax.rem(s, 2) == 0
    odd = lax.rem(s, 2) == 1

    def own_copies(h):
        columns = pl.ds(pl.multiple_of(h * D, D), D)
        return [
            pltpu.make_async_copy(
                ref.at[pl.ds(T * (1 - slot), T), columns], kv.at[h, i, slot], own_sem.at[h]
            )
            for i, ref in enumerate((k_hbm, v_hbm))
            for slot in range(2)
        ]

    @pl.loop(0, KVH)
    def _(h):
        for copy in own_copies(h):
            copy.start()

    st_copies = [
        pltpu.make_async_copy(st_hbm.at[group], st.at[i], st_sem.at[i])
        for i, group in enumerate((g, g_prev))
    ]
    for copy in st_copies:
        copy.start()
    q_copy = pltpu.make_async_copy(q_hbm, q_vm, q_sem)
    q_copy.start()

    @pl.when(s == 2)
    def _():
        kv[:, :, 7:9] = jnp.zeros((KVH, 2, 2, T, D), kv.dtype)

    @pl.when(s == 1)
    def _():
        kv[:, :, 7:8] = jnp.zeros((KVH, 2, 1, T, D), kv.dtype)

    half = n_inner // 2
    at_end = lax.rem(s, half) >= half - 2
    at_start = lax.rem(s, half) < 2
    flip = lax.rem(s + half, n_inner)
    ring_on = lax.rem(s + 2, half) + half * (s // half)
    ring_back = lax.rem(s + half - 2, half) + half * (s // half)
    last, lends = s >= n_inner - 2, at_end & (s < half)
    before_last = s == n_inner - 4

    rows_y = n_outer // 2
    y_first = lax.rem(g, rows_y) == 0
    turns = (lax.rem(g, rows_y) == rows_y - 1) & at_start
    far, far_next = lax.rem(g + rows_y, n_outer), lax.rem(g_next + rows_y, n_outer)

    turned = (lax.rem(g, rows_y) == rows_y - 1) & (lax.rem(s, half) // 2 == 1)

    def turns_for(h):
        return jnp.where(s < half, lax.rem(h, 3) != 0, lax.rem(h, 4) != 0)

    def detours(h):
        return lax.rem(h, 3) == 1

    barrier = pltpu.get_barrier_semaphore()

    def greet(group, inner):
        pl.semaphore_signal(barrier, inc=1, device_id=(group, inner), device_id_type=MESH)

    greet(g_prev, s)
    greet(g, shard(-2))
    greet(g, shard(-1))

    @pl.when(even)
    def _():
        greet(g, shard(1))

    @pl.when(s < 2)
    def _():
        greet(g, ring_back)

    @pl.when(s == 0)
    def _():
        greet(g, shard(-4))
        greet(g, shard(2))

    @pl.when(lends)
    def _():
        greet(g, flip)

    @pl.when(turned)
    def _():
        greet(far, shard(-2))

    @pl.when(y_first & at_start)
    def _():
        greet(lax.rem(g_prev + rows_y, n_outer), shard(2))

    count = 3 + lax.rem(s, 2)
    for extra in (last, lends, before_last, s == 2, turns, turned):
        count += extra.astype(jnp.int32)
    pl.semaphore_wait(barrier, count)

    def remote(h, src, dst, sem, target):
        return pltpu.make_async_remote_copy(
            src_ref=kv.at[h, :, src],
            dst_ref=kv.at[h, :, dst],
            send_sem=send.at[sem, h],
            recv_sem=recv.at[dst, h],
            device_id=target,
            device_id_type=MESH,
        )

    def pair(h, src, dst, sem, target):
        return pltpu.make_async_remote_copy(
            src_ref=kv.at[h, :, pl.ds(src, 2)],
            dst_ref=kv.at[h, :, pl.ds(dst, 2)],
            send_sem=send.at[sem, h],
            recv_sem=recv.at[dst, h],
            device_id=target,
            device_id_type=MESH,
        )

    def to_next_group(h, act):
        @pl.when(turns & turns_for(h))
        def _():
            act(pair(h, 0, 10, 0, (far, shard(2))))

        @pl.when(jnp.logical_not(turns & turns_for(h)))
        def _():
            act(pair(h, 0, 5, 0, (g_next, s)))

    def from_turn(h, act):
        @pl.when(turned & turns_for(h))
        def _():
            act(pair(h, 10, 5, 11, (far_next, shard(-2))))

    me = (g, s)
    two_on, one_on, one_back = (g, shard(2)), (g, shard(1)), (g, shard(-1))
    via, beside = (g, flip), (g, ring_on)

    def first(h):
        detour = last & detours(h)
        straight = jnp.logical_not(detour)
        return [
            (straight, 1, 3, 1, two_on),
            (last & straight, 0, 8, 2, two_on),
            (detour, 1, 11, 1, via),
            (detour, 0, 10, 2, via),
            (even, 1, 2, 3, one_on),
            (s == n_inner - 3, 0, 7, 2, one_back),
        ]

    passed = [
        (None, 3, 4, 4, one_on),
        (s < 2, 8, 9, 5, one_on),
        (odd, 3, 2, 6, one_back),
    ]
    passed_high = [
        (s == 2, 9, 7, 8, (g, shard(-2))),
        (before_last, 7, 9, 8, (g, shard(4))),
    ]
    between = [(None, 11, 3, 9, beside), (None, 10, 8, 10, beside)]

    def each(table, h, act):
        for condition, *entry in table:
            if condition is None:
                act(remote(h, *entry))
            else:
                @pl.when(condition)
                def _(entry=entry):
                    act(remote(h, *entry))

    def send_own(h):
        pltpu.make_async_copy(kv.at[h, :, pl.ds(0, 2)], kv.at[h, :, pl.ds(0, 2)], own_sem.at[h]).wait()
        each(first(h), h, lambda copy: copy.start())

    def send_on(h):
        to_next_group(h, lambda copy: copy.start())

    for h in range(LEAD):
        send_own(h)
        send_on(h)

    early = ((lax.rem(s, half) >= half - 4) | (lax.rem(s, half) < 4)) & jnp.logical_not(turns)

    @pl.when(early)
    def _():
        @pl.loop(LEAD, LEAD_EARLY)
        def _(h):
            send_own(h)

    lead = jnp.where(turns, LEAD_TURN, LEAD)

    @pl.when(turns)
    def _():
        @pl.loop(LEAD, LEAD_TURN)
        def _(h):
            send_own(h)
            send_on(h)

    def send_ahead(h):
        @pl.when(jnp.logical_not(early) & (h + lead < KVH))
        def _():
            send_own(h + lead)

        @pl.when(early & (h + LEAD_EARLY < KVH))
        def _():
            send_own(h + LEAD_EARLY)

        @pl.when(h + lead < KVH)
        def _():
            send_on(h + lead)

    def arrived(h, dst):
        remote(h, dst, dst, 0, me).wait_recv()

    def pass_on(h):
        arrived(h, 3)

        @pl.when(s < 2)
        def _():
            arrived(h, 8)

        each(passed, h, lambda copy: copy.start())

    def pass_high(h):
        @pl.when(s == 2)
        def _():
            arrived(h, 9)

        @pl.when(before_last)
        def _():
            arrived(h, 7)

        each(passed_high, h, lambda copy: copy.start())

    def relay(h):
        @pl.when(lends & detours(h))
        def _():
            arrived(h, 11)
            arrived(h, 10)
            each(between, h, lambda copy: copy.start())

    def pass_turn(h):
        @pl.when(turned & turns_for(h))
        def _():
            pair(h, 10, 10, 0, me).wait_recv()

        from_turn(h, lambda copy: copy.start())

    seam = at_end | (s < 2)
    passes_high = (s == 2) | before_last
    for h in range(4):
        relay(h)
    pass_on(0)

    @pl.when(seam)
    def _():
        pass_on(1)
        pass_on(2)

    @pl.when(passes_high)
    def _():
        pass_high(0)
        pass_high(1)

    @pl.when(before_last)
    def _():
        pass_high(2)


    for h in range(3):
        pass_turn(h)

    for copy in st_copies:
        copy.wait()
    other = jnp.where(st[1, 0:1, 0:1] < st[0, 0:1, 0:1], INF, -INF).astype(jnp.float32)
    row = lax.broadcasted_iota(jnp.int32, (T, REP * T), 0)
    query = lax.rem(lax.broadcasted_iota(jnp.int32, (T, REP * T), 1), T)
    diagonal[...] = jnp.where(row <= query, INF, -INF).astype(jnp.float32)

    q_copy.wait()

    def columns(h, r):
        return pl.ds(pl.multiple_of(h * (REP * D) + r * D, D), D)

    def attend(h, wrapped):
        q = jnp.concatenate(
            [q_vm[row0:row0 + T, columns(h, r)] for row0 in (0, T) for r in range(REP)], axis=0
        )
        results = []
        for c in range(2 * REP * T // 256):
            slots = 10 if wrapped and c > 0 else 7
            keys = kv[h, 0, 0:slots].reshape(slots * T, D)
            values = kv[h, 1, 0:slots].reshape(slots * T, D)
            scores = lax.dot_general(
                keys, q[c * 256:(c + 1) * 256], (((1,), (1,)), ((), ())), preferred_element_type=jnp.float32
            )
            blocks, sums = [], []
            for b in range(2):
                block = 2 * c + b
                high = block >= 3
                lanes = slice((block % 3) * 128, (block % 3 + 1) * 128)
                parts = [scores[slot * T:(slot + 1) * T, b * 128:(b + 1) * 128] for slot in range(slots)]
                own = 0 if high else 1
                parts[own] = jnp.minimum(parts[own], diagonal[:, lanes])
                for slot in (5, 6):
                    parts[slot] = jnp.minimum(parts[slot], other)
                for j in range(1, 4):
                    if wrapped and high:
                        parts[6 + j] = jnp.minimum(parts[6 + j], jnp.where(s < j, INF, -INF))
                    if wrapped and not high:
                        parts[1 + j] = jnp.minimum(parts[1 + j], jnp.where(s >= j, INF, -INF))
                        if slots > 7:
                            parts[6 + j] = None
                if not high:
                    parts[0] = None
                top = None
                for part in parts:
                    if part is not None:
                        peak = jnp.max(part, axis=0, keepdims=True)
                        top = peak if top is None else jnp.maximum(top, peak)
                total, rounded = None, []
                for part in parts:
                    if part is None:
                        rounded.append(jnp.zeros((T, 128), jnp.bfloat16))
                    else:
                        weights = jnp.exp2((part - top) * (SCALE * LOG2_E))
                        here = jnp.sum(weights, axis=0, keepdims=True)
                        total = here if total is None else total + here
                        rounded.append(weights.astype(jnp.bfloat16))
                blocks.append(jnp.concatenate(rounded, axis=0))
                sums.append(total)
            weighted = lax.dot_general(
                values, jnp.concatenate(blocks, axis=1), (((0,), (0,)), ((), ())), preferred_element_type=jnp.float32
            )
            results.append((weighted / jnp.concatenate(sums, axis=1)).T.astype(o_vm.dtype))
        result = jnp.concatenate(results, axis=0)
        for half_index in range(2):
            for r in range(REP):
                start = (half_index * REP + r) * T
                o_vm[half_index * T:(half_index + 1) * T, columns(h, r)] = result[start:start + T]

    def out_copy(h):
        columns = pl.ds(pl.multiple_of(h * (REP * D), REP * D), REP * D)
        return pltpu.make_async_copy(o_vm.at[:, columns], o_hbm.at[:, columns], o_sem.at[h])

    @pl.loop(0, KVH)
    def _(h):
        @pl.when(h + 4 < KVH)
        def _():
            relay(h + 4)

        @pl.when(seam & (h + 3 < KVH))
        def _():
            pass_on(h + 3)

        @pl.when(before_last & (h + 3 < KVH))
        def _():
            pass_high(h + 3)

        @pl.when((s == 2) & (h + 2 < KVH))
        def _():
            pass_high(h + 2)

        send_ahead(h)

        @pl.when(jnp.logical_not(seam) & (h + 1 < KVH))
        def _():
            pass_on(h + 1)

        @pl.when(h + 3 < KVH)
        def _():
            pass_turn(h + 3)

        arrived(h, 2)
        arrived(h, 4)

        @pl.when(s == 0)
        def _():
            arrived(h, 7)

        @pl.when(s < 2)
        def _():
            arrived(h, 9)

        pair(h, 5, 5, 0, me).wait_recv()

        @pl.when(s >= 3)
        def _():
            attend(h, False)

        @pl.when(s < 3)
        def _():
            attend(h, True)

        out_copy(h).start()

    @pl.loop(0, KVH)
    def _(h):
        to_next_group(h, lambda copy: copy.wait_send())
        from_turn(h, lambda copy: copy.wait_send())
        each(first(h), h, lambda copy: copy.wait_send())
        each(passed, h, lambda copy: copy.wait_send())
        each(passed_high, h, lambda copy: copy.wait_send())

        @pl.when(lends & detours(h))
        def _():
            each(between, h, lambda copy: copy.wait_send())

        out_copy(h).wait()


def solution(mesh):
    n_outer, n_inner = mesh.shape["outer"], mesh.shape["inner"]

    def on_device(queries, keys, values, stretch_of):
        rows, width = queries.shape
        any_space = pl.BlockSpec(memory_space=pl.ANY)
        return pl.pallas_call(
            lambda *refs: kernel(n_outer, n_inner, *refs),
            out_shape=jax.ShapeDtypeStruct((rows, width), jnp.bfloat16),
            in_specs=[any_space] * 4,
            out_specs=any_space,
            scratch_shapes=[
                pltpu.VMEM((rows, width), jnp.bfloat16),
                pltpu.VMEM((KVH, 2, SLOTS, T, D), jnp.bfloat16),
                pltpu.VMEM((rows, width), jnp.bfloat16),
                pltpu.VMEM((2, 2, n_inner), jnp.int32),
                pltpu.VMEM((T, REP * T), jnp.float32),
                pltpu.SemaphoreType.DMA,
                pltpu.SemaphoreType.DMA((KVH,)),
                pltpu.SemaphoreType.DMA((2,)),
                pltpu.SemaphoreType.DMA((KVH,)),
                pltpu.SemaphoreType.DMA((SLOTS, KVH)),
                pltpu.SemaphoreType.DMA((12, KVH)),
            ],
            compiler_params=pltpu.CompilerParams(
                collective_id=0, has_side_effects=True, vmem_limit_bytes=48 * 1024 * 1024
            ),
            cost_estimate=pl.CostEstimate(flops=2 * 10**9, bytes_accessed=6 * 10**6, transcendentals=4 * 10**6),
        )(*(
            pltpu.with_memory_space_constraint(array, pltpu.HBM)
            for array in (queries, keys, values, stretch_of.transpose(0, 2, 1))
        ))

    rows = P(("outer", "inner"), None)
    return jax.shard_map(
        on_device, mesh=mesh, in_specs=(rows, rows, rows, P()), out_specs=rows, check_vma=False
    )
```

```python
import jax
import jax.numpy as jnp
from jax import lax
from jax.experimental import pallas as pl
from jax.experimental.pallas import tpu as pltpu
from jax.sharding import PartitionSpec as P

MESH = pl.DeviceIdType.MESH
KVH = 8
REP = 4
D = 128
T = 96
SCALE = D ** (-0.5)
LEAD = 3
LEAD_EARLY = 6
LEAD_TURN = 6
LOG2_E = 1.4426950408889634
INF = float("inf")

SLOTS = 12


def kernel(n_outer, n_inner, q_hbm, k_hbm, v_hbm, st_hbm, o_hbm, q_vm, kv, o_vm, st, diagonal,
           q_sem, own_sem, st_sem, o_sem, recv, send):
    g = lax.axis_index("outer")
    s = lax.axis_index("inner")
    g_next, g_prev = lax.rem(g + 1, n_outer), lax.rem(g + n_outer - 1, n_outer)

    def shard(distance):
        return lax.rem(s + distance + n_inner, n_inner)

    even = lax.rem(s, 2) == 0
    odd = lax.rem(s, 2) == 1

    def own_copies(h):
        columns = pl.ds(pl.multiple_of(h * D, D), D)
        return [
            pltpu.make_async_copy(
                ref.at[pl.ds(T * (1 - slot), T), columns], kv.at[h, i, slot], own_sem.at[h]
            )
            for i, ref in enumerate((k_hbm, v_hbm))
            for slot in range(2)
        ]

    @pl.loop(0, KVH)
    def _(h):
        for copy in own_copies(h):
            copy.start()

    st_copies = [
        pltpu.make_async_copy(st_hbm.at[group], st.at[i], st_sem.at[i])
        for i, group in enumerate((g, g_prev))
    ]
    for copy in st_copies:
        copy.start()
    q_copy = pltpu.make_async_copy(q_hbm, q_vm, q_sem)
    q_copy.start()

    @pl.when(s == 2)
    def _():
        kv[:, :, 7:9] = jnp.zeros((KVH, 2, 2, T, D), kv.dtype)

    @pl.when(s == 1)
    def _():
        kv[:, :, 7:8] = jnp.zeros((KVH, 2, 1, T, D), kv.dtype)

    half = n_inner // 2
    at_end = lax.rem(s, half) >= half - 2
    at_start = lax.rem(s, half) < 2
    flip = lax.rem(s + half, n_inner)
    ring_on = lax.rem(s + 2, half) + half * (s // half)
    ring_back = lax.rem(s + half - 2, half) + half * (s // half)
    last, lends = s >= n_inner - 2, at_end & (s < half)
    before_last = s == n_inner - 4

    rows_y = n_outer // 2
    y_first = lax.rem(g, rows_y) == 0
    turns = (lax.rem(g, rows_y) == rows_y - 1) & at_start
    far, far_next = lax.rem(g + rows_y, n_outer), lax.rem(g_next + rows_y, n_outer)

    turned = (lax.rem(g, rows_y) == rows_y - 1) & (lax.rem(s, half) // 2 == 1)

    def turns_for(h):
        return (lax.rem(h, 2) == 1) | ((s >= half) & (lax.rem(h, 4) != 0))

    def detours(h):
        return lax.rem(h, 3) == 1

    barrier = pltpu.get_barrier_semaphore()

    def greet(group, inner):
        pl.semaphore_signal(barrier, inc=1, device_id=(group, inner), device_id_type=MESH)

    greet(g_prev, s)
    greet(g, shard(-2))
    greet(g, shard(-1))

    @pl.when(even)
    def _():
        greet(g, shard(1))

    @pl.when(s < 2)
    def _():
        greet(g, ring_back)

    @pl.when(s == 0)
    def _():
        greet(g, shard(-4))
        greet(g, shard(2))

    @pl.when(lends)
    def _():
        greet(g, flip)

    @pl.when(turned)
    def _():
        greet(far, shard(-2))

    @pl.when(y_first & at_start)
    def _():
        greet(lax.rem(g_prev + rows_y, n_outer), shard(2))

    count = 3 + lax.rem(s, 2)
    for extra in (last, lends, before_last, s == 2, turns, turned):
        count += extra.astype(jnp.int32)
    pl.semaphore_wait(barrier, count)

    def remote(h, src, dst, sem, target):
        return pltpu.make_async_remote_copy(
            src_ref=kv.at[h, :, src],
            dst_ref=kv.at[h, :, dst],
            send_sem=send.at[sem, h],
            recv_sem=recv.at[dst, h],
            device_id=target,
            device_id_type=MESH,
        )

    def pair(h, src, dst, sem, target):
        return pltpu.make_async_remote_copy(
            src_ref=kv.at[h, :, pl.ds(src, 2)],
            dst_ref=kv.at[h, :, pl.ds(dst, 2)],
            send_sem=send.at[sem, h],
            recv_sem=recv.at[dst, h],
            device_id=target,
            device_id_type=MESH,
        )

    def to_next_group(h, act):
        @pl.when(turns & turns_for(h))
        def _():
            act(pair(h, 0, 10, 0, (far, shard(2))))

        @pl.when(jnp.logical_not(turns & turns_for(h)))
        def _():
            act(pair(h, 0, 5, 0, (g_next, s)))

    def from_turn(h, act):
        @pl.when(turned & turns_for(h))
        def _():
            act(pair(h, 10, 5, 11, (far_next, shard(-2))))

    me = (g, s)
    two_on, one_on, one_back = (g, shard(2)), (g, shard(1)), (g, shard(-1))
    via, beside = (g, flip), (g, ring_on)

    def first(h):
        detour = last & detours(h)
        straight = jnp.logical_not(detour)
        return [
            (straight, 1, 3, 1, two_on),
            (last & straight, 0, 8, 2, two_on),
            (detour, 1, 11, 1, via),
            (detour, 0, 10, 2, via),
            (even, 1, 2, 3, one_on),
            (s == n_inner - 3, 0, 7, 2, one_back),
        ]

    passed = [
        (None, 3, 4, 4, one_on),
        (s < 2, 8, 9, 5, one_on),
        (odd, 3, 2, 6, one_back),
    ]
    passed_high = [
        (s == 2, 9, 7, 8, (g, shard(-2))),
        (before_last, 7, 9, 8, (g, shard(4))),
    ]
    between = [(None, 11, 3, 9, beside), (None, 10, 8, 10, beside)]

    def each(table, h, act):
        for condition, *entry in table:
            if condition is None:
                act(remote(h, *entry))
            else:
                @pl.when(condition)
                def _(entry=entry):
                    act(remote(h, *entry))

    def send_own(h):
        pltpu.make_async_copy(kv.at[h, :, pl.ds(0, 2)], kv.at[h, :, pl.ds(0, 2)], own_sem.at[h]).wait()
        each(first(h), h, lambda copy: copy.start())

    def send_on(h):
        to_next_group(h, lambda copy: copy.start())

    for h in range(LEAD):
        send_own(h)
        send_on(h)

    early = ((lax.rem(s, half) >= half - 4) | (lax.rem(s, half) < 4)) & jnp.logical_not(turns)

    @pl.when(early)
    def _():
        @pl.loop(LEAD, LEAD_EARLY)
        def _(h):
            send_own(h)

    lead = jnp.where(turns, LEAD_TURN, LEAD)

    @pl.when(turns)
    def _():
        @pl.loop(LEAD, LEAD_TURN)
        def _(h):
            send_own(h)
            send_on(h)

    def send_ahead(h):
        @pl.when(jnp.logical_not(early) & (h + lead < KVH))
        def _():
            send_own(h + lead)

        @pl.when(early & (h + LEAD_EARLY < KVH))
        def _():
            send_own(h + LEAD_EARLY)

        @pl.when(h + lead < KVH)
        def _():
            send_on(h + lead)

    def arrived(h, dst):
        remote(h, dst, dst, 0, me).wait_recv()

    def pass_on(h):
        arrived(h, 3)

        @pl.when(s < 2)
        def _():
            arrived(h, 8)

        each(passed, h, lambda copy: copy.start())

    def pass_high(h):
        @pl.when(s == 2)
        def _():
            arrived(h, 9)

        @pl.when(before_last)
        def _():
            arrived(h, 7)

        each(passed_high, h, lambda copy: copy.start())

    def relay(h):
        @pl.when(lends & detours(h))
        def _():
            arrived(h, 11)
            arrived(h, 10)
            each(between, h, lambda copy: copy.start())

    def pass_turn(h):
        @pl.when(turned & turns_for(h))
        def _():
            pair(h, 10, 10, 0, me).wait_recv()

        from_turn(h, lambda copy: copy.start())

    seam = at_end | (s < 2)
    passes_high = (s == 2) | before_last
    for h in range(4):
        relay(h)
    pass_on(0)

    @pl.when(seam)
    def _():
        pass_on(1)
        pass_on(2)

    @pl.when(passes_high)
    def _():
        pass_high(0)
        pass_high(1)

    @pl.when(before_last)
    def _():
        pass_high(2)


    for h in range(2):
        pass_turn(h)

    for copy in st_copies:
        copy.wait()
    other = jnp.where(st[1, 0:1, 0:1] < st[0, 0:1, 0:1], INF, -INF).astype(jnp.float32)
    row = lax.broadcasted_iota(jnp.int32, (T, REP * T), 0)
    query = lax.rem(lax.broadcasted_iota(jnp.int32, (T, REP * T), 1), T)
    diagonal[...] = jnp.where(row <= query, INF, -INF).astype(jnp.float32)

    q_copy.wait()

    def columns(h, r):
        return pl.ds(pl.multiple_of(h * (REP * D) + r * D, D), D)

    def attend(h, wrapped):
        q = jnp.concatenate(
            [q_vm[row0:row0 + T, columns(h, r)] for row0 in (0, T) for r in range(REP)], axis=0
        )
        results = []
        for c in range(2 * REP * T // 256):
            slots = 10 if wrapped and c > 0 else 7
            keys = kv[h, 0, 0:slots].reshape(slots * T, D)
            values = kv[h, 1, 0:slots].reshape(slots * T, D)
            scores = lax.dot_general(
                keys, q[c * 256:(c + 1) * 256], (((1,), (1,)), ((), ())), preferred_element_type=jnp.float32
            )
            blocks, sums = [], []
            for b in range(2):
                block = 2 * c + b
                high = block >= 3
                lanes = slice((block % 3) * 128, (block % 3 + 1) * 128)
                parts = [scores[slot * T:(slot + 1) * T, b * 128:(b + 1) * 128] for slot in range(slots)]
                own = 0 if high else 1
                parts[own] = jnp.minimum(parts[own], diagonal[:, lanes])
                for slot in (5, 6):
                    parts[slot] = jnp.minimum(parts[slot], other)
                for j in range(1, 4):
                    if wrapped and high:
                        parts[6 + j] = jnp.minimum(parts[6 + j], jnp.where(s < j, INF, -INF))
                    if wrapped and not high:
                        parts[1 + j] = jnp.minimum(parts[1 + j], jnp.where(s >= j, INF, -INF))
                        if slots > 7:
                            parts[6 + j] = None
                if not high:
                    parts[0] = None
                top = None
                for part in parts:
                    if part is not None:
                        peak = jnp.max(part, axis=0, keepdims=True)
                        top = peak if top is None else jnp.maximum(top, peak)
                total, rounded = None, []
                for part in parts:
                    if part is None:
                        rounded.append(jnp.zeros((T, 128), jnp.bfloat16))
                    else:
                        weights = jnp.exp2((part - top) * (SCALE * LOG2_E))
                        here = jnp.sum(weights, axis=0, keepdims=True)
                        total = here if total is None else total + here
                        rounded.append(weights.astype(jnp.bfloat16))
                blocks.append(jnp.concatenate(rounded, axis=0))
                sums.append(total)
            weighted = lax.dot_general(
                values, jnp.concatenate(blocks, axis=1), (((0,), (0,)), ((), ())), preferred_element_type=jnp.float32
            )
            results.append((weighted / jnp.concatenate(sums, axis=1)).T.astype(o_vm.dtype))
        result = jnp.concatenate(results, axis=0)
        for half_index in range(2):
            for r in range(REP):
                start = (half_index * REP + r) * T
                o_vm[half_index * T:(half_index + 1) * T, columns(h, r)] = result[start:start + T]

    def out_copy(h):
        columns = pl.ds(pl.multiple_of(h * (REP * D), REP * D), REP * D)
        return pltpu.make_async_copy(o_vm.at[:, columns], o_hbm.at[:, columns], o_sem.at[h])

    @pl.loop(0, KVH)
    def _(h):
        @pl.when(h + 4 < KVH)
        def _():
            relay(h + 4)

        @pl.when(seam & (h + 3 < KVH))
        def _():
            pass_on(h + 3)

        @pl.when(before_last & (h + 3 < KVH))
        def _():
            pass_high(h + 3)

        @pl.when((s == 2) & (h + 2 < KVH))
        def _():
            pass_high(h + 2)

        send_ahead(h)

        @pl.when(jnp.logical_not(seam) & (h + 1 < KVH))
        def _():
            pass_on(h + 1)

        @pl.when(h + 2 < KVH)
        def _():
            pass_turn(h + 2)

        arrived(h, 2)
        arrived(h, 4)

        @pl.when(s == 0)
        def _():
            arrived(h, 7)

        @pl.when(s < 2)
        def _():
            arrived(h, 9)

        pair(h, 5, 5, 0, me).wait_recv()

        @pl.when(s >= 3)
        def _():
            attend(h, False)

        @pl.when(s < 3)
        def _():
            attend(h, True)

        out_copy(h).start()

    @pl.loop(0, KVH)
    def _(h):
        to_next_group(h, lambda copy: copy.wait_send())
        from_turn(h, lambda copy: copy.wait_send())
        each(first(h), h, lambda copy: copy.wait_send())
        each(passed, h, lambda copy: copy.wait_send())
        each(passed_high, h, lambda copy: copy.wait_send())

        @pl.when(lends & detours(h))
        def _():
            each(between, h, lambda copy: copy.wait_send())

        out_copy(h).wait()


def solution(mesh):
    n_outer, n_inner = mesh.shape["outer"], mesh.shape["inner"]

    def on_device(queries, keys, values, stretch_of):
        rows, width = queries.shape
        any_space = pl.BlockSpec(memory_space=pl.ANY)
        return pl.pallas_call(
            lambda *refs: kernel(n_outer, n_inner, *refs),
            out_shape=jax.ShapeDtypeStruct((rows, width), jnp.bfloat16),
            in_specs=[any_space] * 4,
            out_specs=any_space,
            scratch_shapes=[
                pltpu.VMEM((rows, width), jnp.bfloat16),
                pltpu.VMEM((KVH, 2, SLOTS, T, D), jnp.bfloat16),
                pltpu.VMEM((rows, width), jnp.bfloat16),
                pltpu.VMEM((2, 2, n_inner), jnp.int32),
                pltpu.VMEM((T, REP * T), jnp.float32),
                pltpu.SemaphoreType.DMA,
                pltpu.SemaphoreType.DMA((KVH,)),
                pltpu.SemaphoreType.DMA((2,)),
                pltpu.SemaphoreType.DMA((KVH,)),
                pltpu.SemaphoreType.DMA((SLOTS, KVH)),
                pltpu.SemaphoreType.DMA((12, KVH)),
            ],
            compiler_params=pltpu.CompilerParams(
                collective_id=0, has_side_effects=True, vmem_limit_bytes=48 * 1024 * 1024
            ),
            cost_estimate=pl.CostEstimate(flops=2 * 10**9, bytes_accessed=6 * 10**6, transcendentals=4 * 10**6),
        )(*(
            pltpu.with_memory_space_constraint(array, pltpu.HBM)
            for array in (queries, keys, values, stretch_of.transpose(0, 2, 1))
        ))

    rows = P(("outer", "inner"), None)
    return jax.shard_map(
        on_device, mesh=mesh, in_specs=(rows, rows, rows, P()), out_specs=rows, check_vma=False
    )
```

```python
import jax
import jax.numpy as jnp
from jax import lax
from jax.experimental import pallas as pl
from jax.experimental.pallas import tpu as pltpu
from jax.sharding import PartitionSpec as P

MESH = pl.DeviceIdType.MESH
KVH = 8
REP = 4
D = 128
T = 96
SCALE = D ** (-0.5)
LEAD = 3
LEAD_EARLY = 6
LEAD_TURN = 8
LOG2_E = 1.4426950408889634
INF = float("inf")

SLOTS = 12


def kernel(n_outer, n_inner, q_hbm, k_hbm, v_hbm, st_hbm, o_hbm, q_vm, kv, o_vm, st, diagonal,
           q_sem, own_sem, st_sem, o_sem, recv, send):
    g = lax.axis_index("outer")
    s = lax.axis_index("inner")
    g_next, g_prev = lax.rem(g + 1, n_outer), lax.rem(g + n_outer - 1, n_outer)

    def shard(distance):
        return lax.rem(s + distance + n_inner, n_inner)

    even = lax.rem(s, 2) == 0
    odd = lax.rem(s, 2) == 1

    def own_copies(h):
        columns = pl.ds(pl.multiple_of(h * D, D), D)
        return [
            pltpu.make_async_copy(
                ref.at[pl.ds(T * (1 - slot), T), columns], kv.at[h, i, slot], own_sem.at[h]
            )
            for i, ref in enumerate((k_hbm, v_hbm))
            for slot in range(2)
        ]

    @pl.loop(0, KVH)
    def _(h):
        for copy in own_copies(h):
            copy.start()

    st_copies = [
        pltpu.make_async_copy(st_hbm.at[group], st.at[i], st_sem.at[i])
        for i, group in enumerate((g, g_prev))
    ]
    for copy in st_copies:
        copy.start()
    q_copy = pltpu.make_async_copy(q_hbm, q_vm, q_sem)
    q_copy.start()

    @pl.when(s == 2)
    def _():
        kv[:, :, 7:9] = jnp.zeros((KVH, 2, 2, T, D), kv.dtype)

    @pl.when(s == 1)
    def _():
        kv[:, :, 7:8] = jnp.zeros((KVH, 2, 1, T, D), kv.dtype)

    half = n_inner // 2
    at_end = lax.rem(s, half) >= half - 2
    at_start = lax.rem(s, half) < 2
    flip = lax.rem(s + half, n_inner)
    ring_on = lax.rem(s + 2, half) + half * (s // half)
    ring_back = lax.rem(s + half - 2, half) + half * (s // half)
    last, lends = s >= n_inner - 2, at_end & (s < half)
    before_last = s == n_inner - 4

    rows_y = n_outer // 2
    y_first = lax.rem(g, rows_y) == 0
    turns = (lax.rem(g, rows_y) == rows_y - 1) & at_start
    far, far_next = lax.rem(g + rows_y, n_outer), lax.rem(g_next + rows_y, n_outer)

    turned = (lax.rem(g, rows_y) == rows_y - 1) & (lax.rem(s, half) // 2 == 1)

    def turns_for(h):
        return (lax.rem(h, 2) == 1) | ((s >= half) & (lax.rem(h, 4) != 0))

    def detours(h):
        return lax.rem(h, 3) == 1

    barrier = pltpu.get_barrier_semaphore()

    def greet(group, inner):
        pl.semaphore_signal(barrier, inc=1, device_id=(group, inner), device_id_type=MESH)

    greet(g_prev, s)
    greet(g, shard(-2))
    greet(g, shard(-1))

    @pl.when(even)
    def _():
        greet(g, shard(1))

    @pl.when(s < 2)
    def _():
        greet(g, ring_back)

    @pl.when(s == 0)
    def _():
        greet(g, shard(-4))
        greet(g, shard(2))

    @pl.when(lends)
    def _():
        greet(g, flip)

    @pl.when(turned)
    def _():
        greet(far, shard(-2))

    @pl.when(y_first & at_start)
    def _():
        greet(lax.rem(g_prev + rows_y, n_outer), shard(2))

    count = 3 + lax.rem(s, 2)
    for extra in (last, lends, before_last, s == 2, turns, turned):
        count += extra.astype(jnp.int32)
    pl.semaphore_wait(barrier, count)

    def remote(h, src, dst, sem, target):
        return pltpu.make_async_remote_copy(
            src_ref=kv.at[h, :, src],
            dst_ref=kv.at[h, :, dst],
            send_sem=send.at[sem, h],
            recv_sem=recv.at[dst, h],
            device_id=target,
            device_id_type=MESH,
        )

    def pair(h, src, dst, sem, target):
        return pltpu.make_async_remote_copy(
            src_ref=kv.at[h, :, pl.ds(src, 2)],
            dst_ref=kv.at[h, :, pl.ds(dst, 2)],
            send_sem=send.at[sem, h],
            recv_sem=recv.at[dst, h],
            device_id=target,
            device_id_type=MESH,
        )

    def to_next_group(h, act):
        @pl.when(turns & turns_for(h))
        def _():
            act(pair(h, 0, 10, 0, (far, shard(2))))

        @pl.when(jnp.logical_not(turns & turns_for(h)))
        def _():
            act(pair(h, 0, 5, 0, (g_next, s)))

    def from_turn(h, act):
        @pl.when(turned & turns_for(h))
        def _():
            act(pair(h, 10, 5, 11, (far_next, shard(-2))))

    me = (g, s)
    two_on, one_on, one_back = (g, shard(2)), (g, shard(1)), (g, shard(-1))
    via, beside = (g, flip), (g, ring_on)

    def first(h):
        detour = last & detours(h)
        straight = jnp.logical_not(detour)
        return [
            (straight, 1, 3, 1, two_on),
            (last & straight, 0, 8, 2, two_on),
            (detour, 1, 11, 1, via),
            (detour, 0, 10, 2, via),
            (even, 1, 2, 3, one_on),
            (s == n_inner - 3, 0, 7, 2, one_back),
        ]

    passed = [
        (None, 3, 4, 4, one_on),
        (s < 2, 8, 9, 5, one_on),
        (odd, 3, 2, 6, one_back),
    ]
    passed_high = [
        (s == 2, 9, 7, 8, (g, shard(-2))),
        (before_last, 7, 9, 8, (g, shard(4))),
    ]
    between = [(None, 11, 3, 9, beside), (None, 10, 8, 10, beside)]

    def each(table, h, act):
        for condition, *entry in table:
            if condition is None:
                act(remote(h, *entry))
            else:
                @pl.when(condition)
                def _(entry=entry):
                    act(remote(h, *entry))

    def send_own(h):
        pltpu.make_async_copy(kv.at[h, :, pl.ds(0, 2)], kv.at[h, :, pl.ds(0, 2)], own_sem.at[h]).wait()
        each(first(h), h, lambda copy: copy.start())

    def send_on(h):
        to_next_group(h, lambda copy: copy.start())

    for h in range(LEAD):
        send_own(h)
        send_on(h)

    early = ((lax.rem(s, half) >= half - 4) | (lax.rem(s, half) < 4)) & jnp.logical_not(turns)

    @pl.when(early)
    def _():
        @pl.loop(LEAD, LEAD_EARLY)
        def _(h):
            send_own(h)

    lead = jnp.where(turns, LEAD_TURN, LEAD)

    @pl.when(turns)
    def _():
        @pl.loop(LEAD, LEAD_TURN)
        def _(h):
            send_own(h)
            send_on(h)

    def send_ahead(h):
        @pl.when(jnp.logical_not(early) & (h + lead < KVH))
        def _():
            send_own(h + lead)

        @pl.when(early & (h + LEAD_EARLY < KVH))
        def _():
            send_own(h + LEAD_EARLY)

        @pl.when(h + lead < KVH)
        def _():
            send_on(h + lead)

    def arrived(h, dst):
        remote(h, dst, dst, 0, me).wait_recv()

    def pass_on(h):
        arrived(h, 3)

        @pl.when(s < 2)
        def _():
            arrived(h, 8)

        each(passed, h, lambda copy: copy.start())

    def pass_high(h):
        @pl.when(s == 2)
        def _():
            arrived(h, 9)

        @pl.when(before_last)
        def _():
            arrived(h, 7)

        each(passed_high, h, lambda copy: copy.start())

    def relay(h):
        @pl.when(lends & detours(h))
        def _():
            arrived(h, 11)
            arrived(h, 10)
            each(between, h, lambda copy: copy.start())

    def pass_turn(h):
        @pl.when(turned & turns_for(h))
        def _():
            pair(h, 10, 10, 0, me).wait_recv()

        from_turn(h, lambda copy: copy.start())

    seam = at_end | (s < 2)
    passes_high = (s == 2) | before_last
    for h in range(4):
        relay(h)
    pass_on(0)

    @pl.when(seam)
    def _():
        pass_on(1)
        pass_on(2)

    @pl.when(passes_high)
    def _():
        pass_high(0)
        pass_high(1)

    @pl.when(before_last)
    def _():
        pass_high(2)


    for h in range(3):
        pass_turn(h)

    for copy in st_copies:
        copy.wait()
    other = jnp.where(st[1, 0:1, 0:1] < st[0, 0:1, 0:1], INF, -INF).astype(jnp.float32)
    row = lax.broadcasted_iota(jnp.int32, (T, REP * T), 0)
    query = lax.rem(lax.broadcasted_iota(jnp.int32, (T, REP * T), 1), T)
    diagonal[...] = jnp.where(row <= query, INF, -INF).astype(jnp.float32)

    q_copy.wait()

    def columns(h, r):
        return pl.ds(pl.multiple_of(h * (REP * D) + r * D, D), D)

    def attend(h, wrapped):
        q = jnp.concatenate(
            [q_vm[row0:row0 + T, columns(h, r)] for row0 in (0, T) for r in range(REP)], axis=0
        )
        results = []
        for c in range(2 * REP * T // 256):
            slots = 10 if wrapped and c > 0 else 7
            keys = kv[h, 0, 0:slots].reshape(slots * T, D)
            values = kv[h, 1, 0:slots].reshape(slots * T, D)
            scores = lax.dot_general(
                keys, q[c * 256:(c + 1) * 256], (((1,), (1,)), ((), ())), preferred_element_type=jnp.float32
            )
            blocks, sums = [], []
            for b in range(2):
                block = 2 * c + b
                high = block >= 3
                lanes = slice((block % 3) * 128, (block % 3 + 1) * 128)
                parts = [scores[slot * T:(slot + 1) * T, b * 128:(b + 1) * 128] for slot in range(slots)]
                own = 0 if high else 1
                parts[own] = jnp.minimum(parts[own], diagonal[:, lanes])
                for slot in (5, 6):
                    parts[slot] = jnp.minimum(parts[slot], other)
                for j in range(1, 4):
                    if wrapped and high:
                        parts[6 + j] = jnp.minimum(parts[6 + j], jnp.where(s < j, INF, -INF))
                    if wrapped and not high:
                        parts[1 + j] = jnp.minimum(parts[1 + j], jnp.where(s >= j, INF, -INF))
                        if slots > 7:
                            parts[6 + j] = None
                if not high:
                    parts[0] = None
                top = None
                for part in parts:
                    if part is not None:
                        peak = jnp.max(part, axis=0, keepdims=True)
                        top = peak if top is None else jnp.maximum(top, peak)
                total, rounded = None, []
                for part in parts:
                    if part is None:
                        rounded.append(jnp.zeros((T, 128), jnp.bfloat16))
                    else:
                        weights = jnp.exp2((part - top) * (SCALE * LOG2_E))
                        here = jnp.sum(weights, axis=0, keepdims=True)
                        total = here if total is None else total + here
                        rounded.append(weights.astype(jnp.bfloat16))
                blocks.append(jnp.concatenate(rounded, axis=0))
                sums.append(total)
            weighted = lax.dot_general(
                values, jnp.concatenate(blocks, axis=1), (((0,), (0,)), ((), ())), preferred_element_type=jnp.float32
            )
            results.append((weighted / jnp.concatenate(sums, axis=1)).T.astype(o_vm.dtype))
        result = jnp.concatenate(results, axis=0)
        for half_index in range(2):
            for r in range(REP):
                start = (half_index * REP + r) * T
                o_vm[half_index * T:(half_index + 1) * T, columns(h, r)] = result[start:start + T]

    def out_copy(h):
        columns = pl.ds(pl.multiple_of(h * (REP * D), REP * D), REP * D)
        return pltpu.make_async_copy(o_vm.at[:, columns], o_hbm.at[:, columns], o_sem.at[h])

    @pl.loop(0, KVH)
    def _(h):
        @pl.when(h + 4 < KVH)
        def _():
            relay(h + 4)

        @pl.when(seam & (h + 3 < KVH))
        def _():
            pass_on(h + 3)

        @pl.when(before_last & (h + 3 < KVH))
        def _():
            pass_high(h + 3)

        @pl.when((s == 2) & (h + 2 < KVH))
        def _():
            pass_high(h + 2)

        send_ahead(h)

        @pl.when(jnp.logical_not(seam) & (h + 1 < KVH))
        def _():
            pass_on(h + 1)

        @pl.when(h + 3 < KVH)
        def _():
            pass_turn(h + 3)

        arrived(h, 2)
        arrived(h, 4)

        @pl.when(s == 0)
        def _():
            arrived(h, 7)

        @pl.when(s < 2)
        def _():
            arrived(h, 9)

        pair(h, 5, 5, 0, me).wait_recv()

        @pl.when(s >= 3)
        def _():
            attend(h, False)

        @pl.when(s < 3)
        def _():
            attend(h, True)

        out_copy(h).start()

    @pl.loop(0, KVH)
    def _(h):
        to_next_group(h, lambda copy: copy.wait_send())
        from_turn(h, lambda copy: copy.wait_send())
        each(first(h), h, lambda copy: copy.wait_send())
        each(passed, h, lambda copy: copy.wait_send())
        each(passed_high, h, lambda copy: copy.wait_send())

        @pl.when(lends & detours(h))
        def _():
            each(between, h, lambda copy: copy.wait_send())

        out_copy(h).wait()


def solution(mesh):
    n_outer, n_inner = mesh.shape["outer"], mesh.shape["inner"]

    def on_device(queries, keys, values, stretch_of):
        rows, width = queries.shape
        any_space = pl.BlockSpec(memory_space=pl.ANY)
        return pl.pallas_call(
            lambda *refs: kernel(n_outer, n_inner, *refs),
            out_shape=jax.ShapeDtypeStruct((rows, width), jnp.bfloat16),
            in_specs=[any_space] * 4,
            out_specs=any_space,
            scratch_shapes=[
                pltpu.VMEM((rows, width), jnp.bfloat16),
                pltpu.VMEM((KVH, 2, SLOTS, T, D), jnp.bfloat16),
                pltpu.VMEM((rows, width), jnp.bfloat16),
                pltpu.VMEM((2, 2, n_inner), jnp.int32),
                pltpu.VMEM((T, REP * T), jnp.float32),
                pltpu.SemaphoreType.DMA,
                pltpu.SemaphoreType.DMA((KVH,)),
                pltpu.SemaphoreType.DMA((2,)),
                pltpu.SemaphoreType.DMA((KVH,)),
                pltpu.SemaphoreType.DMA((SLOTS, KVH)),
                pltpu.SemaphoreType.DMA((12, KVH)),
            ],
            compiler_params=pltpu.CompilerParams(
                collective_id=0, has_side_effects=True, vmem_limit_bytes=48 * 1024 * 1024
            ),
            cost_estimate=pl.CostEstimate(flops=2 * 10**9, bytes_accessed=6 * 10**6, transcendentals=4 * 10**6),
        )(*(
            pltpu.with_memory_space_constraint(array, pltpu.HBM)
            for array in (queries, keys, values, stretch_of.transpose(0, 2, 1))
        ))

    rows = P(("outer", "inner"), None)
    return jax.shard_map(
        on_device, mesh=mesh, in_specs=(rows, rows, rows, P()), out_specs=rows, check_vma=False
    )
```
